32 devices in a mesh: section: 2 (over x), node: 16 (over z, y, core).
Axes of the slice: x: 2, y: 2, z: 4, core: 2. Of those that a mesh axis runs over, the one named last changes fastest.
Arguments:
- in_nodes: float32 [8, 256, 512], P(None, 'node'), may hold values from -6 to 6
- in_edges: float32 [8, 2048, 512], P(None, 'node'), may hold values from -6 to 6
- senders: int32 [2048], P('node'), may hold values from 0 to 255, as said below
- receivers: int32 [2048], P('node'), may hold values from 0 to 255, as said below
- edge_w1: float32 [2, 1536, 512], P('section'), may hold values from -0.15625 to 0.15625
- edge_w2: float32 [2, 512, 512], P('section'), may hold values from -0.25 to 0.25
- edge_vec: float32 [2, 4, 512], P('section'), may hold values from -2 to 2
- node_w1: float32 [2, 1024, 512], P('section'), may hold values from -0.1875 to 0.1875
- node_w2: float32 [2, 512, 512], P('section'), may hold values from -0.25 to 0.25
- node_vec: float32 [2, 4, 512], P('section'), may hold values from -2 to 2
- cot_nodes: float32 [8, 256, 512], P(None, 'node'), may hold values from -6 to 6
- cot_edges: float32 [8, 2048, 512], P(None, 'node'), may hold values from -6 to 6
- lengths: int32 [4], replicated, may hold values from 1 to 2
- step_mask: int32 [4, 2], replicated, may hold values 0 or 1
Outputs:
- act_nodes: float32 [2, 8, 256, 512], P('section', None, 'node')
- act_edges: float32 [2, 8, 2048, 512], P('section', None, 'node')
- grad_nodes: float32 [2, 8, 256, 512], P('section', None, 'node')
- grad_edges: float32 [2, 8, 2048, 512], P('section', None, 'node')
- grad_edge_w1: float32 [2, 1536, 512], P('section')
- grad_edge_w2: float32 [2, 512, 512], P('section')
- grad_edge_vec: float32 [2, 4, 512], P('section')
- grad_node_w1: float32 [2, 1024, 512], P('section')
- grad_node_w2: float32 [2, 512, 512], P('section')
- grad_node_vec: float32 [2, 4, 512], P('section')
The draws below stay inside these ranges and needn't reach their ends.
Inputs may be any that keep to these rules, and one draw needn't show every extreme that they name: `senders`: edge row k lies on node device d = k // 128; its sender lies in node block d - 1, d or d + 1 taken cyclically, block b holding nodes b * 16 to (b + 1) * 16 - 1. `receivers`: edge row k lies on node device d = k // 128; its receiver lies in node block d - 1, d or d + 1 taken cyclically.
All inputs are finite; a program needn't handle non-finite values.
Results may differ from the reference program's by a relative error of at most 0.0003.
Values sent between devices are 32-bit elements; how exact they have to be, the bound alone decides.
No kernel may reach another device: no remote copies, remote signals or barrier semaphores. Data moves between devices by JAX's collectives and lax.ppermute only.
A program may use at most 192 MiB of HBM per device.

```python
import jax
import jax.numpy as jnp
from jax import lax

L = 512
NODE_DEV = 16
EDGE_DEV = 128
MICRO = 4
STEPS = 2
SAMPLES = 8
NODES = 256
EDGES = 2048
N_NODE = 16


def endpoint_rows(key):
    keys = jax.random.split(key, 2)
    row_index = jnp.arange(EDGES, dtype=jnp.int32)
    home_block = row_index // EDGE_DEV
    offset = jax.random.randint(keys[0], (EDGES,), -1, 2)
    block = (home_block + offset + N_NODE) % N_NODE
    inside = jax.random.randint(keys[1], (EDGES,), 0, NODE_DEV)
    return (block * NODE_DEV + inside).astype(jnp.int32)


def draw_senders(key, part):
    key = jax.random.fold_in(key, 13)
    index_rows = endpoint_rows(key)
    return index_rows.at[0].set(NODES - 1).at[1].set(0)


def draw_receivers(key, part):
    key = jax.random.fold_in(key, 14)
    index_rows = endpoint_rows(key)
    return index_rows.at[0].set(0).at[1].set(NODES - 1)


def vector_rows(key):
    keys = jax.random.split(key, 4)
    bias_in = jnp.clip(0.5 * jax.random.normal(keys[0], (2, 1, L), jnp.float32), -2.0, 2.0)
    bias_out = jnp.clip(0.5 * jax.random.normal(keys[1], (2, 1, L), jnp.float32), -2.0, 2.0)
    gain_rows = jax.random.uniform(keys[2], (2, 1, L), jnp.float32, 0.5, 1.5)
    shift_rows = jnp.clip(0.3 * jax.random.normal(keys[3], (2, 1, L), jnp.float32), -2.0, 2.0)
    return jnp.concatenate([bias_in, bias_out, gain_rows, shift_rows], axis=1).astype(jnp.float32)


def draw_edge_vec(key, part):
    key = jax.random.fold_in(key, 11)
    return vector_rows(key)


def draw_node_vec(key, part):
    key = jax.random.fold_in(key, 12)
    return vector_rows(key)


def draw_lengths(key, part):
    key = jax.random.fold_in(key, 15)
    keys = jax.random.split(key, 2)
    drawn = jax.random.randint(keys[0], (MICRO,), 1, STEPS + 1)
    order = jax.random.permutation(keys[1], MICRO)
    return drawn.at[order[0]].set(STEPS).at[order[1]].set(1).astype(jnp.int32)


def set_ends(entries, key, smallest, top_value):
    longest = entries.shape.index(max(entries.shape))
    spots = []
    for shift in (0, 1):
        where = [jax.random.randint(jax.random.fold_in(key, axis), (), 0, length) for axis, length in enumerate(entries.shape)]
        where[longest] = (where[longest] + shift) % entries.shape[longest]
        spots.append(tuple(where))
    return entries.at[spots[0]].set(smallest).at[spots[1]].set(top_value)


def level_of(own_key, dims, shards, low, top_value):
    def one(position, shards_of):
        steps = jax.random.uniform(jax.random.fold_in(jax.random.fold_in(own_key, 6), position), (shards_of,), jnp.float32, low / len(shards), top_value / len(shards))
        return jnp.repeat(jnp.exp(steps), dims[position] // shards_of).reshape((-1,) + (1,) * (len(dims) - position - 1))

    level = one(*shards[0])
    for cut in shards[1:]:
        level = level * one(*cut)
    return level


def noise(stream_key, shape, spread, limit, pieces=(), kind=jnp.bfloat16):
    result = jax.random.normal(stream_key, shape, jnp.float32) * spread
    if len(pieces) > 0:
        result = level_of(stream_key, shape, pieces, -0.22, 0.18) * result
    return jnp.clip(result, min=-limit, max=limit).astype(kind)


def setup_inputs(seed: int = 0) -> dict:
    seeds = jax.random.split(jax.random.key(seed), 15)
    return {
        "in_nodes": noise(seeds[0], (SAMPLES, NODES, L), 1.0, 6.0, ((1, 16),), jnp.float32),
        "in_edges": noise(seeds[1], (SAMPLES, EDGES, L), 1.0, 6.0, ((1, 16),), jnp.float32),
        "senders": draw_senders(jax.random.fold_in(seeds[14], 71), 0),
        "receivers": draw_receivers(jax.random.fold_in(seeds[14], 71), 0),
        "edge_w1": noise(seeds[4], (2, 3 * L, L), (3 * L) ** -0.5, 0.15625, ((0, 2),), jnp.float32),
        "edge_w2": noise(seeds[5], (2, L, L), L ** -0.5, 0.25, ((0, 2),), jnp.float32),
        "edge_vec": draw_edge_vec(jax.random.fold_in(seeds[14], 71), 0),
        "node_w1": noise(seeds[7], (2, 2 * L, L), (2 * L) ** -0.5, 0.1875, ((0, 2),), jnp.float32),
        "node_w2": noise(seeds[8], (2, L, L), L ** -0.5, 0.25, ((0, 2),), jnp.float32),
        "node_vec": draw_node_vec(jax.random.fold_in(seeds[14], 71), 0),
        "cot_nodes": noise(seeds[10], (SAMPLES, NODES, L), 1.0, 6.0, ((1, 16),), jnp.float32),
        "cot_edges": noise(seeds[11], (SAMPLES, EDGES, L), 1.0, 6.0, ((1, 16),), jnp.float32),
        "lengths": draw_lengths(jax.random.fold_in(seeds[14], 71), 0),
        "step_mask": set_ends((jax.random.randint(seeds[13], (MICRO, STEPS), 0, 8) < 7).astype(jnp.int32), jax.random.fold_in(seeds[13], 1), 0, 1),
    }


@jax.custom_vjp
def low(v):
    return lax.optimization_barrier(v.astype(jnp.bfloat16)).astype(jnp.float32)

@jax.custom_vjp
def low_back(v):
    return v

def low_keep(v):
    return (low(v), None)

def low_pass(kept, grad):
    return (grad,)

def back_keep(v):
    return (v, None)

def back_low(kept, grad):
    return (low(grad),)
low.defvjp(low_keep, low_pass)
low_back.defvjp(back_keep, back_low)
norm_eps = 1e-05

def layer_norm(inputs, gain_row, shift_row):
    row_mean = lax.optimization_barrier(jnp.mean(inputs, axis=-1, keepdims=True))
    centred = inputs - row_mean
    row_var = lax.optimization_barrier(jnp.mean(centred * centred, axis=-1, keepdims=True))
    return centred * lax.rsqrt(row_var + norm_eps) * gain_row + shift_row

def two_layer_mlp(joined, weight_in, weight_out, vectors):
    hidden = jax.nn.silu(jnp.dot(joined, weight_in, precision=lax.Precision.HIGHEST) + vectors[0])
    return layer_norm(jnp.dot(hidden, weight_out, precision=lax.Precision.HIGHEST) + vectors[1], vectors[2], vectors[3])

def processor(node_state, edge_state, senders, receivers, params):
    sent_rows = node_state[senders]
    recv_rows = node_state[receivers]
    message = two_layer_mlp(jnp.concatenate([edge_state, sent_rows, recv_rows], axis=1), params[0], params[1], params[2])
    gathered = jax.ops.segment_sum(message, receivers, num_segments=node_state.shape[0])
    update = two_layer_mlp(jnp.concatenate([node_state, gathered], axis=1), params[3], params[4], params[5])
    return (node_state + update, edge_state + message)

def reference(in_nodes, in_edges, senders, receivers, edge_w1, edge_w2, edge_vec, node_w1, node_w2, node_vec, cot_nodes, cot_edges, lengths, step_mask):
    step_index = jnp.arange(STEPS, dtype=jnp.int32)
    live_steps = (step_index[None, :] < lengths[:, None]).astype(jnp.int32) * step_mask
    sample_weight = live_steps.reshape(-1).astype(jnp.float32)
    all_params = (edge_w1, edge_w2, edge_vec, node_w1, node_w2, node_vec)
    first_params = tuple((weight_set[0] for weight_set in all_params))
    second_params = tuple((weight_set[1] for weight_set in all_params))

    def apply_layer(node_state, edge_state, params):
        return processor(node_state, edge_state, senders, receivers, params)

    def per_sample(totals, sample_item):
        node_state, edge_state, cot_node, cot_edge, weight_now = sample_item
        middle, pull_first = jax.vjp(apply_layer, node_state, edge_state, first_params)
        final, pull_second = jax.vjp(apply_layer, middle[0], middle[1], second_params)
        mid_grad_n, mid_grad_e, grads_second = pull_second((weight_now * cot_node, weight_now * cot_edge))
        in_grad_n, in_grad_e, grads_first = pull_first((mid_grad_n, mid_grad_e))
        totals = jax.tree.map(lambda summed, grad_a, grad_b: summed + jnp.stack([grad_a, grad_b]), totals, grads_first, grads_second)
        return (totals, (middle[0], middle[1], final[0], final[1], in_grad_n, in_grad_e, mid_grad_n, mid_grad_e))
    zero_grads = tuple((jnp.zeros_like(weight_set) for weight_set in all_params))
    totals, results = lax.scan(per_sample, zero_grads, (in_nodes, in_edges, cot_nodes, cot_edges, sample_weight))
    act_nodes = jnp.stack([results[0], results[2]])
    act_edges = jnp.stack([results[1], results[3]])
    grad_nodes = jnp.stack([results[4], results[6]])
    grad_edges = jnp.stack([results[5], results[7]])
    return (act_nodes, act_edges, grad_nodes, grad_edges, totals[0], totals[1], totals[2], totals[3], totals[4], totals[5])
```

```python
from types import SimpleNamespace

import jax
import jax.numpy as jnp
from jax import lax
from jax.experimental import pallas as pl
from jax.experimental.pallas import tpu as pltpu
from jax.sharding import PartitionSpec as P

f32, bf16 = jnp.float32, jnp.bfloat16
norm_eps = 1e-05
NN = ((1,), (0,))
NT = ((1,), (1,))
TN = ((0,), (0,))
group_sizes = (4, 4)
MIB = 1024 * 1024


def split(x):
    hi = x.astype(bf16)
    return hi, (x - hi.astype(f32)).astype(bf16)


def dot1(a, b, dims):
    return lax.dot_general(a, b, (dims, ((), ())), preferred_element_type=f32)


def dot3(a, b, dims):
    return dot1(a[0], b[0], dims) + (dot1(a[0], b[1], dims) + dot1(a[1], b[0], dims))


def dot3_few(a, b, dims):
    rows = a[0].shape[0]
    both = dot1(jnp.concatenate(a, axis=0), b[0], dims)
    return both[:rows] + (both[rows:] + dot1(a[0], b[1], dims))


def normalized(u):
    c = u - jnp.mean(u, axis=-1, keepdims=True)
    r = lax.rsqrt(jnp.mean(c * c, axis=-1, keepdims=True) + norm_eps)
    return c * r, r


def norm_back(gu, n, r, gain):
    t = gu * gain
    return r * (t - jnp.mean(t, axis=-1, keepdims=True) - n * jnp.mean(t * n, axis=-1, keepdims=True))


def column_sums(*xs):
    F = xs[0].shape[-1]
    return jnp.concatenate([jnp.sum(x, axis=0, keepdims=True) for x in xs] + [jnp.zeros((8 - len(xs), F), f32)], axis=0)


class Copies:
    def __init__(self, sems):
        self.sems, self.all = sems, []

    def __call__(self, src, dst):
        c = pltpu.make_async_copy(src, dst, self.sems.at[len(self.all)])
        self.all.append(c)
        c.start()
        return c

    def wait(self):
        wait(*self.all)


def wait(*copies):
    for c in copies:
        c.wait()


def far(*shape, dtype=f32):
    return pltpu.HBM(shape, dtype)


def near(*shape, dtype=f32):
    return pltpu.VMEM(shape, dtype)


resident = []


def call(body, name, scalars={}, hbm={}, vmem={}, free={}, outs={}, grow={}, scratch={}, after=(), micros=2, copies=24, active=None):
    args, specs, where = [], [], {}

    def add(values, space, pinned):
        for key, value in values.items():
            at = []
            for x in value if isinstance(value, (list, tuple)) else [value]:
                at.append(len(args))
                args.append(pltpu.with_memory_space_constraint(x, space) if pinned else x)
                specs.append(pl.BlockSpec(memory_space=space))
            where[key] = at if isinstance(value, (list, tuple)) else at[0]

    add(scalars, pltpu.SMEM, False)
    add(hbm, pltpu.HBM, True)
    add(vmem, pltpu.VMEM, True)
    add(free, pl.ANY, False)
    add(dict(after=[x for x in after if x.shape == (8, 128)]), pltpu.HBM, True)
    add(dict(arrived=[x for x in after if x.shape != (8, 128)]), pl.ANY, False)
    used = {id(x) for value in vmem.values() for x in (value if isinstance(value, (list, tuple)) else [value])}
    add(dict(kept=[x for x in resident if id(x) not in used]), pltpu.VMEM, True)
    shapes, out_specs, aliases = [], [], {}
    for key, value in list(outs.items()) + list(grow.items()) + [("token", far(8, 128))]:
        old, shape = value if key in grow else (None, value)
        space = pl.ANY if isinstance(shape, jax.ShapeDtypeStruct) else shape.memory_space
        where[key] = -1 - len(shapes)
        if old is not None:
            aliases[len(args)] = len(shapes)
            args.append(pltpu.with_memory_space_constraint(old, space))
            specs.append(pl.BlockSpec(memory_space=space))
        shapes.append(shape)
        out_specs.append(pl.BlockSpec(memory_space=space))
    first_out, first_scratch = len(args), len(args) + len(shapes)
    kept = dict(scratch)

    def kernel(*refs):
        k = SimpleNamespace()
        pick = lambda i: refs[i] if i >= 0 else refs[first_out - 1 - i]
        for key, at in where.items():
            setattr(k, key, [pick(i) for i in at] if isinstance(at, list) else pick(at))
        for i, key in enumerate(kept):
            setattr(k, key, refs[first_scratch + i])
        k.load, k.store = Copies(refs[-2]), Copies(refs[-1])
        if active is None:
            body(k)
        else:
            pl.when(k.here[0] == active)(lambda: body(k))

    res = pl.pallas_call(
        kernel,
        out_shape=shapes,
        in_specs=specs,
        out_specs=out_specs,
        scratch_shapes=list(kept.values()) + [pltpu.SemaphoreType.DMA((copies,))] * 2,
        input_output_aliases=aliases,
        compiler_params=pltpu.CompilerParams(vmem_limit_bytes=12 * MIB),
        cost_estimate=pl.CostEstimate(flops=int(micros * 1.15e9), bytes_accessed=0, transcendentals=0),
        name=name,
    )(*args)
    return SimpleNamespace(**{key: res[-1 - at] for key, at in where.items() if not isinstance(at, list) and at < 0})


def prepare(w1, w2, ends=None, here=None, W=0, after=()):
    F = w1.shape[1]

    def body(k):
        c1, c2 = k.load(k.w1, k.b1), k.load(k.w2, k.b2)
        if ends is not None:
            hots = []
            for src, ref in zip(k.ends, (k.e0, k.e1)):
                k.load(src, ref).wait()
                total = k.here[2] * (W // 3)
                at = ref[...] - (k.here[1] - 1) * (W // 3)
                at = jnp.where(at < 0, at + total, at)
                at = jnp.where(at >= total, at - total, at)
                hots.append((lax.broadcasted_iota(jnp.int32, (W, at.shape[1]), 0) == at).astype(f32).astype(bf16))
            both = jnp.concatenate(hots, axis=0)
            k.gather[...] = jnp.concatenate([both, both], axis=0)
            k.scatter[...] = jnp.concatenate([both, both], axis=1)
        c2.wait()
        k.h2[...], k.l2[...] = split(k.b2[...])
        c1.wait()
        k.h1[...], k.l1[...] = split(k.b1[...])

    half = lambda *s: near(*s, dtype=bf16)
    outs = dict(h1=half(*w1.shape), l1=half(*w1.shape), h2=half(*w2.shape), l2=half(*w2.shape))
    scalars, hbm = {}, dict(w1=w1, w2=w2)
    scratch = dict(b1=pltpu.VMEM(w1.shape, f32), b2=pltpu.VMEM(w2.shape, f32))
    if ends is not None:
        rows = ends[0].shape[1]
        outs.update(gather=half(4 * W, rows), scatter=half(2 * W, 2 * rows))
        scalars = dict(here=here)
        hbm.update(ends=list(ends))
        scratch.update(e0=pltpu.VMEM((1, rows), jnp.int32), e1=pltpu.VMEM((1, rows), jnp.int32))
    r = call(body, "prepare", scalars, hbm, outs=outs, scratch=scratch, after=after)
    resident.extend([r.h1, r.l1, r.h2, r.l2])
    if ends is not None:
        resident.extend([r.gather, r.scatter])
    return r, dict(w1=[r.h1, r.l1], w2=[r.h2, r.l2])


def side_rows(par, nr):
    return pl.multiple_of((1 - par) * 2 * nr, 16), pl.multiple_of(par * 2 * nr, 16)


def window_parts(k, ref, nr):
    a_at, b_at = side_rows(k.here[1] % 2, nr)
    return [ref.at[:, pl.ds(a_at, nr), :], ref.at[:, nr:2 * nr, :], ref.at[:, pl.ds(b_at, nr), :]]


def sample_weight(k, sample, micro, steps):
    m, t = divmod(sample, steps)
    return jnp.where(t < k.here[3 + m], k.here[3 + micro + sample], 0).astype(f32)


def load_views(k, views, refs, targets, g):
    return [k.load(ref.at[pl.ds(view[1], g)], target) for view, ref, target in zip(views, refs, targets)]


def arrays(views):
    return [v[0] for v in views]


def edge_forward(g, active, here, e, v, n, hot, w, vec, act, box, relay, after, micros):
    rows, F = e[0].shape[1:]
    nr = v[0][0].shape[1]
    W = 3 * nr
    cs = 2 if g % 2 == 0 else 1

    def body(k):
        load, store = k.load, k.store
        cv = load_views(k, v, k.v, window_parts(k, k.vb, nr), g)
        ce = [load(k.e.at[pl.ds(e[1] + s, cs)], k.eb.at[pl.ds(s, cs)]) for s in range(0, g, cs)]
        (w1h, w1l), (w2h, w2l), vec = k.w1, k.w2, k.vec
        wait(*cv)
        vw = split(k.vb[...].reshape(g * W, F))
        for i in (0, 1):
            part = pl.ds((i + 1) * F, F)
            h, l = split(dot3(vw, (w1h[part], w1l[part]), NN).reshape(g, W, F))
            k.pp[:, i * W:(i + 1) * W] = h
            k.pp[:, (i + 2) * W:(i + 3) * W] = l
        for s in range(0, g, cs):
            ce[s // cs].wait()
            to = pl.ds(s, cs)
            x = k.eb[to].reshape(cs * rows, F)
            a = dot3(split(x), (w1h[0:F], w1l[0:F]), NN) + vec[0:1]
            a = a + jnp.concatenate([dot1(k.gather[...], k.pp[s + t], TN) for t in range(cs)], axis=0)
            k.out_a[to] = a.reshape(cs, rows, F)
            h = a / (1 + jnp.exp(-a))
            n_, r = normalized(dot3(split(h), (w2h[...], w2l[...]), NN) + vec[1:2])
            k.out_n[to] = n_.reshape(cs, rows, F)
            k.out_r[to] = jnp.broadcast_to(r, (cs * rows, 128)).reshape(cs, rows, 128)
            m = n_ * vec[2:3] + vec[3:4]
            k.ob[to] = (x + m).reshape(cs, rows, F)
            if relay:
                store(k.ob.at[to], k.out_e.at[to])
            store(k.ob.at[to], k.act.at[pl.ds(n + s, cs)])
            mh, ml = split(m.reshape(cs, rows, F))
            for t in range(cs):
                k.sb[s + t] = dot1(k.scatter[W:], jnp.concatenate([mh[t], ml[t]], axis=0), NN)
        sides = window_parts(k, k.sb, nr)
        store(sides[0], k.box_a.at[pl.ds(box[2], g)])
        store(sides[1], k.own)
        store(sides[2], k.box_b.at[pl.ds(box[2], g)])
        store.wait()

    outs = dict(out_a=near(g, rows, F), out_n=near(g, rows, F), out_r=near(g, rows, 128), own=far(g, nr, F))
    if relay:
        outs.update(out_e=far(g, rows, F))
    old = box[0] or (None, None)
    grow = dict(act=(act[0], far(act[1], rows, F)), box_a=(old[0], far(box[1], nr, F)), box_b=(old[1], far(box[1], nr, F)))
    full = pltpu.VMEM((g, rows, F), f32)
    scratch = dict(eb=full, ob=full, vb=pltpu.VMEM((g, W, F), f32), sb=pltpu.VMEM((g, W, F), f32), pp=pltpu.VMEM((g, 4 * W, F), bf16))
    return call(body, "edge_forward", dict(here=here), active=active, vmem=dict(**w, gather=hot.gather, scatter=hot.scatter, vec=vec), free=dict(e=e[0], v=arrays(v)), outs=outs, grow=grow, scratch=scratch, after=after, micros=micros)


def node_stage(g, forward, backward, active, here, v, n, w, vec, parts, act=None, stash=None, weights=None, cot=None, box=None, after=(), micros=2):
    nr, F = v[0].shape[1:]
    R = g * nr

    def body(k):
        load, store = k.load, k.store
        cx = [load(k.v.at[pl.ds(v[1], g)], k.zb.at[:, :, 0:F])] + load_views(k, parts, k.parts, [k.pb.at[i] for i in range(len(parts))], g)
        if forward and backward:
            cx.append(load(k.cot.at[pl.ds(n, g)], k.gb))
        w1, w2, vec = (k.w1[0][...], k.w1[1][...]), (k.w2[0][...], k.w2[1][...]), k.vec
        wait(*cx)
        given = sum([k.pb[i] for i in range(1, len(parts))], k.pb[0])
        k.zb[:, :, F:] = given if forward else k.gathered[...]
        z = k.zb[...].reshape(R, 2 * F)
        zs = split(z)
        if forward:
            a = dot3_few(zs, w1, NN) + vec[0:1]
            h = a / (1 + jnp.exp(-a))
            n_, r = normalized(dot3_few(split(h), w2, NN) + vec[1:2])
            k.ob[...] = (z[:, :F] + n_ * vec[2:3] + vec[3:4]).reshape(g, nr, F)
            if not backward:
                store(k.ob, k.out_v)
                k.out_a[...] = a.reshape(g, nr, F)
                k.out_n[...] = n_.reshape(g, nr, F)
                k.out_r[...] = jnp.broadcast_to(r, (R, 128)).reshape(g, nr, 128)
                k.out_g[...] = given
            store(k.ob, k.act.at[pl.ds(n, g)])
        else:
            a, n_, r = k.a[...].reshape(R, F), k.n[...].reshape(R, F), k.r[...].reshape(R, 128)[:, 0:1]
        if backward:
            if forward:
                for s in range(g):
                    k.gb[s] = k.gb[s] * sample_weight(k, n + s, *weights)
                gu = k.gb[...].reshape(R, F)
            else:
                gu = given.reshape(R, F)
            gp = norm_back(gu, n_, r, vec[2:3])
            q = 1 / (1 + jnp.exp(-a))
            hs, gps = split(a * q), split(gp)
            ga = dot3_few(gps, w2, NT) * (q * (1 + a * (1 - q)))
            gas = split(ga)
            gz = dot3_few(gas, w1, NT)
            k.ggb[...] = gz[:, F:].reshape(g, nr, F)
            for ref in (k.box_a, k.box_b):
                store(k.ggb, ref.at[pl.ds(box[2], g)])
            k.own[...] = k.ggb[...]
            k.out_gv[...] = (gu + gz[:, :F]).reshape(g, nr, F)
            for i, x in enumerate((zs[0][:, :F], zs[1][:, :F], zs[0][:, F:], zs[1][:, F:], hs[0], hs[1], gas[0], gas[1], gps[0], gps[1])):
                k.ops[i] = x
            k.dv[...] = column_sums(ga, gp, gu * n_, gu)
        store.wait()

    hbm, vmem, free = {}, dict(**w, vec=vec), dict(v=v[0], parts=arrays(parts))
    shape = near(g, nr, F)
    outs, grow = {}, {}
    if not forward:
        vmem.update(a=stash.out_a, n=stash.out_n, r=stash.out_r, gathered=stash.out_g)
    elif backward:
        hbm.update(cot=cot)
    if forward:
        grow.update(act=(act[0], far(act[1], nr, F)))
        if not backward:
            outs.update(out_v=far(g, nr, F), out_a=shape, out_n=shape, out_r=near(g, nr, 128), out_g=shape)
    if backward:
        old = box[0] or (None, None)
        outs.update(own=shape, out_gv=shape, ops=near(10, R, F, dtype=bf16), dv=near(8, F))
        grow.update(box_a=(old[0], far(box[1], nr, F)), box_b=(old[1], far(box[1], nr, F)))
    small = pltpu.VMEM((g, nr, F), f32)
    scratch = dict(zb=pltpu.VMEM((g, nr, 2 * F), f32), pb=pltpu.VMEM((len(parts), g, nr, F), f32), gb=small, ob=small, ggb=small)
    return call(body, "node_stage", dict(here=here), hbm, vmem, free, active=active, outs=outs, grow=grow, scratch=scratch, after=after, micros=micros)


def node_weights(active, here, m, acc, first, after):
    _, R, F = m.ops.shape

    def body(k):
        o = k.ops
        for i, (x, y) in enumerate(((0, 6), (2, 6), (4, 8))):
            part = pl.ds(i * F, F)
            d = dot3((o[x], o[x + 1]), (o[y], o[y + 1]), TN)
            k.total[part] = d if first else k.total[part] + d

    grow = dict(total=(acc and acc.total, near(3 * F, F)))
    return call(body, "node_weights", dict(here=here), active=active, vmem=dict(ops=m.ops), grow=grow, after=after, micros=0.01)


def edge_backward(g, active, here, weights, ge, gg, n, stash, gv, hot, w, vec, box, after, micros):
    rows, F = ge[0].shape[1:]
    nr = gv.shape[1]
    W = 3 * nr
    cs = 2 if g % 2 == 0 else 1

    def body(k):
        load, store = k.load, k.store
        gg_at = window_parts(k, k.ggb, nr)
        cg = load_views(k, (gg[0], gg[2]), k.gg, (gg_at[0], gg_at[2]), g)
        cx = [load(k.ge.at[pl.ds(ge[1] + s, cs)], k.gb.at[pl.ds(s, cs)]) for s in range(0, g, cs)]
        k.ggb[:, nr:2 * nr] = k.gg_own[...]
        (w1h, w1l), (w2h, w2l), vec = k.w1, k.w2, k.vec
        wait(*cg)
        h, l = split(k.ggb[...])
        k.gg2[:, 0:W] = h
        k.gg2[:, W:] = l
        flat = lambda x: x.reshape(cs * rows, x.shape[-1])
        sums = []
        for s in range(0, g, cs):
            to = pl.ds(s, cs)
            cx[s // cs].wait()
            if weights:
                for t in range(s, s + cs):
                    k.gb[t] = k.gb[t] * sample_weight(k, n + t, *weights)
            hot_r = k.gather[pl.ds(W, W)]
            gu = flat(k.gb[to]) + jnp.concatenate([dot1(hot_r, k.gg2[s + t, 0:W], TN) + dot1(hot_r, k.gg2[s + t, W:], TN) for t in range(cs)], axis=0)
            n_, a = flat(k.n[to]), flat(k.a[to])
            gp = norm_back(gu, n_, flat(k.r[to])[:, 0:1], vec[2:3])
            gps = split(gp)
            q = 1 / (1 + jnp.exp(-a))
            ga = dot3(gps, (w2h[...], w2l[...]), NT) * (q * (1 + a * (1 - q)))
            gas = split(ga)
            for i, x in enumerate((*split(a * q), *gps, *gas)):
                k.ops[i, pl.ds(s * rows, cs * rows)] = x
            for t in range(cs):
                both = jnp.concatenate([x[t * rows:(t + 1) * rows] for x in gas], axis=0)
                k.ssb[s + t] = dot1(k.scatter[...], both, NN)
            sums.append(column_sums(ga, gp, gu * n_, gu))
        ss = split(k.ssb[:, 0:W].reshape(g * W, F))
        sr = split(k.ssb[:, W:].reshape(g * W, F))
        for i, x in enumerate((*ss, *sr)):
            k.sops[i] = x
        wg = dot3(ss, (w1h[F:2 * F], w1l[F:2 * F]), NT) + dot3(sr, (w1h[2 * F:], w1l[2 * F:]), NT)
        k.wgb[...] = wg.reshape(g, W, F)
        k.wgb[:, nr:2 * nr] += k.gv[...]
        sides = window_parts(k, k.wgb, nr)
        store(sides[0], k.box_a.at[pl.ds(box[2], g)])
        store(sides[2], k.box_b.at[pl.ds(box[2], g)])
        k.own[...] = k.wgb[:, nr:2 * nr]
        k.dv[...] = sum(sums[1:], sums[0])
        store.wait()

    free = dict(ge=ge[0], gg=[gg[0][0], gg[2][0]])
    vmem = dict(**w, vec=vec, a=stash.out_a, n=stash.out_n, r=stash.out_r, gv=gv, gg_own=gg[1], gather=hot.gather, scatter=hot.scatter)
    old = box[0] or (None, None)
    outs = dict(own=near(g, nr, F), ops=near(6, g * rows, F, dtype=bf16), sops=near(4, g * W, F, dtype=bf16), dv=near(8, F))
    grow = dict(box_a=(old[0], far(box[1], nr, F)), box_b=(old[1], far(box[1], nr, F)))
    scratch = dict(gb=pltpu.VMEM((g, rows, F), f32), ggb=pltpu.VMEM((g, W, F), f32), gg2=pltpu.VMEM((g, 2 * W, F), bf16), ssb=pltpu.VMEM((g, 2 * W, F), f32), wgb=pltpu.VMEM((g, W, F), f32))
    return call(body, "edge_backward", dict(here=here), active=active, vmem=vmem, free=free, outs=outs, grow=grow, scratch=scratch, after=after, micros=micros)


def add_parts(active, here, views, own, n, grad, relay, after):
    g, (nr, F) = sum(x.shape[0] for x in own), own[0].shape[1:]

    def body(k):
        wait(*load_views(k, views, k.views, [k.pb.at[i] for i in (0, 1)], g))
        done = 0
        for x in k.own:
            to = pl.ds(done, x.shape[0])
            k.pb[0, to] = k.pb[0, to] + k.pb[1, to] + x[...]
            done += x.shape[0]
        if relay:
            k.store(k.pb.at[0], k.out)
        k.store(k.pb.at[0], k.grad.at[pl.ds(n, g)])
        k.store.wait()

    outs = dict(out=far(g, nr, F)) if relay else {}
    grow = dict(grad=(grad[0], far(grad[1], nr, F)))
    return call(body, "add_parts", dict(here=here), active=active, vmem=dict(own=own), free=dict(views=arrays(views)), outs=outs, grow=grow, scratch=dict(pb=pltpu.VMEM((2, g, nr, F), f32)), after=after, micros=0.01)


def edge_out(g, active, here, weights, ge, n, ops, w, grad, relay, after, micros):
    rows, F = ge[0].shape[1:]
    halves = (0, 1) if g % 2 == 0 else (0,)
    m = g // len(halves)

    def body(k):
        cs = [k.load(k.ge.at[pl.ds(ge[1] + i * m, m)], k.gb.at[pl.ds(i * m, m)]) for i in halves]
        w1h, w1l = k.w1
        for i in halves:
            own = dot3([k.ops[x, pl.ds(i * m * rows, m * rows)] for x in (4, 5)], (w1h[0:F], w1l[0:F]), NT)
            cs[i].wait()
            if weights:
                for t in range(i * m, (i + 1) * m):
                    k.gb[t] = k.gb[t] * sample_weight(k, n + t, *weights)
            to = pl.ds(i * m, m)
            k.gb[to] = k.gb[to] + own.reshape(m, rows, F)
            if relay:
                k.store(k.gb.at[to], k.out_ge.at[to])
            k.store(k.gb.at[to], k.grad.at[pl.ds(n + i * m, m)])
        k.store.wait()

    outs = dict(out_ge=far(g, rows, F)) if relay else {}
    grow = dict(grad=(grad[0], far(grad[1], rows, F)))
    return call(body, "edge_out", dict(here=here), active=active, vmem=dict(ops=ops, w1=w["w1"]), free=dict(ge=ge[0]), outs=outs, grow=grow, scratch=dict(gb=pltpu.VMEM((g, rows, F), f32)), after=after, micros=micros)


def edge_weights(g, active, here, b, node_dv, e, v, pad, acc, first, after, micros):
    rows, F = e[0].shape[1:]
    nr = v[0][0].shape[1]
    W = 3 * nr

    def body(k):
        ce = k.load(k.e.at[pl.ds(e[1], g)], k.eb)
        cv = load_views(k, v, k.v, window_parts(k, k.vb, nr), g)
        o = k.ops

        def put(total, i, x, y):
            part = pl.ds(i * F, F)
            d = dot3(x, y, TN)
            total[part] = d if first else total[part] + d

        put(k.total_2, 0, (o[0], o[1]), (o[2], o[3]))
        if first:
            k.total_2[F:] = jnp.zeros((pad, F), f32)
        k.total_2[F:F + 8] += k.dv[...]
        if node_dv:
            k.total_2[F + 8:F + 16] = sum([x[...] for x in k.node_dv[1:]], k.node_dv[0][...])
        wait(*cv)
        vs = split(k.vb[...].reshape(g * W, F))
        for i in (0, 1):
            put(k.total_1, i + 1, vs, (k.sops[2 * i], k.sops[2 * i + 1]))
        ce.wait()
        put(k.total_1, 0, split(k.eb[...].reshape(g * rows, F)), (o[4], o[5]))

    vmem = dict(ops=b.ops, sops=b.sops, dv=b.dv)
    if node_dv:
        vmem.update(node_dv=node_dv)
    grow = dict(total_1=(acc and acc.total_1, near(3 * F, F)), total_2=(acc and acc.total_2, near(F + pad, F)))
    scratch = dict(eb=pltpu.VMEM((g, rows, F), f32), vb=pltpu.VMEM((g, W, F), f32))
    return call(body, "edge_weights", dict(here=here), active=active, vmem=vmem, free=dict(e=e[0], v=arrays(v)), grow=grow, scratch=scratch, after=after, micros=micros)


def gate(after, *xs):
    return call(lambda k: None, "gate", grow={name: (x, far(*x.shape)) for name, x in zip("xyz", xs)}, after=after, micros=0.01)


class Total:
    def __init__(self, x, here, orders, cuts):
        count = lax.axis_size("node")
        self.here, self.orders = dict(here=here), orders
        self.swaps = [[(i, i ^ (1 << (y if i % 2 else x))) for i in range(count)] for x, y in zip(*orders)]
        self.x, self.cuts = x, cuts
        self.rows, self.F = x.shape
        self.sizes, rows = [], self.rows
        while len(self.sizes) < len(self.swaps) and rows % 16 == 0:
            rows //= 2
            self.sizes.append(rows)
        self.got, self.result, self.token, self.done = [], None, None, False
        self.steps = self.run()

    def flag(self, ref, step):
        x, y = (order[step] for order in self.orders)
        node = ref.here[1]
        return jnp.where(node % 2 == 1, node >> y, node >> x) & 1

    def partial(self, k):
        K, sizes = len(self.sizes), self.sizes
        size = sizes[min(k, K - 1)]

        def body(ref):
            def start(after):
                at = sum(self.flag(ref, m) * sizes[m] for m in range(after + 1, k)) if after + 1 < k else 0
                if k < K:
                    at = at + (1 - self.flag(ref, k)) * size
                return pl.multiple_of(at, 8)

            cs = [ref.load(x.at[pl.ds(start(j), size)], ref.buf.at[j]) for j, x in enumerate(ref.got)]
            total = ref.x[pl.ds(start(-1), size)]
            for j in range(k):
                cs[j].wait()
                total = total + ref.buf[j]
            ref.out[...] = total

        scratch = dict(buf=pltpu.VMEM((max(k, 1), size, self.F), f32))
        r = call(body, "partial_sum", self.here, vmem=dict(x=self.x), free=dict(got=self.got[:k]), outs=dict(out=near(size, self.F)), scratch=scratch, after=self.after)
        self.token = (r.token,)
        return r.out

    def add(self, x, y):
        def body(k):
            k.load(k.y, k.buf).wait()
            k.out[...] = k.x[...] + k.buf[...]

        r = call(body, "add", vmem=dict(x=x), free=dict(y=y), outs=dict(out=near(*x.shape)), scratch=dict(buf=pltpu.VMEM(x.shape, f32)), after=self.after)
        self.token = (r.token,)
        return r.out

    def join(self, own, got, step):
        R = own.shape[0]

        def body(k):
            bit = self.flag(k, step)
            mine, other = pl.multiple_of(bit * R, 8), pl.multiple_of((1 - bit) * R, 8)
            c = k.load(k.got, k.joined.at[pl.ds(other, R)])
            k.joined[pl.ds(mine, R)] = k.own[...]
            c.wait()

        def last_body(k):
            body(k)
            done = 0
            for ref, rows in zip(k.out, self.cuts):
                k.store(k.joined.at[pl.ds(done, rows)], ref)
                done += rows
            k.store.wait()

        joined = (2 * R, self.F)
        if step:
            outs, scratch = dict(joined=near(*joined)), {}
        else:
            outs, scratch = {f"out{i}": far(n, self.F) for i, n in enumerate(self.cuts)}, dict(joined=pltpu.VMEM(joined, f32))

        def run(k):
            if step:
                body(k)
            else:
                k.out = [getattr(k, key) for key in outs]
                last_body(k)

        r = call(run, "join", self.here, vmem=dict(own=own), free=dict(got=got), outs=outs, scratch=scratch, after=self.after)
        self.token = (r.token,)
        return [getattr(r, key) for key in outs]

    def run(self):
        K = len(self.sizes)
        for k in range(K):
            send = self.partial(k)
            self.got.append(lax.ppermute(send, "node", self.swaps[k]))
            yield
        own = self.partial(K)
        for pairs in self.swaps[K:]:
            got = lax.ppermute(own, "node", pairs)
            yield
            own = self.add(own, got)
        for k in reversed(range(K)):
            got = lax.ppermute(own, "node", self.swaps[k])
            yield
            self.result = self.join(own, got, k)
            own = self.result[0]
        self.done = True

    def step(self, after):
        if self.done:
            return after
        self.after = after
        next(self.steps, None)
        return self.token


def on_device(in_nodes, in_edges, senders, receivers, edge_w1, edge_w2, edge_vec, node_w1, node_w2, node_vec, cot_nodes, cot_edges, lengths, step_mask):
    samples, nr, F = in_nodes.shape
    count = lax.axis_size("node")
    section, node = lax.axis_index("section"), lax.axis_index("node")
    evec, nvec = edge_vec[0], node_vec[0]
    here = jnp.concatenate([jnp.stack([section, node, count]).astype(jnp.int32), lengths, step_mask.reshape(-1)])
    live = step_mask.shape

    def partner(i, side):
        return i ^ 1 if side == 0 else (i - 1 + 2 * (i % 2)) % count

    def swap(x, side, planes):
        if planes is None:
            return lax.ppermute(x, "node", [(i, partner(i, side)) for i in range(count)])
        return lax.ppermute(x, ("section", "node"), [(s * count + i, s * count + partner(i, side)) for s in planes for i in range(count)])

    def beside(to_a, to_b, planes=None):
        return swap(to_a, 0, planes), swap(to_b, 1, planes)

    def across(x, source, side=None):
        if side is None:
            return lax.ppermute(x, "section", [(source, 1 - source)])
        return lax.ppermute(x, ("section", "node"), [(source * count + i, (1 - source) * count + partner(i, side)) for i in range(count)])

    p, q = [(sum(group_sizes[:i]), n) for i, n in enumerate(group_sizes)]
    both = p[1] + q[1]
    pad = 8 * count
    act_e = act_n = acc_n = acc_e = grad_e = grad_n = None
    after = ()

    def done(r):
        nonlocal after
        after = (r.token,)
        return r

    def stay(r, *names):
        r.kept = [getattr(r, name) for name in names]
        resident.extend(r.kept)
        return r

    def leave(*rs):
        for r in rs:
            resident[:] = [x for x in resident if all(x is not y for y in r.kept)]

    resident.clear()
    from_a, from_b = beside(in_nodes, in_nodes)
    hot, ew = prepare(edge_w1[0], edge_w2[0], (senders.reshape(1, -1), receivers.reshape(1, -1)), here, 3 * nr)

    def forward_0(c):
        nonlocal act_e
        v = [(x, c[0]) for x in (from_a, in_nodes, from_b)]
        f = done(edge_forward(c[1], 0, here, (in_edges, c[0]), v, c[0], hot, ew, evec, (act_e, samples), (None, c[1], 0), True, after, 0.01))
        act_e, f.v, f.e = f.act, v, (in_edges, c[0])
        return stay(f, "out_a", "out_n", "out_r")

    def nodes_0(c, f, got):
        nonlocal act_n
        m = done(node_stage(c[1], True, False, 0, here, (in_nodes, c[0]), c[0], nw, nvec, [(got[0], 0), (f.own, 0), (got[1], 0)], act=(act_n, samples), after=after, micros=0.01))
        act_n = m.act
        return stay(m, "out_a", "out_n", "out_r", "out_g")

    def forward_1(c, e, nodes, box):
        nonlocal act_e
        v = [(x, 0) for x in nodes]
        f = done(edge_forward(c[1], 1, here, (e, 0), v, c[0], hot, ew, evec, (act_e, samples), box, False, after, 0.01))
        act_e, f.v, f.e = f.act, v, (e, 0)
        return stay(f, "out_a", "out_n", "out_r")

    def middle_1(c, f, got, at, box):
        nonlocal act_n
        m = done(node_stage(c[1], True, True, 1, here, f.v[1], c[0], nw, nvec, [(got[0], at), (f.own, 0), (got[1], at)], act=(act_n, samples), weights=live, cot=cot_nodes, box=box, after=after, micros=0.01))
        act_n = m.act
        return stay(m, "ops", "dv", "own", "out_gv")

    def backward_1(c, f, m, got, at, box):
        b = done(edge_backward(c[1], 1, here, live, (cot_edges, c[0]), ((got[0], at), m.own, (got[1], at)), c[0], f, m.out_gv, hot, ew, evec, box, after, 0.01))
        leave(f)
        return stay(b, "ops", "sops", "dv", "own")

    def add_1(c, b, got, at):
        nonlocal grad_n
        r = done(add_parts(1, here, [(x, at) for x in got], [b.own], c[0], (grad_n, samples), True, after))
        grad_n = r.grad
        return across(r.out, 1)

    def out_1(c, b):
        nonlocal grad_e
        r = done(edge_out(c[1], 1, here, live, (cot_edges, c[0]), c[0], b.ops, ew, (grad_e, samples), True, after, 0.01))
        grad_e = r.grad
        return across(r.out_ge, 1)

    def middle_0(c, gv, stash):
        m = done(node_stage(c[1], False, True, 0, here, (in_nodes, c[0]), c[0], nw, nvec, [(gv, 0)], stash=stash, box=(None, c[1], 0), after=after, micros=50))
        m.got = beside(m.box_a, m.box_b, (0,))
        leave(stash)
        return stay(m, "ops", "dv", "own", "out_gv")

    def backward_0(c, ge, f, m, box):
        b = done(edge_backward(c[1], 0, here, None, (ge, 0), ((m.got[0], 0), m.own, (m.got[1], 0)), c[0], f, m.out_gv, hot, ew, evec, box, after, 50))
        leave(f)
        return stay(b, "ops", "sops", "dv", "own")

    def out_0(c, ge, b):
        nonlocal grad_e
        grad_e = done(edge_out(c[1], 0, here, None, (ge, 0), c[0], b.ops, ew, (grad_e, samples), False, after, 2)).grad

    def node_grads(on, m, first):
        nonlocal acc_n
        acc_n = done(node_weights(on, here, m, acc_n, first, after))
        leave(m)

    def edge_grads(on, c, b, f, first, node_dv=()):
        nonlocal acc_e
        acc_e = done(edge_weights(c[1], on, here, b, list(node_dv), f.e, f.v, pad, acc_e, first, after, 2))
        leave(b)

    f0p = forward_0(p)
    got = beside(f0p.box_a, f0p.box_b)
    e0 = across(f0p.out_e, 0)
    _, nw = prepare(node_w1[0], node_w2[0], after=after)
    n0p = nodes_0(p, f0p, got)
    v0 = [across(n0p.out_v, 0, side) for side in (0, None, 1)]
    f0q = forward_0(q)
    held = done(gate(after + tuple(v0), f0q.out_e, f0q.box_a, f0q.box_b))
    e1 = across(held.x, 0)
    got_q = beside(held.y, held.z, (0,))
    f1p = forward_1(p, e0, v0, (None, p[1], 0))
    got = beside(f1p.box_a, f1p.box_b)
    n0q = nodes_0(q, f0q, got_q)
    v1, y = across(n0q.out_v, 0), across(n0q.out_v, 0, 1)
    n1p = middle_1(p, f1p, got, 0, (None, both, 0))
    v1 = done(gate(after, v1)).x
    f1q = forward_1(q, e1, (swap(v1, 0, None), v1, y), ((n1p.box_a, n1p.box_b), both, p[1]))
    got = beside(f1q.box_a, f1q.box_b)
    b1p = backward_1(p, f1p, n1p, got, 0, (None, both, 0))
    n1q = middle_1(q, f1q, got, p[1], ((b1p.box_a, b1p.box_b), both, p[1]))
    got = beside(n1q.box_a, n1q.box_b)
    gv0 = add_1(p, b1p, got, 0)
    ge0 = out_1(p, b1p)
    b1q = backward_1(q, f1q, n1q, got, p[1], (None, q[1], 0))
    got = beside(b1q.box_a, b1q.box_b)
    m0p = middle_0(p, gv0, n0p)
    gv1 = add_1(q, b1q, got, 0)
    ge1 = out_1(q, b1q)
    node_grads(1, n1p, True)
    node_grads(1, n1q, False)
    edge_grads(1, p, b1p, f1p, True)
    edge_grads(1, q, b1q, f1q, False, (n1p.dv, n1q.dv))
    b0p = backward_0(p, ge0, f0p, m0p, (None, both, 0))
    m0q = middle_0(q, gv1, n0q)
    edge_grads(0, p, b0p, f0p, True)
    node_grads(0, m0p, True)
    node_grads(0, m0q, False)
    b0q = backward_0(q, ge1, f0q, m0q, ((b0p.box_a, b0p.box_b), both, p[1]))
    bits = list(range(count.bit_length() - 1))
    yzz, zyz, yzz_turned = [[0] + [bits[i] for i in order] + bits[4:] for order in ((1, 2, 3), (2, 1, 3), (1, 3, 2))]
    total_n = Total(acc_n.total, here, (yzz, zyz), (2 * F, F))
    after = total_n.step(after)
    edge_grads(0, q, b0q, f0q, False, (m0p.dv, m0q.dv))
    total_a = Total(acc_e.total_1, here, (yzz_turned, zyz), (3 * F,))
    total_b = Total(acc_e.total_2, here, (yzz, zyz), (F, pad))
    totals = [total_n, total_a, total_b]
    after = total_a.step(after)
    after = total_b.step(after)
    for t in totals:
        after = t.step(after)
    out_0(p, ge0, b0p)
    out_0(q, ge1, b0q)
    for t in totals:
        after = t.step(after)
    held = done(gate(after, b0q.box_a, b0q.box_b))
    got = beside(held.x, held.y, (0,))
    for t in totals:
        after = t.step(after)
    grad_n = done(add_parts(0, here, [(x, 0) for x in got], [b0p.own, b0q.own], 0, (grad_n, samples), False, after)).grad
    while not all(t.done for t in totals):
        for t in totals:
            after = t.step(after)
    vecs = total_b.result[1]
    return (
        act_n[None], act_e[None], grad_n[None], grad_e[None],
        total_a.result[0][None], total_b.result[0][None], vecs[None, 0:4],
        total_n.result[0][None], total_n.result[1][None], vecs[None, 8:12],
    )


def solution(mesh):
    nodes, rows, weights = P(None, "node", None), P("node"), P("section", None, None)
    stacked = P("section", None, "node", None)
    in_specs = (nodes, nodes, rows, rows) + (weights,) * 6 + (nodes, nodes, P(), P())
    out_specs = (stacked,) * 4 + (weights,) * 6
    return jax.shard_map(on_device, mesh=mesh, in_specs=in_specs, out_specs=out_specs, check_vma=False)
```

```python
from types import SimpleNamespace

import jax
import jax.numpy as jnp
from jax import lax
from jax.experimental import pallas as pl
from jax.experimental.pallas import tpu as pltpu
from jax.sharding import PartitionSpec as P

f32, bf16 = jnp.float32, jnp.bfloat16
norm_eps = 1e-05
NN = ((1,), (0,))
NT = ((1,), (1,))
TN = ((0,), (0,))
group_sizes = (4, 4)
relay_sizes = ((2, 2), (2, 2))
MIB = 1024 * 1024


def split(x):
    hi = x.astype(bf16)
    return hi, (x - hi.astype(f32)).astype(bf16)


def dot1(a, b, dims):
    return lax.dot_general(a, b, (dims, ((), ())), preferred_element_type=f32)


def dot3(a, b, dims):
    return dot1(a[0], b[0], dims) + (dot1(a[0], b[1], dims) + dot1(a[1], b[0], dims))


def dot3_few(a, b, dims):
    rows = a[0].shape[0]
    both = dot1(jnp.concatenate(a, axis=0), b[0], dims)
    return both[:rows] + (both[rows:] + dot1(a[0], b[1], dims))


def normalized(u):
    c = u - jnp.mean(u, axis=-1, keepdims=True)
    r = lax.rsqrt(jnp.mean(c * c, axis=-1, keepdims=True) + norm_eps)
    return c * r, r


def norm_back(gu, n, r, gain):
    t = gu * gain
    return r * (t - jnp.mean(t, axis=-1, keepdims=True) - n * jnp.mean(t * n, axis=-1, keepdims=True))


def column_sums(*xs):
    F = xs[0].shape[-1]
    return jnp.concatenate([jnp.sum(x, axis=0, keepdims=True) for x in xs] + [jnp.zeros((8 - len(xs), F), f32)], axis=0)


class Copies:
    def __init__(self, sems):
        self.sems, self.all = sems, []

    def __call__(self, src, dst):
        c = pltpu.make_async_copy(src, dst, self.sems.at[len(self.all)])
        self.all.append(c)
        c.start()
        return c

    def wait(self):
        wait(*self.all)


def wait(*copies):
    for c in copies:
        c.wait()


def far(*shape, dtype=f32):
    return pltpu.HBM(shape, dtype)


def near(*shape, dtype=f32):
    return pltpu.VMEM(shape, dtype)


resident = []


def loose(*shape):
    return jax.ShapeDtypeStruct(shape, f32)


def call(body, name, scalars={}, hbm={}, vmem={}, free={}, outs={}, grow={}, scratch={}, after=(), micros=2, copies=24, active=None):
    args, specs, where = [], [], {}

    def add(values, space, pinned):
        for key, value in values.items():
            at = []
            for x in value if isinstance(value, (list, tuple)) else [value]:
                at.append(len(args))
                args.append(pltpu.with_memory_space_constraint(x, space) if pinned else x)
                specs.append(pl.BlockSpec(memory_space=space))
            where[key] = at if isinstance(value, (list, tuple)) else at[0]

    add(scalars, pltpu.SMEM, False)
    add(hbm, pltpu.HBM, True)
    add(vmem, pltpu.VMEM, True)
    add(free, pl.ANY, False)
    add(dict(after=[x for x in after if x.shape == (8, 128)]), pltpu.HBM, True)
    add(dict(arrived=[x for x in after if x.shape != (8, 128)]), pl.ANY, False)
    used = {id(x) for value in vmem.values() for x in (value if isinstance(value, (list, tuple)) else [value])}
    add(dict(kept=[x for x in resident if id(x) not in used]), pltpu.VMEM, True)
    shapes, out_specs, aliases = [], [], {}
    for key, value in list(outs.items()) + list(grow.items()) + [("token", far(8, 128))]:
        old, shape = value if key in grow else (None, value)
        space = pl.ANY if isinstance(shape, jax.ShapeDtypeStruct) else shape.memory_space
        where[key] = -1 - len(shapes)
        if old is not None:
            aliases[len(args)] = len(shapes)
            args.append(old if space is pl.ANY else pltpu.with_memory_space_constraint(old, space))
            specs.append(pl.BlockSpec(memory_space=space))
        shapes.append(shape)
        out_specs.append(pl.BlockSpec(memory_space=space))
    first_out, first_scratch = len(args), len(args) + len(shapes)
    kept = dict(scratch)

    def kernel(*refs):
        k = SimpleNamespace()
        pick = lambda i: refs[i] if i >= 0 else refs[first_out - 1 - i]
        for key, at in where.items():
            setattr(k, key, [pick(i) for i in at] if isinstance(at, list) else pick(at))
        for i, key in enumerate(kept):
            setattr(k, key, refs[first_scratch + i])
        k.load, k.store = Copies(refs[-2]), Copies(refs[-1])
        if active is None:
            body(k)
        else:
            pl.when(k.here[0] == active)(lambda: body(k))

    res = pl.pallas_call(
        kernel,
        out_shape=shapes,
        in_specs=specs,
        out_specs=out_specs,
        scratch_shapes=list(kept.values()) + [pltpu.SemaphoreType.DMA((copies,))] * 2,
        input_output_aliases=aliases,
        compiler_params=pltpu.CompilerParams(vmem_limit_bytes=12 * MIB),
        cost_estimate=pl.CostEstimate(flops=int(micros * 1.15e9), bytes_accessed=0, transcendentals=0),
        name=name,
    )(*args)
    return SimpleNamespace(**{key: res[-1 - at] for key, at in where.items() if not isinstance(at, list) and at < 0})


def prepare(w1, w2, ends=None, here=None, W=0, after=()):
    F = w1.shape[1]

    def body(k):
        c1, c2 = k.load(k.w1, k.b1), k.load(k.w2, k.b2)
        if ends is not None:
            hots = []
            for src, ref in zip(k.ends, (k.e0, k.e1)):
                k.load(src, ref).wait()
                total = k.here[2] * (W // 3)
                at = ref[...] - (k.here[1] - 1) * (W // 3)
                at = jnp.where(at < 0, at + total, at)
                at = jnp.where(at >= total, at - total, at)
                hots.append((lax.broadcasted_iota(jnp.int32, (W, at.shape[1]), 0) == at).astype(f32).astype(bf16))
            both = jnp.concatenate(hots, axis=0)
            k.gather[...] = jnp.concatenate([both, both], axis=0)
            k.scatter[...] = jnp.concatenate([both, both], axis=1)
        c2.wait()
        k.h2[...], k.l2[...] = split(k.b2[...])
        c1.wait()
        k.h1[...], k.l1[...] = split(k.b1[...])

    half = lambda *s: near(*s, dtype=bf16)
    outs = dict(h1=half(*w1.shape), l1=half(*w1.shape), h2=half(*w2.shape), l2=half(*w2.shape))
    scalars, hbm = {}, dict(w1=w1, w2=w2)
    scratch = dict(b1=pltpu.VMEM(w1.shape, f32), b2=pltpu.VMEM(w2.shape, f32))
    if ends is not None:
        rows = ends[0].shape[1]
        outs.update(gather=half(4 * W, rows), scatter=half(2 * W, 2 * rows))
        scalars = dict(here=here)
        hbm.update(ends=list(ends))
        scratch.update(e0=pltpu.VMEM((1, rows), jnp.int32), e1=pltpu.VMEM((1, rows), jnp.int32))
    r = call(body, "prepare", scalars, hbm, outs=outs, scratch=scratch, after=after)
    resident.extend([r.h1, r.l1, r.h2, r.l2])
    if ends is not None:
        resident.extend([r.gather, r.scatter])
    return r, dict(w1=[r.h1, r.l1], w2=[r.h2, r.l2])


def side_rows(par, nr):
    return pl.multiple_of((1 - par) * 2 * nr, 16), pl.multiple_of(par * 2 * nr, 16)


def window_parts(k, ref, nr):
    a_at, b_at = side_rows(k.here[1] % 2, nr)
    return [ref.at[:, pl.ds(a_at, nr), :], ref.at[:, nr:2 * nr, :], ref.at[:, pl.ds(b_at, nr), :]]


def sample_weight(k, sample, micro, steps):
    m, t = divmod(sample, steps)
    return jnp.where(t < k.here[3 + m], k.here[3 + micro + sample], 0).astype(f32)


def load_views(k, views, refs, targets, g):
    return [k.load(ref.at[pl.ds(view[1], g)], target) for view, ref, target in zip(views, refs, targets)]


def arrays(views):
    return [v[0] for v in views]


def chunk(g):
    return 2 if g % 2 == 0 else 1


def edge_forward(g, active, here, e, v, n, hot, w, vec, act, box, relay, after, micros):
    rows, F = e[0][0].shape[1:]
    nr = v[0][0].shape[1]
    W = 3 * nr
    cs = chunk(g)

    def body(k):
        load, store = k.load, k.store
        cv = load_views(k, v, k.v, window_parts(k, k.vb, nr), g)
        ce = load_views(k, e, k.e, [k.eb.at[pl.ds(s, cs)] for s in range(0, g, cs)], cs)
        (w1h, w1l), (w2h, w2l), vec = k.w1, k.w2, k.vec
        wait(*cv)
        vw = split(k.vb[...].reshape(g * W, F))
        for i in (0, 1):
            part = pl.ds((i + 1) * F, F)
            h, l = split(dot3(vw, (w1h[part], w1l[part]), NN).reshape(g, W, F))
            k.pp[:, i * W:(i + 1) * W] = h
            k.pp[:, (i + 2) * W:(i + 3) * W] = l
        for s in range(0, g, cs):
            ce[s // cs].wait()
            to = pl.ds(s, cs)
            x = k.eb[to].reshape(cs * rows, F)
            a = dot3(split(x), (w1h[0:F], w1l[0:F]), NN) + vec[0:1]
            a = a + jnp.concatenate([dot1(k.gather[...], k.pp[s + t], TN) for t in range(cs)], axis=0)
            k.out_a[to] = a.reshape(cs, rows, F)
            h = a / (1 + jnp.exp(-a))
            n_, r = normalized(dot3(split(h), (w2h[...], w2l[...]), NN) + vec[1:2])
            k.out_n[to] = n_.reshape(cs, rows, F)
            k.out_r[to] = jnp.broadcast_to(r, (cs * rows, 128)).reshape(cs, rows, 128)
            m = n_ * vec[2:3] + vec[3:4]
            k.ob[to] = (x + m).reshape(cs, rows, F)
            if relay:
                store(k.ob.at[to], getattr(k, relays[s][0]).at[pl.ds(relays[s][1], cs)])
            store(k.ob.at[to], k.act.at[pl.ds(n + s, cs)])
            mh, ml = split(m.reshape(cs, rows, F))
            for t in range(cs):
                k.sb[s + t] = dot1(k.scatter[W:], jnp.concatenate([mh[t], ml[t]], axis=0), NN)
        sides = window_parts(k, k.sb, nr)
        store(sides[0], k.box_a.at[pl.ds(box[2], g)])
        store(sides[1], k.own)
        store(sides[2], k.box_b.at[pl.ds(box[2], g)])
        store.wait()

    outs = dict(out_a=near(g, rows, F), out_n=near(g, rows, F), out_r=near(g, rows, 128), own=far(g, nr, F))
    names = "abcd"[:len(relay)]
    outs.update({key: far(size, rows, F) for key, size in zip(names, relay)})
    relays = [(key, at) for key, size in zip(names, relay) for at in range(size)]
    old = box[0] or (None, None)
    grow = dict(act=(act[0], far(act[1], rows, F)), box_a=(old[0], far(box[1], nr, F)), box_b=(old[1], far(box[1], nr, F)))
    full = pltpu.VMEM((g, rows, F), f32)
    scratch = dict(eb=full, ob=full, vb=pltpu.VMEM((g, W, F), f32), sb=pltpu.VMEM((g, W, F), f32), pp=pltpu.VMEM((g, 4 * W, F), bf16))
    r = call(body, "edge_forward", dict(here=here), active=active, vmem=dict(**w, gather=hot.gather, scatter=hot.scatter, vec=vec), free=dict(e=arrays(e), v=arrays(v)), outs=outs, grow=grow, scratch=scratch, after=after, micros=micros)
    r.relay = [getattr(r, key) for key in names]
    return r


def node_stage(g, forward, backward, active, here, v, n, w, vec, parts, act=None, stash=None, weights=None, cot=None, box=None, after=(), micros=2):
    nr, F = v[0].shape[1:]
    R = g * nr

    def body(k):
        load, store = k.load, k.store
        cx = [load(k.v.at[pl.ds(v[1], g)], k.zb.at[:, :, 0:F])] + load_views(k, parts, k.parts, [k.pb.at[i] for i in range(len(parts))], g)
        if forward and backward:
            cx.append(load(k.cot.at[pl.ds(n, g)], k.gb))
        w1, w2, vec = (k.w1[0][...], k.w1[1][...]), (k.w2[0][...], k.w2[1][...]), k.vec
        wait(*cx)
        given = sum([k.pb[i] for i in range(1, len(parts))], k.pb[0])
        k.zb[:, :, F:] = given if forward else k.gathered[...]
        z = k.zb[...].reshape(R, 2 * F)
        zs = split(z)
        if forward:
            a = dot3_few(zs, w1, NN) + vec[0:1]
            h = a / (1 + jnp.exp(-a))
            n_, r = normalized(dot3_few(split(h), w2, NN) + vec[1:2])
            k.ob[...] = (z[:, :F] + n_ * vec[2:3] + vec[3:4]).reshape(g, nr, F)
            if not backward:
                store(k.ob, k.out_v)
                k.out_a[...] = a.reshape(g, nr, F)
                k.out_n[...] = n_.reshape(g, nr, F)
                k.out_r[...] = jnp.broadcast_to(r, (R, 128)).reshape(g, nr, 128)
                k.out_g[...] = given
            store(k.ob, k.act.at[pl.ds(n, g)])
        else:
            a, n_, r = k.a[...].reshape(R, F), k.n[...].reshape(R, F), k.r[...].reshape(R, 128)[:, 0:1]
        if backward:
            if forward:
                for s in range(g):
                    k.gb[s] = k.gb[s] * sample_weight(k, n + s, *weights)
                gu = k.gb[...].reshape(R, F)
            else:
                gu = given.reshape(R, F)
            gp = norm_back(gu, n_, r, vec[2:3])
            q = 1 / (1 + jnp.exp(-a))
            hs, gps = split(a * q), split(gp)
            ga = dot3_few(gps, w2, NT) * (q * (1 + a * (1 - q)))
            gas = split(ga)
            gz = dot3_few(gas, w1, NT)
            k.ggb[...] = gz[:, F:].reshape(g, nr, F)
            for ref in (k.box_a, k.box_b):
                store(k.ggb, ref.at[pl.ds(box[2], g)])
            k.own[...] = k.ggb[...]
            k.out_gv[...] = (gu + gz[:, :F]).reshape(g, nr, F)
            for i, x in enumerate((zs[0][:, :F], zs[1][:, :F], zs[0][:, F:], zs[1][:, F:], hs[0], hs[1], gas[0], gas[1], gps[0], gps[1])):
                k.ops[i] = x
            k.dv[...] = column_sums(ga, gp, gu * n_, gu)
        store.wait()

    hbm, vmem, free = {}, dict(**w, vec=vec), dict(v=v[0], parts=arrays(parts))
    shape = near(g, nr, F)
    outs, grow = {}, {}
    if not forward:
        vmem.update(a=stash.out_a, n=stash.out_n, r=stash.out_r, gathered=stash.out_g)
    elif backward:
        hbm.update(cot=cot)
    if forward:
        grow.update(act=(act[0], far(act[1], nr, F)))
        if not backward:
            outs.update(out_v=far(g, nr, F), out_a=shape, out_n=shape, out_r=near(g, nr, 128), out_g=shape)
    if backward:
        old = box[0] or (None, None)
        outs.update(own=shape, out_gv=shape, ops=near(10, R, F, dtype=bf16), dv=near(8, F))
        grow.update(box_a=(old[0], far(box[1], nr, F)), box_b=(old[1], far(box[1], nr, F)))
    small = pltpu.VMEM((g, nr, F), f32)
    scratch = dict(zb=pltpu.VMEM((g, nr, 2 * F), f32), pb=pltpu.VMEM((len(parts), g, nr, F), f32), gb=small, ob=small, ggb=small)
    return call(body, "node_stage", dict(here=here), hbm, vmem, free, active=active, outs=outs, grow=grow, scratch=scratch, after=after, micros=micros)


def node_weights(active, here, m, acc, first, after):
    _, R, F = m.ops.shape

    def body(k):
        o = k.ops
        for i, (x, y) in enumerate(((0, 6), (2, 6), (4, 8))):
            part = pl.ds(i * F, F)
            d = dot3((o[x], o[x + 1]), (o[y], o[y + 1]), TN)
            k.total[part] = d if first else k.total[part] + d

    grow = dict(total=(acc and acc.total, near(3 * F, F)))
    return call(body, "node_weights", dict(here=here), active=active, vmem=dict(ops=m.ops), grow=grow, after=after, micros=0.01)


def edge_backward(g, active, here, weights, ge, gg, n, stash, gv, hot, w, vec, box, after, micros):
    rows, F = ge[0].shape[1:]
    nr = gv.shape[1]
    W = 3 * nr
    cs = 2 if g % 2 == 0 else 1

    def body(k):
        load, store = k.load, k.store
        gg_at = window_parts(k, k.ggb, nr)
        cg = load_views(k, (gg[0], gg[2]), k.gg, (gg_at[0], gg_at[2]), g)
        cx = [load(k.ge.at[pl.ds(ge[1] + s, cs)], k.gb.at[pl.ds(s, cs)]) for s in range(0, g, cs)]
        k.ggb[:, nr:2 * nr] = k.gg_own[...]
        (w1h, w1l), (w2h, w2l), vec = k.w1, k.w2, k.vec
        wait(*cg)
        h, l = split(k.ggb[...])
        k.gg2[:, 0:W] = h
        k.gg2[:, W:] = l
        flat = lambda x: x.reshape(cs * rows, x.shape[-1])
        sums = []
        for s in range(0, g, cs):
            to = pl.ds(s, cs)
            cx[s // cs].wait()
            if weights:
                for t in range(s, s + cs):
                    k.gb[t] = k.gb[t] * sample_weight(k, n + t, *weights)
            hot_r = k.gather[pl.ds(W, W)]
            gu = flat(k.gb[to]) + jnp.concatenate([dot1(hot_r, k.gg2[s + t, 0:W], TN) + dot1(hot_r, k.gg2[s + t, W:], TN) for t in range(cs)], axis=0)
            n_, a = flat(k.n[to]), flat(k.a[to])
            gp = norm_back(gu, n_, flat(k.r[to])[:, 0:1], vec[2:3])
            gps = split(gp)
            q = 1 / (1 + jnp.exp(-a))
            ga = dot3(gps, (w2h[...], w2l[...]), NT) * (q * (1 + a * (1 - q)))
            gas = split(ga)
            for i, x in enumerate((*split(a * q), *gps, *gas)):
                k.ops[i, pl.ds(s * rows, cs * rows)] = x
            for t in range(cs):
                both = jnp.concatenate([x[t * rows:(t + 1) * rows] for x in gas], axis=0)
                k.ssb[s + t] = dot1(k.scatter[...], both, NN)
            sums.append(column_sums(ga, gp, gu * n_, gu))
        ss = split(k.ssb[:, 0:W].reshape(g * W, F))
        sr = split(k.ssb[:, W:].reshape(g * W, F))
        for i, x in enumerate((*ss, *sr)):
            k.sops[i] = x
        wg = dot3(ss, (w1h[F:2 * F], w1l[F:2 * F]), NT) + dot3(sr, (w1h[2 * F:], w1l[2 * F:]), NT)
        k.wgb[...] = wg.reshape(g, W, F)
        k.wgb[:, nr:2 * nr] += k.gv[...]
        sides = window_parts(k, k.wgb, nr)
        store(sides[0], k.box_a.at[pl.ds(box[2], g)])
        store(sides[2], k.box_b.at[pl.ds(box[2], g)])
        k.own[...] = k.wgb[:, nr:2 * nr]
        k.dv[...] = sum(sums[1:], sums[0])
        store.wait()

    free = dict(ge=ge[0], gg=[gg[0][0], gg[2][0]])
    vmem = dict(**w, vec=vec, a=stash.out_a, n=stash.out_n, r=stash.out_r, gv=gv, gg_own=gg[1], gather=hot.gather, scatter=hot.scatter)
    old = box[0] or (None, None)
    outs = dict(own=near(g, nr, F), ops=near(6, g * rows, F, dtype=bf16), sops=near(4, g * W, F, dtype=bf16), dv=near(8, F))
    grow = dict(box_a=(old[0], far(box[1], nr, F)), box_b=(old[1], far(box[1], nr, F)))
    scratch = dict(gb=pltpu.VMEM((g, rows, F), f32), ggb=pltpu.VMEM((g, W, F), f32), gg2=pltpu.VMEM((g, 2 * W, F), bf16), ssb=pltpu.VMEM((g, 2 * W, F), f32), wgb=pltpu.VMEM((g, W, F), f32))
    return call(body, "edge_backward", dict(here=here), active=active, vmem=vmem, free=free, outs=outs, grow=grow, scratch=scratch, after=after, micros=micros)


def add_parts(active, here, views, own, n, grad, relay, after):
    g, (nr, F) = sum(x.shape[0] for x in own), own[0].shape[1:]

    def body(k):
        wait(*load_views(k, views, k.views, [k.pb.at[i] for i in (0, 1)], g))
        done = 0
        for x in k.own:
            to = pl.ds(done, x.shape[0])
            k.pb[0, to] = k.pb[0, to] + k.pb[1, to] + x[...]
            done += x.shape[0]
        if relay:
            k.store(k.pb.at[0], k.out)
        k.store(k.pb.at[0], k.grad.at[pl.ds(n, g)])
        k.store.wait()

    outs = dict(out=far(g, nr, F)) if relay else {}
    grow = dict(grad=(grad[0], far(grad[1], nr, F)))
    return call(body, "add_parts", dict(here=here), active=active, vmem=dict(own=own), free=dict(views=arrays(views)), outs=outs, grow=grow, scratch=dict(pb=pltpu.VMEM((2, g, nr, F), f32)), after=after, micros=0.01)


def edge_out(g, active, here, weights, ge, n, ops, w, grad, relay, after, micros):
    rows, F = ge[0].shape[1:]
    halves = (0, 1) if g % 2 == 0 else (0,)
    m = g // len(halves)

    def body(k):
        cs = [k.load(k.ge.at[pl.ds(ge[1] + i * m, m)], k.gb.at[pl.ds(i * m, m)]) for i in halves]
        w1h, w1l = k.w1
        for i in halves:
            own = dot3([k.ops[x, pl.ds(i * m * rows, m * rows)] for x in (4, 5)], (w1h[0:F], w1l[0:F]), NT)
            cs[i].wait()
            if weights:
                for t in range(i * m, (i + 1) * m):
                    k.gb[t] = k.gb[t] * sample_weight(k, n + t, *weights)
            to = pl.ds(i * m, m)
            k.gb[to] = k.gb[to] + own.reshape(m, rows, F)
            if relay:
                k.store(k.gb.at[to], k.out_ge.at[to])
            k.store(k.gb.at[to], k.grad.at[pl.ds(n + i * m, m)])
        k.store.wait()

    outs = dict(out_ge=far(g, rows, F)) if relay else {}
    grow = dict(grad=(grad[0], far(grad[1], rows, F)))
    return call(body, "edge_out", dict(here=here), active=active, vmem=dict(ops=ops, w1=w["w1"]), free=dict(ge=ge[0]), outs=outs, grow=grow, scratch=dict(gb=pltpu.VMEM((g, rows, F), f32)), after=after, micros=micros)


def edge_weights(g, active, here, b, node_dv, e, v, pad, acc, first, after, micros):
    rows, F = e[0][0].shape[1:]
    nr = v[0][0].shape[1]
    W = 3 * nr

    def body(k):
        cs = chunk(g)
        ce = load_views(k, e, k.e, [k.eb.at[pl.ds(s, cs)] for s in range(0, g, cs)], cs)
        cv = load_views(k, v, k.v, window_parts(k, k.vb, nr), g)
        o = k.ops

        def put(total, i, x, y):
            part = pl.ds(i * F, F)
            d = dot3(x, y, TN)
            total[part] = d if first else total[part] + d

        put(k.total, 3, (o[0], o[1]), (o[2], o[3]))
        if first:
            k.total[4 * F:] = jnp.zeros((pad, F), f32)
        k.total[4 * F:4 * F + 8] += k.dv[...]
        if node_dv:
            k.total[4 * F + 8:4 * F + 16] = sum([x[...] for x in k.node_dv[1:]], k.node_dv[0][...])
        wait(*cv)
        vs = split(k.vb[...].reshape(g * W, F))
        for i in (0, 1):
            put(k.total, i + 1, vs, (k.sops[2 * i], k.sops[2 * i + 1]))
        wait(*ce)
        put(k.total, 0, split(k.eb[...].reshape(g * rows, F)), (o[4], o[5]))

    vmem = dict(ops=b.ops, sops=b.sops, dv=b.dv)
    if node_dv:
        vmem.update(node_dv=node_dv)
    grow = dict(total=(acc and acc.total, near(4 * F + pad, F)))
    scratch = dict(eb=pltpu.VMEM((g, rows, F), f32), vb=pltpu.VMEM((g, W, F), f32))
    return call(body, "edge_weights", dict(here=here), active=active, vmem=vmem, free=dict(e=arrays(e), v=arrays(v)), grow=grow, scratch=scratch, after=after, micros=micros)


def gate(after, *xs, make=far, micros=0.01):
    return call(lambda k: None, "gate", grow={name: (x, make(*x.shape)) for name, x in zip("xyzuvw", xs)}, after=after, micros=micros)


class Total:
    def __init__(self, x, here, orders, cuts):
        count = lax.axis_size("node")
        self.here, self.orders = dict(here=here), orders
        self.swaps = [[(i, i ^ (1 << (y if i % 2 else x))) for i in range(count)] for x, y in zip(*orders)]
        self.x, self.cuts = x, cuts
        self.rows, self.F = x.shape
        self.sizes, rows = [], self.rows
        while len(self.sizes) < len(self.swaps) and rows % 16 == 0:
            rows //= 2
            self.sizes.append(rows)
        self.got, self.result, self.token, self.done = [], None, None, False
        self.steps = self.run()

    def flag(self, ref, step):
        x, y = (order[step] for order in self.orders)
        node = ref.here[1]
        return jnp.where(node % 2 == 1, node >> y, node >> x) & 1

    def partial(self, k):
        K, sizes = len(self.sizes), self.sizes
        size = sizes[min(k, K - 1)]

        def body(ref):
            def start(after):
                at = sum(self.flag(ref, m) * sizes[m] for m in range(after + 1, k)) if after + 1 < k else 0
                if k < K:
                    at = at + (1 - self.flag(ref, k)) * size
                return pl.multiple_of(at, 8)

            cs = [ref.load(x.at[pl.ds(start(j), size)], ref.buf.at[j]) for j, x in enumerate(ref.got)]
            total = ref.x[pl.ds(start(-1), size)]
            for j in range(k):
                cs[j].wait()
                total = total + ref.buf[j]
            ref.out[...] = total

        scratch = dict(buf=pltpu.VMEM((max(k, 1), size, self.F), f32))
        r = call(body, "partial_sum", self.here, vmem=dict(x=self.x), free=dict(got=self.got[:k]), outs=dict(out=near(size, self.F)), scratch=scratch, after=self.after, micros=50)
        self.token = (r.token,)
        return r.out

    def add(self, x, y):
        def body(k):
            k.load(k.y, k.buf).wait()
            k.out[...] = k.x[...] + k.buf[...]

        r = call(body, "add", vmem=dict(x=x), free=dict(y=y), outs=dict(out=near(*x.shape)), scratch=dict(buf=pltpu.VMEM(x.shape, f32)), after=self.after, micros=50)
        self.token = (r.token,)
        return r.out

    def join(self, own, got, step):
        R = own.shape[0]

        def body(k):
            bit = self.flag(k, step)
            mine, other = pl.multiple_of(bit * R, 8), pl.multiple_of((1 - bit) * R, 8)
            c = k.load(k.got, k.joined.at[pl.ds(other, R)])
            k.joined[pl.ds(mine, R)] = k.own[...]
            c.wait()

        def last_body(k):
            body(k)
            done = 0
            for ref, rows in zip(k.out, self.cuts):
                k.store(k.joined.at[pl.ds(done, rows)], ref)
                done += rows
            k.store.wait()

        joined = (2 * R, self.F)
        if step:
            outs, scratch = dict(joined=near(*joined)), {}
        else:
            outs, scratch = {f"out{i}": far(n, self.F) for i, n in enumerate(self.cuts)}, dict(joined=pltpu.VMEM(joined, f32))

        def run(k):
            if step:
                body(k)
            else:
                k.out = [getattr(k, key) for key in outs]
                last_body(k)

        r = call(run, "join", self.here, vmem=dict(own=own), free=dict(got=got), outs=outs, scratch=scratch, after=self.after, micros=50)
        self.token = (r.token,)
        return [getattr(r, key) for key in outs]

    def run(self):
        K = len(self.sizes)
        for k in range(K):
            send = self.partial(k)
            self.got.append(lax.ppermute(send, "node", self.swaps[k]))
            yield
        own = self.partial(K)
        for pairs in self.swaps[K:]:
            got = lax.ppermute(own, "node", pairs)
            yield
            own = self.add(own, got)
        for k in reversed(range(K)):
            got = lax.ppermute(own, "node", self.swaps[k])
            yield
            self.result = self.join(own, got, k)
            own = self.result[0]
        self.done = True

    def step(self, after):
        if self.done:
            return after
        self.after = after
        next(self.steps, None)
        return self.token


def on_device(in_nodes, in_edges, senders, receivers, edge_w1, edge_w2, edge_vec, node_w1, node_w2, node_vec, cot_nodes, cot_edges, lengths, step_mask):
    samples, nr, F = in_nodes.shape
    count = lax.axis_size("node")
    section, node = lax.axis_index("section"), lax.axis_index("node")
    evec, nvec = edge_vec[0], node_vec[0]
    here = jnp.concatenate([jnp.stack([section, node, count]).astype(jnp.int32), lengths, step_mask.reshape(-1)])
    live = step_mask.shape

    def partner(i, side):
        return i ^ 1 if side == 0 else (i - 1 + 2 * (i % 2)) % count

    def swap(x, side, planes):
        if planes is None:
            return lax.ppermute(x, "node", [(i, partner(i, side)) for i in range(count)])
        return lax.ppermute(x, ("section", "node"), [(s * count + i, s * count + partner(i, side)) for s in planes for i in range(count)])

    def beside(to_a, to_b, planes=None):
        return swap(to_a, 0, planes), swap(to_b, 1, planes)

    def across(x, source, side=None):
        if side is None:
            return lax.ppermute(x, "section", [(source, 1 - source)])
        return lax.ppermute(x, ("section", "node"), [(source * count + i, (1 - source) * count + partner(i, side)) for i in range(count)])

    p, q = [(sum(group_sizes[:i]), n) for i, n in enumerate(group_sizes)]
    both = p[1] + q[1]
    pad = 8 * count
    act_e = act_n = acc_n = acc_e = grad_e = grad_n = None
    after = ()

    def done(r):
        nonlocal after
        after = (r.token,)
        return r

    def stay(r, *names):
        r.kept = [getattr(r, name) for name in names]
        resident.extend(r.kept)
        return r

    def leave(*rs):
        for r in rs:
            resident[:] = [x for x in resident if all(x is not y for y in r.kept)]

    resident.clear()
    from_a, from_b = beside(in_nodes, in_nodes)
    hot, ew = prepare(edge_w1[0], edge_w2[0], (senders.reshape(1, -1), receivers.reshape(1, -1)), here, 3 * nr)

    def forward_0(c, relay):
        nonlocal act_e
        v = [(x, c[0]) for x in (from_a, in_nodes, from_b)]
        e = [(in_edges, c[0] + s) for s in range(0, c[1], chunk(c[1]))]
        f = done(edge_forward(c[1], 0, here, e, v, c[0], hot, ew, evec, (act_e, samples), (None, c[1], 0), relay, after, 0.01))
        act_e, f.v, f.e = f.act, v, e
        return stay(f, "out_a", "out_n", "out_r")

    def nodes_0(c, f, got):
        nonlocal act_n
        m = done(node_stage(c[1], True, False, 0, here, (in_nodes, c[0]), c[0], nw, nvec, [(got[0], 0), (f.own, 0), (got[1], 0)], act=(act_n, samples), after=after, micros=0.01))
        act_n = m.act
        return stay(m, "out_a", "out_n", "out_r", "out_g")

    def forward_1(c, e, nodes, box):
        nonlocal act_e
        v, e = [(x, 0) for x in nodes], [(x, s) for x in e for s in range(0, x.shape[0], chunk(c[1]))]
        f = done(edge_forward(c[1], 1, here, e, v, c[0], hot, ew, evec, (act_e, samples), box, (), after, 0.01))
        act_e, f.v, f.e = f.act, v, e
        return stay(f, "out_a", "out_n", "out_r")

    def middle_1(c, f, got, at, box):
        nonlocal act_n
        m = done(node_stage(c[1], True, True, 1, here, f.v[1], c[0], nw, nvec, [(got[0], at), (f.own, 0), (got[1], at)], act=(act_n, samples), weights=live, cot=cot_nodes, box=box, after=after, micros=0.01))
        act_n = m.act
        return stay(m, "ops", "dv", "own", "out_gv")

    def backward_1(c, f, m, got, at, box):
        b = done(edge_backward(c[1], 1, here, live, (cot_edges, c[0]), ((got[0], at), m.own, (got[1], at)), c[0], f, m.out_gv, hot, ew, evec, box, after, 0.01))
        leave(f)
        return stay(b, "ops", "sops", "dv", "own")

    def add_1(c, b, got, at):
        nonlocal grad_n
        r = done(add_parts(1, here, [(x, at) for x in got], [b.own], c[0], (grad_n, samples), True, after))
        grad_n = r.grad
        return across(r.out, 1)

    def out_1(c, b):
        nonlocal grad_e
        r = done(edge_out(c[1], 1, here, live, (cot_edges, c[0]), c[0], b.ops, ew, (grad_e, samples), True, after, 0.01))
        grad_e = r.grad
        return across(r.out_ge, 1)

    def middle_0(c, gv, stash):
        m = done(node_stage(c[1], False, True, 0, here, (in_nodes, c[0]), c[0], nw, nvec, [(gv, 0)], stash=stash, box=(None, c[1], 0), after=after, micros=50))
        m.got = beside(m.box_a, m.box_b, (0,))
        leave(stash)
        return stay(m, "ops", "dv", "own", "out_gv")

    def backward_0(c, ge, f, m, box):
        b = done(edge_backward(c[1], 0, here, None, (ge, 0), ((m.got[0], 0), m.own, (m.got[1], 0)), c[0], f, m.out_gv, hot, ew, evec, box, after, 50))
        leave(f)
        return stay(b, "ops", "sops", "dv", "own")

    def out_0(c, ge, b):
        nonlocal grad_e
        grad_e = done(edge_out(c[1], 0, here, None, (ge, 0), c[0], b.ops, ew, (grad_e, samples), False, after, 2)).grad

    def node_grads(on, m, first):
        nonlocal acc_n
        acc_n = done(node_weights(on, here, m, acc_n, first, after))
        leave(m)

    def edge_grads(on, c, b, f, first, node_dv=()):
        nonlocal acc_e
        acc_e = done(edge_weights(c[1], on, here, b, list(node_dv), f.e, f.v, pad, acc_e, first, after, 2))
        leave(b)

    f0p = forward_0(p, relay_sizes[0])
    got = beside(f0p.box_a, f0p.box_b)
    e0 = [across(f0p.relay[0], 0)]
    _, nw = prepare(node_w1[0], node_w2[0], after=after)
    n0p = nodes_0(p, f0p, got)
    v0, y = across(n0p.out_v, 0), across(n0p.out_v, 0, 1)
    held = done(gate(after, *f0p.relay[1:]))
    first = (v0, y) + tuple(e0)
    e0 += [across(getattr(held, key), 0) for key, _ in zip("xyz", f0p.relay[1:])]
    f0q = forward_0(q, relay_sizes[1])
    v0 = (swap(v0, 0, (1,)), v0, y)
    held = done(gate(after + first, f0q.box_a, f0q.box_b, *f0q.relay, micros=50))
    e1 = [across(getattr(held, key), 0) for key, _ in zip("zuvw", f0q.relay)]
    got_q = beside(held.x, held.y, (0,))
    f1p = forward_1(p, e0, v0, (None, p[1], 0))
    got = beside(f1p.box_a, f1p.box_b)
    n0q = nodes_0(q, f0q, got_q)
    v1, y = across(n0q.out_v, 0), across(n0q.out_v, 0, 1)
    n1p = middle_1(p, f1p, got, 0, (None, p[1], 0))
    got_p = beside(n1p.box_a, n1p.box_b)
    v1 = done(gate(after, v1, make=loose)).x
    f1q = forward_1(q, e1, (swap(v1, 0, None), v1, y), (None, q[1], 0))
    got_q = beside(f1q.box_a, f1q.box_b)
    b1p = backward_1(p, f1p, n1p, got_p, 0, (None, p[1], 0))
    got_p = beside(b1p.box_a, b1p.box_b)
    n1q = middle_1(q, f1q, got_q, 0, (None, q[1], 0))
    got_q = beside(n1q.box_a, n1q.box_b)
    gv0 = add_1(p, b1p, got_p, 0)
    ge0 = out_1(p, b1p)
    b1q = backward_1(q, f1q, n1q, got_q, 0, (None, q[1], 0))
    got_q = beside(b1q.box_a, b1q.box_b)
    m0p = middle_0(p, gv0, n0p)
    node_grads(1, n1p, True)
    gv1 = add_1(q, b1q, got_q, 0)
    ge1 = out_1(q, b1q)
    node_grads(1, n1q, False)
    edge_grads(1, p, b1p, f1p, True)
    edge_grads(1, q, b1q, f1q, False, (n1p.dv, n1q.dv))
    b0p = backward_0(p, ge0, f0p, m0p, (None, both, 0))
    m0q = middle_0(q, gv1, n0q)
    edge_grads(0, p, b0p, f0p, True)
    b0q = backward_0(q, ge1, f0q, m0q, ((b0p.box_a, b0p.box_b), both, p[1]))
    edge_grads(0, q, b0q, f0q, False, (m0p.dv, m0q.dv))
    bits = list(range(count.bit_length() - 1))
    yzz, zyz, yzz_turned = [[0] + [bits[i] for i in order] + bits[4:] for order in ((1, 2, 3), (2, 1, 3), (1, 3, 2))]
    total_e = Total(acc_e.total, here, (yzz_turned, zyz), (3 * F, F, pad))
    after = total_e.step(after)
    node_grads(0, m0p, True)
    node_grads(0, m0q, False)
    total_n = Total(acc_n.total, here, (yzz, zyz), (2 * F, F))
    totals = [total_e, total_n]
    after = total_n.step(after)
    for t in totals:
        after = t.step(after)
    out_0(p, ge0, b0p)
    out_0(q, ge1, b0q)
    for t in totals:
        after = t.step(after)
    held = done(gate(after, b0q.box_a, b0q.box_b))
    got = beside(held.x, held.y, (0,))
    for t in totals:
        after = t.step(after)
    grad_n = done(add_parts(0, here, [(x, 0) for x in got], [b0p.own, b0q.own], 0, (grad_n, samples), False, after)).grad
    while not all(t.done for t in totals):
        for t in totals:
            after = t.step(after)
    edge_1, edge_2, vecs = total_e.result
    node_1, node_2 = total_n.result
    return (
        act_n[None], act_e[None], grad_n[None], grad_e[None],
        edge_1[None], edge_2[None], vecs[None, 0:4], node_1[None], node_2[None], vecs[None, 8:12],
    )


def solution(mesh):
    nodes, rows, weights = P(None, "node", None), P("node"), P("section", None, None)
    stacked = P("section", None, "node", None)
    in_specs = (nodes, nodes, rows, rows) + (weights,) * 6 + (nodes, nodes, P(), P())
    out_specs = (stacked,) * 4 + (weights,) * 6
    return jax.shard_map(on_device, mesh=mesh, in_specs=in_specs, out_specs=out_specs, check_vma=False)
```

```python
from types import SimpleNamespace

import jax
import jax.numpy as jnp
from jax import lax
from jax.experimental import pallas as pl
from jax.experimental.pallas import tpu as pltpu
from jax.sharding import PartitionSpec as P

f32, bf16 = jnp.float32, jnp.bfloat16
norm_eps = 1e-05
NN = ((1,), (0,))
NT = ((1,), (1,))
TN = ((0,), (0,))
group_sizes = (4, 4)
relay_sizes = ((2, 2), (2, 2))
MIB = 1024 * 1024


def split(x):
    hi = x.astype(bf16)
    return hi, (x - hi.astype(f32)).astype(bf16)


def dot1(a, b, dims):
    return lax.dot_general(a, b, (dims, ((), ())), preferred_element_type=f32)


def dot3(a, b, dims):
    return dot1(a[0], b[0], dims) + (dot1(a[0], b[1], dims) + dot1(a[1], b[0], dims))


def dot3_few(a, b, dims):
    rows = a[0].shape[0]
    both = dot1(jnp.concatenate(a, axis=0), b[0], dims)
    return both[:rows] + (both[rows:] + dot1(a[0], b[1], dims))


def normalized(u):
    c = u - jnp.mean(u, axis=-1, keepdims=True)
    r = lax.rsqrt(jnp.mean(c * c, axis=-1, keepdims=True) + norm_eps)
    return c * r, r


def norm_back(gu, n, r, gain):
    t = gu * gain
    return r * (t - jnp.mean(t, axis=-1, keepdims=True) - n * jnp.mean(t * n, axis=-1, keepdims=True))


def column_sums(*xs):
    F = xs[0].shape[-1]
    return jnp.concatenate([jnp.sum(x, axis=0, keepdims=True) for x in xs] + [jnp.zeros((8 - len(xs), F), f32)], axis=0)


class Copies:
    def __init__(self, sems):
        self.sems, self.all = sems, []

    def __call__(self, src, dst):
        c = pltpu.make_async_copy(src, dst, self.sems.at[len(self.all)])
        self.all.append(c)
        c.start()
        return c

    def wait(self):
        wait(*self.all)


def wait(*copies):
    for c in copies:
        c.wait()


def far(*shape, dtype=f32):
    return pltpu.HBM(shape, dtype)


def near(*shape, dtype=f32):
    return pltpu.VMEM(shape, dtype)


resident = []


def loose(*shape):
    return jax.ShapeDtypeStruct(shape, f32)


def call(body, name, scalars={}, hbm={}, vmem={}, free={}, outs={}, grow={}, scratch={}, after=(), micros=2, copies=24, active=None):
    args, specs, where = [], [], {}

    def add(values, space, pinned):
        for key, value in values.items():
            at = []
            for x in value if isinstance(value, (list, tuple)) else [value]:
                at.append(len(args))
                args.append(pltpu.with_memory_space_constraint(x, space) if pinned else x)
                specs.append(pl.BlockSpec(memory_space=space))
            where[key] = at if isinstance(value, (list, tuple)) else at[0]

    add(scalars, pltpu.SMEM, False)
    add(hbm, pltpu.HBM, True)
    add(vmem, pltpu.VMEM, True)
    add(free, pl.ANY, False)
    add(dict(after=[x for x in after if x.shape == (8, 128)]), pltpu.HBM, True)
    add(dict(arrived=[x for x in after if x.shape != (8, 128)]), pl.ANY, False)
    used = {id(x) for value in vmem.values() for x in (value if isinstance(value, (list, tuple)) else [value])}
    add(dict(kept=[x for x in resident if id(x) not in used]), pltpu.VMEM, True)
    shapes, out_specs, aliases = [], [], {}
    for key, value in list(outs.items()) + list(grow.items()) + [("token", far(8, 128))]:
        old, shape = value if key in grow else (None, value)
        space = pl.ANY if isinstance(shape, jax.ShapeDtypeStruct) else shape.memory_space
        where[key] = -1 - len(shapes)
        if old is not None:
            aliases[len(args)] = len(shapes)
            args.append(old if space is pl.ANY else pltpu.with_memory_space_constraint(old, space))
            specs.append(pl.BlockSpec(memory_space=space))
        shapes.append(shape)
        out_specs.append(pl.BlockSpec(memory_space=space))
    first_out, first_scratch = len(args), len(args) + len(shapes)
    kept = dict(scratch)

    def kernel(*refs):
        k = SimpleNamespace()
        pick = lambda i: refs[i] if i >= 0 else refs[first_out - 1 - i]
        for key, at in where.items():
            setattr(k, key, [pick(i) for i in at] if isinstance(at, list) else pick(at))
        for i, key in enumerate(kept):
            setattr(k, key, refs[first_scratch + i])
        k.load, k.store = Copies(refs[-2]), Copies(refs[-1])
        if active is None:
            body(k)
        else:
            pl.when(k.here[0] == active)(lambda: body(k))

    res = pl.pallas_call(
        kernel,
        out_shape=shapes,
        in_specs=specs,
        out_specs=out_specs,
        scratch_shapes=list(kept.values()) + [pltpu.SemaphoreType.DMA((copies,))] * 2,
        input_output_aliases=aliases,
        compiler_params=pltpu.CompilerParams(vmem_limit_bytes=12 * MIB),
        cost_estimate=pl.CostEstimate(flops=int(micros * 1.15e9), bytes_accessed=0, transcendentals=0),
        name=name,
    )(*args)
    return SimpleNamespace(**{key: res[-1 - at] for key, at in where.items() if not isinstance(at, list) and at < 0})


def prepare(w1, w2, ends=None, here=None, W=0, after=()):
    F = w1.shape[1]

    def body(k):
        c1, c2 = k.load(k.w1, k.b1), k.load(k.w2, k.b2)
        if ends is not None:
            hots = []
            for src, ref in zip(k.ends, (k.e0, k.e1)):
                k.load(src, ref).wait()
                total = k.here[2] * (W // 3)
                at = ref[...] - (k.here[1] - 1) * (W // 3)
                at = jnp.where(at < 0, at + total, at)
                at = jnp.where(at >= total, at - total, at)
                hots.append((lax.broadcasted_iota(jnp.int32, (W, at.shape[1]), 0) == at).astype(f32).astype(bf16))
            both = jnp.concatenate(hots, axis=0)
            k.gather[...] = jnp.concatenate([both, both], axis=0)
            k.scatter[...] = jnp.concatenate([both, both], axis=1)
        c2.wait()
        k.h2[...], k.l2[...] = split(k.b2[...])
        c1.wait()
        k.h1[...], k.l1[...] = split(k.b1[...])

    half = lambda *s: near(*s, dtype=bf16)
    outs = dict(h1=half(*w1.shape), l1=half(*w1.shape), h2=half(*w2.shape), l2=half(*w2.shape))
    scalars, hbm = {}, dict(w1=w1, w2=w2)
    scratch = dict(b1=pltpu.VMEM(w1.shape, f32), b2=pltpu.VMEM(w2.shape, f32))
    if ends is not None:
        rows = ends[0].shape[1]
        outs.update(gather=half(4 * W, rows), scatter=half(2 * W, 2 * rows))
        scalars = dict(here=here)
        hbm.update(ends=list(ends))
        scratch.update(e0=pltpu.VMEM((1, rows), jnp.int32), e1=pltpu.VMEM((1, rows), jnp.int32))
    r = call(body, "prepare", scalars, hbm, outs=outs, scratch=scratch, after=after)
    resident.extend([r.h1, r.l1, r.h2, r.l2])
    if ends is not None:
        resident.extend([r.gather, r.scatter])
    return r, dict(w1=[r.h1, r.l1], w2=[r.h2, r.l2])


def side_rows(par, nr):
    return pl.multiple_of((1 - par) * 2 * nr, 16), pl.multiple_of(par * 2 * nr, 16)


def window_parts(k, ref, nr):
    a_at, b_at = side_rows(k.here[1] % 2, nr)
    return [ref.at[:, pl.ds(a_at, nr), :], ref.at[:, nr:2 * nr, :], ref.at[:, pl.ds(b_at, nr), :]]


def sample_weight(k, sample, micro, steps):
    m, t = divmod(sample, steps)
    return jnp.where(t < k.here[3 + m], k.here[3 + micro + sample], 0).astype(f32)


def load_views(k, views, refs, targets, g):
    return [k.load(ref.at[pl.ds(view[1], g)], target) for view, ref, target in zip(views, refs, targets)]


def arrays(views):
    return [v[0] for v in views]


def chunk(g):
    return 2 if g % 2 == 0 else 1


def edge_forward(g, active, here, e, v, n, hot, w, vec, act, box, relay, after, micros):
    rows, F = e[0][0].shape[1:]
    nr = v[0][0].shape[1]
    W = 3 * nr
    cs = chunk(g)

    def body(k):
        load, store = k.load, k.store
        cv = load_views(k, v, k.v, window_parts(k, k.vb, nr), g)
        ce = load_views(k, e, k.e, [k.eb.at[pl.ds(s, cs)] for s in range(0, g, cs)], cs)
        (w1h, w1l), (w2h, w2l), vec = k.w1, k.w2, k.vec
        wait(*cv)
        vw = split(k.vb[...].reshape(g * W, F))
        for i in (0, 1):
            part = pl.ds((i + 1) * F, F)
            h, l = split(dot3(vw, (w1h[part], w1l[part]), NN).reshape(g, W, F))
            k.pp[:, i * W:(i + 1) * W] = h
            k.pp[:, (i + 2) * W:(i + 3) * W] = l
        for s in range(0, g, cs):
            ce[s // cs].wait()
            to = pl.ds(s, cs)
            x = k.eb[to].reshape(cs * rows, F)
            a = dot3(split(x), (w1h[0:F], w1l[0:F]), NN) + vec[0:1]
            a = a + jnp.concatenate([dot1(k.gather[...], k.pp[s + t], TN) for t in range(cs)], axis=0)
            k.out_a[to] = a.reshape(cs, rows, F)
            h = a / (1 + jnp.exp(-a))
            n_, r = normalized(dot3(split(h), (w2h[...], w2l[...]), NN) + vec[1:2])
            k.out_n[to] = n_.reshape(cs, rows, F)
            k.out_r[to] = jnp.broadcast_to(r, (cs * rows, 128)).reshape(cs, rows, 128)
            m = n_ * vec[2:3] + vec[3:4]
            k.ob[to] = (x + m).reshape(cs, rows, F)
            if relay:
                store(k.ob.at[to], getattr(k, relays[s][0]).at[pl.ds(relays[s][1], cs)])
            store(k.ob.at[to], k.act.at[pl.ds(n + s, cs)])
            mh, ml = split(m.reshape(cs, rows, F))
            for t in range(cs):
                k.sb[s + t] = dot1(k.scatter[W:], jnp.concatenate([mh[t], ml[t]], axis=0), NN)
        sides = window_parts(k, k.sb, nr)
        store(sides[0], k.box_a.at[pl.ds(box[2], g)])
        store(sides[1], k.own)
        store(sides[2], k.box_b.at[pl.ds(box[2], g)])
        store.wait()

    outs = dict(out_a=near(g, rows, F), out_n=near(g, rows, F), out_r=near(g, rows, 128), own=far(g, nr, F))
    names = "abcd"[:len(relay)]
    outs.update({key: far(size, rows, F) for key, size in zip(names, relay)})
    relays = [(key, at) for key, size in zip(names, relay) for at in range(size)]
    old = box[0] or (None, None)
    grow = dict(act=(act[0], far(act[1], rows, F)), box_a=(old[0], far(box[1], nr, F)), box_b=(old[1], far(box[1], nr, F)))
    full = pltpu.VMEM((g, rows, F), f32)
    scratch = dict(eb=full, ob=full, vb=pltpu.VMEM((g, W, F), f32), sb=pltpu.VMEM((g, W, F), f32), pp=pltpu.VMEM((g, 4 * W, F), bf16))
    r = call(body, "edge_forward", dict(here=here), active=active, vmem=dict(**w, gather=hot.gather, scatter=hot.scatter, vec=vec), free=dict(e=arrays(e), v=arrays(v)), outs=outs, grow=grow, scratch=scratch, after=after, micros=micros)
    r.relay = [getattr(r, key) for key in names]
    return r


def node_stage(g, forward, backward, active, here, v, n, w, vec, parts, act=None, stash=None, weights=None, cot=None, box=None, after=(), micros=2):
    nr, F = v[0].shape[1:]
    R = g * nr

    def body(k):
        load, store = k.load, k.store
        cx = [load(k.v.at[pl.ds(v[1], g)], k.zb.at[:, :, 0:F])] + load_views(k, parts, k.parts, [k.pb.at[i] for i in range(len(parts))], g)
        if forward and backward:
            cx.append(load(k.cot.at[pl.ds(n, g)], k.gb))
        w1, w2, vec = (k.w1[0][...], k.w1[1][...]), (k.w2[0][...], k.w2[1][...]), k.vec
        wait(*cx)
        given = sum([k.pb[i] for i in range(1, len(parts))], k.pb[0])
        k.zb[:, :, F:] = given if forward else k.gathered[...]
        z = k.zb[...].reshape(R, 2 * F)
        zs = split(z)
        if forward:
            a = dot3_few(zs, w1, NN) + vec[0:1]
            h = a / (1 + jnp.exp(-a))
            n_, r = normalized(dot3_few(split(h), w2, NN) + vec[1:2])
            k.ob[...] = (z[:, :F] + n_ * vec[2:3] + vec[3:4]).reshape(g, nr, F)
            if not backward:
                store(k.ob, k.out_v)
                k.out_a[...] = a.reshape(g, nr, F)
                k.out_n[...] = n_.reshape(g, nr, F)
                k.out_r[...] = jnp.broadcast_to(r, (R, 128)).reshape(g, nr, 128)
                k.out_g[...] = given
            store(k.ob, k.act.at[pl.ds(n, g)])
        else:
            a, n_, r = k.a[...].reshape(R, F), k.n[...].reshape(R, F), k.r[...].reshape(R, 128)[:, 0:1]
        if backward:
            if forward:
                for s in range(g):
                    k.gb[s] = k.gb[s] * sample_weight(k, n + s, *weights)
                gu = k.gb[...].reshape(R, F)
            else:
                gu = given.reshape(R, F)
            gp = norm_back(gu, n_, r, vec[2:3])
            q = 1 / (1 + jnp.exp(-a))
            hs, gps = split(a * q), split(gp)
            ga = dot3_few(gps, w2, NT) * (q * (1 + a * (1 - q)))
            gas = split(ga)
            gz = dot3_few(gas, w1, NT)
            k.ggb[...] = gz[:, F:].reshape(g, nr, F)
            for ref in (k.box_a, k.box_b):
                store(k.ggb, ref.at[pl.ds(box[2], g)])
            k.own[...] = k.ggb[...]
            k.out_gv[...] = (gu + gz[:, :F]).reshape(g, nr, F)
            for i, x in enumerate((zs[0][:, :F], zs[1][:, :F], zs[0][:, F:], zs[1][:, F:], hs[0], hs[1], gas[0], gas[1], gps[0], gps[1])):
                k.ops[i] = x
            k.dv[...] = column_sums(ga, gp, gu * n_, gu)
        store.wait()

    hbm, vmem, free = {}, dict(**w, vec=vec), dict(v=v[0], parts=arrays(parts))
    shape = near(g, nr, F)
    outs, grow = {}, {}
    if not forward:
        vmem.update(a=stash.out_a, n=stash.out_n, r=stash.out_r, gathered=stash.out_g)
    elif backward:
        hbm.update(cot=cot)
    if forward:
        grow.update(act=(act[0], far(act[1], nr, F)))
        if not backward:
            outs.update(out_v=far(g, nr, F), out_a=shape, out_n=shape, out_r=near(g, nr, 128), out_g=shape)
    if backward:
        old = box[0] or (None, None)
        outs.update(own=shape, out_gv=shape, ops=near(10, R, F, dtype=bf16), dv=near(8, F))
        grow.update(box_a=(old[0], far(box[1], nr, F)), box_b=(old[1], far(box[1], nr, F)))
    small = pltpu.VMEM((g, nr, F), f32)
    scratch = dict(zb=pltpu.VMEM((g, nr, 2 * F), f32), pb=pltpu.VMEM((len(parts), g, nr, F), f32), gb=small, ob=small, ggb=small)
    return call(body, "node_stage", dict(here=here), hbm, vmem, free, active=active, outs=outs, grow=grow, scratch=scratch, after=after, micros=micros)


def node_weights(active, here, m, acc, first, after):
    _, R, F = m.ops.shape

    def body(k):
        o = k.ops
        for i, (x, y) in enumerate(((0, 6), (2, 6), (4, 8))):
            part = pl.ds(i * F, F)
            d = dot3((o[x], o[x + 1]), (o[y], o[y + 1]), TN)
            k.total[part] = d if first else k.total[part] + d

    grow = dict(total=(acc and acc.total, near(3 * F, F)))
    return call(body, "node_weights", dict(here=here), active=active, vmem=dict(ops=m.ops), grow=grow, after=after, micros=0.01)


def edge_backward(g, active, here, weights, ge, gg, n, stash, gv, hot, w, vec, box, after, micros):
    rows, F = ge[0].shape[1:]
    nr = gv.shape[1]
    W = 3 * nr
    cs = 2 if g % 2 == 0 else 1

    def body(k):
        load, store = k.load, k.store
        gg_at = window_parts(k, k.ggb, nr)
        cg = load_views(k, (gg[0], gg[2]), k.gg, (gg_at[0], gg_at[2]), g)
        cx = [load(k.ge.at[pl.ds(ge[1] + s, cs)], k.gb.at[pl.ds(s, cs)]) for s in range(0, g, cs)]
        k.ggb[:, nr:2 * nr] = k.gg_own[...]
        (w1h, w1l), (w2h, w2l), vec = k.w1, k.w2, k.vec
        wait(*cg)
        h, l = split(k.ggb[...])
        k.gg2[:, 0:W] = h
        k.gg2[:, W:] = l
        flat = lambda x: x.reshape(cs * rows, x.shape[-1])
        sums = []
        for s in range(0, g, cs):
            to = pl.ds(s, cs)
            cx[s // cs].wait()
            if weights:
                for t in range(s, s + cs):
                    k.gb[t] = k.gb[t] * sample_weight(k, n + t, *weights)
            hot_r = k.gather[pl.ds(W, W)]
            gu = flat(k.gb[to]) + jnp.concatenate([dot1(hot_r, k.gg2[s + t, 0:W], TN) + dot1(hot_r, k.gg2[s + t, W:], TN) for t in range(cs)], axis=0)
            n_, a = flat(k.n[to]), flat(k.a[to])
            gp = norm_back(gu, n_, flat(k.r[to])[:, 0:1], vec[2:3])
            gps = split(gp)
            q = 1 / (1 + jnp.exp(-a))
            ga = dot3(gps, (w2h[...], w2l[...]), NT) * (q * (1 + a * (1 - q)))
            gas = split(ga)
            for i, x in enumerate((*split(a * q), *gps, *gas)):
                k.ops[i, pl.ds(s * rows, cs * rows)] = x
            for t in range(cs):
                both = jnp.concatenate([x[t * rows:(t + 1) * rows] for x in gas], axis=0)
                k.ssb[s + t] = dot1(k.scatter[...], both, NN)
            sums.append(column_sums(ga, gp, gu * n_, gu))
        ss = split(k.ssb[:, 0:W].reshape(g * W, F))
        sr = split(k.ssb[:, W:].reshape(g * W, F))
        for i, x in enumerate((*ss, *sr)):
            k.sops[i] = x
        wg = dot3(ss, (w1h[F:2 * F], w1l[F:2 * F]), NT) + dot3(sr, (w1h[2 * F:], w1l[2 * F:]), NT)
        k.wgb[...] = wg.reshape(g, W, F)
        k.wgb[:, nr:2 * nr] += k.gv[...]
        sides = window_parts(k, k.wgb, nr)
        store(sides[0], k.box_a.at[pl.ds(box[2], g)])
        store(sides[2], k.box_b.at[pl.ds(box[2], g)])
        k.own[...] = k.wgb[:, nr:2 * nr]
        k.dv[...] = sum(sums[1:], sums[0])
        store.wait()

    free = dict(ge=ge[0], gg=[gg[0][0], gg[2][0]])
    vmem = dict(**w, vec=vec, a=stash.out_a, n=stash.out_n, r=stash.out_r, gv=gv, gg_own=gg[1], gather=hot.gather, scatter=hot.scatter)
    old = box[0] or (None, None)
    outs = dict(own=near(g, nr, F), ops=near(6, g * rows, F, dtype=bf16), sops=near(4, g * W, F, dtype=bf16), dv=near(8, F))
    grow = dict(box_a=(old[0], far(box[1], nr, F)), box_b=(old[1], far(box[1], nr, F)))
    scratch = dict(gb=pltpu.VMEM((g, rows, F), f32), ggb=pltpu.VMEM((g, W, F), f32), gg2=pltpu.VMEM((g, 2 * W, F), bf16), ssb=pltpu.VMEM((g, 2 * W, F), f32), wgb=pltpu.VMEM((g, W, F), f32))
    return call(body, "edge_backward", dict(here=here), active=active, vmem=vmem, free=free, outs=outs, grow=grow, scratch=scratch, after=after, micros=micros)


def add_parts(active, here, views, own, n, grad, relay, after):
    g, (nr, F) = sum(x.shape[0] for x in own), own[0].shape[1:]

    def body(k):
        wait(*load_views(k, views, k.views, [k.pb.at[i] for i in (0, 1)], g))
        done = 0
        for x in k.own:
            to = pl.ds(done, x.shape[0])
            k.pb[0, to] = k.pb[0, to] + k.pb[1, to] + x[...]
            done += x.shape[0]
        if relay:
            k.store(k.pb.at[0], k.out)
        k.store(k.pb.at[0], k.grad.at[pl.ds(n, g)])
        k.store.wait()

    outs = dict(out=far(g, nr, F)) if relay else {}
    grow = dict(grad=(grad[0], far(grad[1], nr, F)))
    return call(body, "add_parts", dict(here=here), active=active, vmem=dict(own=own), free=dict(views=arrays(views)), outs=outs, grow=grow, scratch=dict(pb=pltpu.VMEM((2, g, nr, F), f32)), after=after, micros=0.01)


def edge_out(g, active, here, weights, ge, n, ops, w, grad, relay, after, micros):
    rows, F = ge[0].shape[1:]
    halves = (0, 1) if g % 2 == 0 else (0,)
    m = g // len(halves)

    def body(k):
        cs = [k.load(k.ge.at[pl.ds(ge[1] + i * m, m)], k.gb.at[pl.ds(i * m, m)]) for i in halves]
        w1h, w1l = k.w1
        for i in halves:
            own = dot3([k.ops[x, pl.ds(i * m * rows, m * rows)] for x in (4, 5)], (w1h[0:F], w1l[0:F]), NT)
            cs[i].wait()
            if weights:
                for t in range(i * m, (i + 1) * m):
                    k.gb[t] = k.gb[t] * sample_weight(k, n + t, *weights)
            to = pl.ds(i * m, m)
            k.gb[to] = k.gb[to] + own.reshape(m, rows, F)
            if relay:
                k.store(k.gb.at[to], k.out_ge.at[to])
            k.store(k.gb.at[to], k.grad.at[pl.ds(n + i * m, m)])
        k.store.wait()

    outs = dict(out_ge=far(g, rows, F)) if relay else {}
    grow = dict(grad=(grad[0], far(grad[1], rows, F)))
    return call(body, "edge_out", dict(here=here), active=active, vmem=dict(ops=ops, w1=w["w1"]), free=dict(ge=ge[0]), outs=outs, grow=grow, scratch=dict(gb=pltpu.VMEM((g, rows, F), f32)), after=after, micros=micros)


def edge_weights(g, active, here, b, node_dv, e, v, pad, acc, first, after, micros):
    rows, F = e[0][0].shape[1:]
    nr = v[0][0].shape[1]
    W = 3 * nr

    def body(k):
        cs = chunk(g)
        ce = load_views(k, e, k.e, [k.eb.at[pl.ds(s, cs)] for s in range(0, g, cs)], cs)
        cv = load_views(k, v, k.v, window_parts(k, k.vb, nr), g)
        o = k.ops

        def put(total, i, x, y):
            part = pl.ds(i * F, F)
            d = dot3(x, y, TN)
            total[part] = d if first else total[part] + d

        put(k.total, 3, (o[0], o[1]), (o[2], o[3]))
        if first:
            k.total[4 * F:] = jnp.zeros((pad, F), f32)
        k.total[4 * F:4 * F + 8] += k.dv[...]
        if node_dv:
            k.total[4 * F + 8:4 * F + 16] = sum([x[...] for x in k.node_dv[1:]], k.node_dv[0][...])
        wait(*cv)
        vs = split(k.vb[...].reshape(g * W, F))
        for i in (0, 1):
            put(k.total, i + 1, vs, (k.sops[2 * i], k.sops[2 * i + 1]))
        wait(*ce)
        put(k.total, 0, split(k.eb[...].reshape(g * rows, F)), (o[4], o[5]))

    vmem = dict(ops=b.ops, sops=b.sops, dv=b.dv)
    if node_dv:
        vmem.update(node_dv=node_dv)
    grow = dict(total=(acc and acc.total, near(4 * F + pad, F)))
    scratch = dict(eb=pltpu.VMEM((g, rows, F), f32), vb=pltpu.VMEM((g, W, F), f32))
    return call(body, "edge_weights", dict(here=here), active=active, vmem=vmem, free=dict(e=arrays(e), v=arrays(v)), grow=grow, scratch=scratch, after=after, micros=micros)


def gate(after, *xs, make=far, micros=0.01):
    return call(lambda k: None, "gate", grow={name: (x, make(*x.shape)) for name, x in zip("xyzuvw", xs)}, after=after, micros=micros)


class Total:
    def __init__(self, x, here, orders, cuts, vecs=False):
        self.vecs = vecs
        count = lax.axis_size("node")
        self.here, self.orders = dict(here=here), orders
        self.swaps = [[(i, i ^ (1 << (y if i % 2 else x))) for i in range(count)] for x, y in zip(*orders)]
        self.x, self.cuts = x, cuts
        self.rows, self.F = x.shape
        self.sizes, rows = [], self.rows
        while len(self.sizes) < len(self.swaps) and rows % 16 == 0:
            rows //= 2
            self.sizes.append(rows)
        self.got, self.result, self.token, self.done = [], None, None, False
        self.steps = self.run()

    def flag(self, ref, step):
        x, y = (order[step] for order in self.orders)
        node = ref.here[1]
        return jnp.where(node % 2 == 1, node >> y, node >> x) & 1

    def partial(self, k):
        K, sizes = len(self.sizes), self.sizes
        size = sizes[min(k, K - 1)]

        def body(ref):
            def start(after):
                at = sum(self.flag(ref, m) * sizes[m] for m in range(after + 1, k)) if after + 1 < k else 0
                if k < K:
                    at = at + (1 - self.flag(ref, k)) * size
                return pl.multiple_of(at, 8)

            total = ref.x[pl.ds(start(-1), size)]
            for j, x in enumerate(ref.got):
                total = total + x[pl.ds(start(j), size)]
            ref.out[...] = total

        r = call(body, "partial_sum", self.here, vmem=dict(x=self.x, got=self.got[:k]), outs=dict(out=near(size, self.F)), after=self.after, micros=50)
        self.token = (r.token,)
        return r.out

    def add(self, x, y):
        def body(k):
            k.out[...] = k.x[...] + k.y[...]

        r = call(body, "add", self.here, vmem=dict(x=x, y=y), outs=dict(out=near(*x.shape)), after=self.after, micros=50)
        self.token = (r.token,)
        return r.out

    def join(self, own, got, step):
        R = own.shape[0]

        def body(k):
            bit = self.flag(k, step)
            k.joined[pl.ds(pl.multiple_of(bit * R, 8), R)] = k.own[...]
            k.joined[pl.ds(pl.multiple_of((1 - bit) * R, 8), R)] = k.got[...]

        r = call(body, "join", self.here, vmem=dict(own=own, got=got), outs=dict(joined=near(2 * R, self.F)), after=self.after, micros=50)
        self.token = (r.token,)
        return r.joined

    def finish(self, own, got):
        R = own.shape[0]
        names = "abcdef"[:len(self.cuts)]

        def put(k, low, high):
            done = 0
            for key, rows in zip(names, self.cuts):
                for src, at in ((low, 0), (high, R)):
                    a, b = max(at, done), min(at + R, done + rows)
                    if a < b:
                        k.store(src.at[pl.ds(a - at, b - a)], getattr(k, key).at[pl.ds(a - done, b - a)])
                done += rows
            if self.vecs:
                assert done >= R
                k.va[...] = high[done - R:done - R + 4]
                k.vb[...] = high[done - R + 8:done - R + 12]
                k.store(k.va, k.first)
                k.store(k.vb, k.second)
            k.store.wait()

        def body(k):
            bit = self.flag(k, 0)
            pl.when(bit == 0)(lambda: put(k, k.own, k.got))
            k.store.all = []
            pl.when(bit == 1)(lambda: put(k, k.got, k.own))

        outs = {key: far(rows, self.F) for key, rows in zip(names, self.cuts)}
        scratch = {}
        if self.vecs:
            outs.update(first=far(4, self.F), second=far(4, self.F))
            scratch.update(va=pltpu.VMEM((4, self.F), f32), vb=pltpu.VMEM((4, self.F), f32))
        r = call(body, "finish", self.here, vmem=dict(own=own, got=got), outs=outs, scratch=scratch, after=self.after, micros=50)
        self.token = (r.token,)
        return [getattr(r, key) for key in outs]

    def run(self):
        K = len(self.sizes)
        for k in range(K):
            send = self.partial(k)
            self.got.append(lax.ppermute(send, "node", self.swaps[k]))
            yield
        own = self.partial(K)
        for pairs in self.swaps[K:]:
            got = lax.ppermute(own, "node", pairs)
            yield
            own = self.add(own, got)
        for k in reversed(range(K)):
            got = lax.ppermute(own, "node", self.swaps[k])
            yield
            if k:
                own = self.join(own, got, k)
            else:
                self.result = self.finish(own, got)
        self.done = True

    def step(self, after):
        if self.done:
            return after
        self.after = after
        next(self.steps, None)
        return self.token


def on_device(in_nodes, in_edges, senders, receivers, edge_w1, edge_w2, edge_vec, node_w1, node_w2, node_vec, cot_nodes, cot_edges, lengths, step_mask):
    samples, nr, F = in_nodes.shape
    count = lax.axis_size("node")
    section, node = lax.axis_index("section"), lax.axis_index("node")
    evec, nvec = edge_vec[0], node_vec[0]
    here = jnp.concatenate([jnp.stack([section, node, count]).astype(jnp.int32), lengths, step_mask.reshape(-1)])
    live = step_mask.shape

    def partner(i, side):
        return i ^ 1 if side == 0 else (i - 1 + 2 * (i % 2)) % count

    def swap(x, side, planes):
        if planes is None:
            return lax.ppermute(x, "node", [(i, partner(i, side)) for i in range(count)])
        return lax.ppermute(x, ("section", "node"), [(s * count + i, s * count + partner(i, side)) for s in planes for i in range(count)])

    def beside(to_a, to_b, planes=None):
        return swap(to_a, 0, planes), swap(to_b, 1, planes)

    def aside(x, source):
        return lax.ppermute(x, ("section", "node"), [(source * count + i, (1 - source) * count + (i ^ 4)) for i in range(count)])

    def back(x, plane):
        return lax.ppermute(x, ("section", "node"), [(plane * count + i, plane * count + (i ^ 4)) for i in range(count)])

    def across(x, source, side=None):
        if side is None:
            return lax.ppermute(x, "section", [(source, 1 - source)])
        return lax.ppermute(x, ("section", "node"), [(source * count + i, (1 - source) * count + partner(i, side)) for i in range(count)])

    p, q = [(sum(group_sizes[:i]), n) for i, n in enumerate(group_sizes)]
    both = p[1] + q[1]
    pad = 8 * count
    act_e = act_n = acc_n = acc_e = grad_e = grad_n = None
    after = ()

    def done(r):
        nonlocal after
        after = (r.token,)
        return r

    def stay(r, *names):
        r.kept = [getattr(r, name) for name in names]
        resident.extend(r.kept)
        return r

    def leave(*rs):
        for r in rs:
            resident[:] = [x for x in resident if all(x is not y for y in r.kept)]

    resident.clear()
    from_a, from_b = beside(in_nodes, in_nodes)
    hot, ew = prepare(edge_w1[0], edge_w2[0], (senders.reshape(1, -1), receivers.reshape(1, -1)), here, 3 * nr)

    def forward_0(c, relay):
        nonlocal act_e
        v = [(x, c[0]) for x in (from_a, in_nodes, from_b)]
        e = [(in_edges, c[0] + s) for s in range(0, c[1], chunk(c[1]))]
        f = done(edge_forward(c[1], 0, here, e, v, c[0], hot, ew, evec, (act_e, samples), (None, c[1], 0), relay, after, 0.01))
        act_e, f.v, f.e = f.act, v, e
        return stay(f, "out_a", "out_n", "out_r")

    def nodes_0(c, f, got):
        nonlocal act_n
        m = done(node_stage(c[1], True, False, 0, here, (in_nodes, c[0]), c[0], nw, nvec, [(got[0], 0), (f.own, 0), (got[1], 0)], act=(act_n, samples), after=after, micros=0.01))
        act_n = m.act
        return stay(m, "out_a", "out_n", "out_r", "out_g")

    def forward_1(c, e, nodes, box):
        nonlocal act_e
        v, e = [(x, 0) for x in nodes], [(x, s) for x in e for s in range(0, x.shape[0], chunk(c[1]))]
        f = done(edge_forward(c[1], 1, here, e, v, c[0], hot, ew, evec, (act_e, samples), box, (), after, 0.01))
        act_e, f.v, f.e = f.act, v, e
        return stay(f, "out_a", "out_n", "out_r")

    def middle_1(c, f, got, at, box):
        nonlocal act_n
        m = done(node_stage(c[1], True, True, 1, here, f.v[1], c[0], nw, nvec, [(got[0], at), (f.own, 0), (got[1], at)], act=(act_n, samples), weights=live, cot=cot_nodes, box=box, after=after, micros=0.01))
        act_n = m.act
        return stay(m, "ops", "dv", "own", "out_gv")

    def backward_1(c, f, m, got, at, box):
        b = done(edge_backward(c[1], 1, here, live, (cot_edges, c[0]), ((got[0], at), m.own, (got[1], at)), c[0], f, m.out_gv, hot, ew, evec, box, after, 0.01))
        leave(f)
        return stay(b, "ops", "sops", "dv", "own")

    def add_1(c, b, got, at):
        nonlocal grad_n
        r = done(add_parts(1, here, [(x, at) for x in got], [b.own], c[0], (grad_n, samples), True, after))
        grad_n = r.grad
        return r.out

    def out_1(c, b):
        nonlocal grad_e
        r = done(edge_out(c[1], 1, here, live, (cot_edges, c[0]), c[0], b.ops, ew, (grad_e, samples), True, after, 0.01))
        grad_e = r.grad
        return across(r.out_ge, 1)

    def middle_0(c, gv, stash):
        m = done(node_stage(c[1], False, True, 0, here, (in_nodes, c[0]), c[0], nw, nvec, [(gv, 0)], stash=stash, box=(None, c[1], 0), after=after, micros=50))
        m.got = beside(m.box_a, m.box_b, (0,))
        leave(stash)
        return stay(m, "ops", "dv", "own", "out_gv")

    def backward_0(c, ge, f, m, box):
        b = done(edge_backward(c[1], 0, here, None, (ge, 0), ((m.got[0], 0), m.own, (m.got[1], 0)), c[0], f, m.out_gv, hot, ew, evec, box, after, 50))
        leave(f)
        return stay(b, "ops", "sops", "dv", "own")

    def out_0(c, ge, b):
        nonlocal grad_e
        grad_e = done(edge_out(c[1], 0, here, None, (ge, 0), c[0], b.ops, ew, (grad_e, samples), False, after, 2)).grad

    def node_grads(on, m, first):
        nonlocal acc_n
        acc_n = done(node_weights(on, here, m, acc_n, first, after))
        leave(m)

    def edge_grads(on, c, b, f, first, node_dv=()):
        nonlocal acc_e
        acc_e = done(edge_weights(c[1], on, here, b, list(node_dv), f.e, f.v, pad, acc_e, first, after, 2))
        leave(b)

    f0p = forward_0(p, relay_sizes[0])
    got = beside(f0p.box_a, f0p.box_b)
    e0 = [across(f0p.relay[0], 0)]
    _, nw = prepare(node_w1[0], node_w2[0], after=after)
    n0p = nodes_0(p, f0p, got)
    v0, y = across(n0p.out_v, 0), across(n0p.out_v, 0, 1)
    held = done(gate(after, *f0p.relay[1:]))
    first = (v0, y) + tuple(e0)
    e0 += [across(getattr(held, key), 0) for key, _ in zip("xyz", f0p.relay[1:])]
    f0q = forward_0(q, relay_sizes[1])
    v0 = (swap(v0, 0, (1,)), v0, y)
    held = done(gate(after + first, f0q.box_a, f0q.box_b, *f0q.relay, micros=50))
    e1 = [across(getattr(held, key), 0) for key, _ in zip("zuvw", f0q.relay)]
    got_q = beside(held.x, held.y, (0,))
    f1p = forward_1(p, e0, v0, (None, p[1], 0))
    got = beside(f1p.box_a, f1p.box_b)
    n0q = nodes_0(q, f0q, got_q)
    v1, y = across(n0q.out_v, 0), across(n0q.out_v, 0, 1)
    n1p = middle_1(p, f1p, got, 0, (None, p[1], 0))
    got_p = beside(n1p.box_a, n1p.box_b)
    b1p = backward_1(p, f1p, n1p, got_p, 0, (None, p[1], 0))
    got_p = beside(b1p.box_a, b1p.box_b)
    v1 = done(gate(after, v1, make=loose)).x
    f1q = forward_1(q, e1, (swap(v1, 0, None), v1, y), (None, q[1], 0))
    got_q = beside(f1q.box_a, f1q.box_b)
    ge0 = out_1(p, b1p)
    gv0 = across(add_1(p, b1p, got_p, 0), 1)
    n1q = middle_1(q, f1q, got_q, 0, (None, q[1], 0))
    got_q = beside(n1q.box_a, n1q.box_b)
    m0p = middle_0(p, gv0, n0p)
    node_grads(1, n1p, True)
    b1q = backward_1(q, f1q, n1q, got_q, 0, (None, q[1], 0))
    got_q = beside(b1q.box_a, b1q.box_b)
    ge1 = out_1(q, b1q)
    gv1 = aside(add_1(q, b1q, got_q, 0), 1)
    node_grads(1, n1q, False)
    edge_grads(1, p, b1p, f1p, True)
    edge_grads(1, q, b1q, f1q, False, (n1p.dv, n1q.dv))
    b0p = backward_0(p, ge0, f0p, m0p, (None, both, 0))
    gv1 = back(done(gate(after, gv1, make=loose)).x, 0)
    edge_grads(0, p, b0p, f0p, True)
    m0q = middle_0(q, gv1, n0q)
    node_grads(0, m0p, True)
    node_grads(0, m0q, False)
    b0q = backward_0(q, ge1, f0q, m0q, ((b0p.box_a, b0p.box_b), both, p[1]))
    got = beside(b0q.box_a, b0q.box_b)
    edge_grads(0, q, b0q, f0q, False, (m0p.dv, m0q.dv))
    bits = list(range(count.bit_length() - 1))
    yzz, zyz, yzz_turned = [[0] + [bits[i] for i in order] + bits[4:] for order in ((1, 2, 3), (2, 1, 3), (1, 3, 2))]
    total_e = Total(acc_e.total, here, (yzz_turned, zyz), (3 * F, F), True)
    after = total_e.step(after)
    total_n = Total(acc_n.total, here, (yzz, zyz), (2 * F, F))
    totals = [total_e, total_n]
    after = total_n.step(after)
    for turn in range(2 * len(bits)):
        for t in totals:
            after = t.step(after)
        if turn == 0:
            out_0(p, ge0, b0p)
            out_0(q, ge1, b0q)
        if turn == 1:
            grad_n = done(add_parts(0, here, [(x, 0) for x in got], [b0p.own, b0q.own], 0, (grad_n, samples), False, after)).grad
    edge_1, edge_2, edge_v, node_v = total_e.result
    node_1, node_2 = total_n.result
    return (
        act_n[None], act_e[None], grad_n[None], grad_e[None],
        edge_1[None], edge_2[None], edge_v[None], node_1[None], node_2[None], node_v[None],
    )


def solution(mesh):
    nodes, rows, weights = P(None, "node", None), P("node"), P("section", None, None)
    stacked = P("section", None, "node", None)
    in_specs = (nodes, nodes, rows, rows) + (weights,) * 6 + (nodes, nodes, P(), P())
    out_specs = (stacked,) * 4 + (weights,) * 6
    return jax.shard_map(on_device, mesh=mesh, in_specs=in_specs, out_specs=out_specs, check_vma=False)
```

```python
from types import SimpleNamespace

import jax
import jax.numpy as jnp
from jax import lax
from jax.experimental import pallas as pl
from jax.experimental.pallas import tpu as pltpu
from jax.sharding import PartitionSpec as P

f32, bf16 = jnp.float32, jnp.bfloat16
norm_eps = 1e-05
NN = ((1,), (0,))
NT = ((1,), (1,))
TN = ((0,), (0,))
group_sizes = (4, 4)
relay_sizes = ((2, 2), (2, 2))
MIB = 1024 * 1024


def split(x):
    hi = x.astype(bf16)
    return hi, (x - hi.astype(f32)).astype(bf16)


def dot1(a, b, dims):
    return lax.dot_general(a, b, (dims, ((), ())), preferred_element_type=f32)


def dot3(a, b, dims):
    return dot1(a[0], b[0], dims) + (dot1(a[0], b[1], dims) + dot1(a[1], b[0], dims))


def dot3_few(a, b, dims):
    rows = a[0].shape[0]
    both = dot1(jnp.concatenate(a, axis=0), b[0], dims)
    return both[:rows] + (both[rows:] + dot1(a[0], b[1], dims))


def normalized(u):
    c = u - jnp.mean(u, axis=-1, keepdims=True)
    r = lax.rsqrt(jnp.mean(c * c, axis=-1, keepdims=True) + norm_eps)
    return c * r, r


def norm_back(gu, n, r, gain):
    t = gu * gain
    return r * (t - jnp.mean(t, axis=-1, keepdims=True) - n * jnp.mean(t * n, axis=-1, keepdims=True))


def column_sums(*xs):
    F = xs[0].shape[-1]
    return jnp.concatenate([jnp.sum(x, axis=0, keepdims=True) for x in xs] + [jnp.zeros((8 - len(xs), F), f32)], axis=0)


class Copies:
    def __init__(self, sems):
        self.sems, self.all = sems, []

    def __call__(self, src, dst):
        c = pltpu.make_async_copy(src, dst, self.sems.at[len(self.all)])
        self.all.append(c)
        c.start()
        return c

    def wait(self):
        wait(*self.all)


def wait(*copies):
    for c in copies:
        c.wait()


def far(*shape, dtype=f32):
    return pltpu.HBM(shape, dtype)


def near(*shape, dtype=f32):
    return pltpu.VMEM(shape, dtype)


resident = []


def loose(*shape):
    return jax.ShapeDtypeStruct(shape, f32)


def call(body, name, scalars={}, hbm={}, vmem={}, free={}, outs={}, grow={}, scratch={}, after=(), micros=2, copies=24, active=None):
    args, specs, where = [], [], {}

    def add(values, space, pinned):
        for key, value in values.items():
            at = []
            for x in value if isinstance(value, (list, tuple)) else [value]:
                at.append(len(args))
                args.append(pltpu.with_memory_space_constraint(x, space) if pinned else x)
                specs.append(pl.BlockSpec(memory_space=space))
            where[key] = at if isinstance(value, (list, tuple)) else at[0]

    add(scalars, pltpu.SMEM, False)
    add(hbm, pltpu.HBM, True)
    add(vmem, pltpu.VMEM, True)
    add(free, pl.ANY, False)
    add(dict(after=[x for x in after if x.shape == (8, 128)]), pltpu.HBM, True)
    add(dict(arrived=[x for x in after if x.shape != (8, 128)]), pl.ANY, False)
    used = {id(x) for value in vmem.values() for x in (value if isinstance(value, (list, tuple)) else [value])}
    add(dict(kept=[x for x in resident if id(x) not in used]), pltpu.VMEM, True)
    shapes, out_specs, aliases = [], [], {}
    for key, value in list(outs.items()) + list(grow.items()) + [("token", far(8, 128))]:
        old, shape = value if key in grow else (None, value)
        space = pl.ANY if isinstance(shape, jax.ShapeDtypeStruct) else shape.memory_space
        where[key] = -1 - len(shapes)
        if old is not None:
            aliases[len(args)] = len(shapes)
            args.append(old if space is pl.ANY else pltpu.with_memory_space_constraint(old, space))
            specs.append(pl.BlockSpec(memory_space=space))
        shapes.append(shape)
        out_specs.append(pl.BlockSpec(memory_space=space))
    first_out, first_scratch = len(args), len(args) + len(shapes)
    kept = dict(scratch)

    def kernel(*refs):
        k = SimpleNamespace()
        pick = lambda i: refs[i] if i >= 0 else refs[first_out - 1 - i]
        for key, at in where.items():
            setattr(k, key, [pick(i) for i in at] if isinstance(at, list) else pick(at))
        for i, key in enumerate(kept):
            setattr(k, key, refs[first_scratch + i])
        k.load, k.store = Copies(refs[-2]), Copies(refs[-1])
        if active is None:
            body(k)
        else:
            pl.when(k.here[0] == active)(lambda: body(k))

    res = pl.pallas_call(
        kernel,
        out_shape=shapes,
        in_specs=specs,
        out_specs=out_specs,
        scratch_shapes=list(kept.values()) + [pltpu.SemaphoreType.DMA((copies,))] * 2,
        input_output_aliases=aliases,
        compiler_params=pltpu.CompilerParams(vmem_limit_bytes=16 * MIB),
        cost_estimate=pl.CostEstimate(flops=int(micros * 1.15e9), bytes_accessed=0, transcendentals=0),
        name=name,
    )(*args)
    return SimpleNamespace(**{key: res[-1 - at] for key, at in where.items() if not isinstance(at, list) and at < 0})


def prepare(w1, w2, ends=None, here=None, W=0, after=()):
    F = w1.shape[1]

    def body(k):
        c2 = k.load(k.w2, k.b2)
        parts = [pl.ds(i, F) for i in range(0, w1.shape[0], F)]
        c1 = [k.load(k.w1.at[part], k.b1.at[part]) for part in parts]
        ce = [k.load(src, ref) for src, ref in zip(k.ends, (k.e0, k.e1))] if ends is not None else []
        c2.wait()
        k.h2[...], k.l2[...] = split(k.b2[...])
        for part, c in zip(parts, c1):
            c.wait()
            k.h1[part], k.l1[part] = split(k.b1[part])
        if ends is not None:
            wait(*ce)
            hots = []
            for ref in (k.e0, k.e1):
                total = k.here[2] * (W // 3)
                at = ref[...] - (k.here[1] - 1) * (W // 3)
                at = jnp.where(at < 0, at + total, at)
                at = jnp.where(at >= total, at - total, at)
                hots.append((lax.broadcasted_iota(jnp.int32, (W, at.shape[1]), 0) == at).astype(f32).astype(bf16))
            both = jnp.concatenate(hots, axis=0)
            k.gather[...] = jnp.concatenate([both, both], axis=0)
            k.scatter[...] = jnp.concatenate([both, both], axis=1)

    half = lambda *s: near(*s, dtype=bf16)
    outs = dict(h1=half(*w1.shape), l1=half(*w1.shape), h2=half(*w2.shape), l2=half(*w2.shape))
    scalars, hbm = {}, dict(w1=w1, w2=w2)
    scratch = dict(b1=pltpu.VMEM(w1.shape, f32), b2=pltpu.VMEM(w2.shape, f32))
    if ends is not None:
        rows = ends[0].shape[1]
        outs.update(gather=half(4 * W, rows), scatter=half(2 * W, 2 * rows))
        scalars = dict(here=here)
        hbm.update(ends=list(ends))
        scratch.update(e0=pltpu.VMEM((1, rows), jnp.int32), e1=pltpu.VMEM((1, rows), jnp.int32))
    r = call(body, "prepare", scalars, hbm, outs=outs, scratch=scratch, after=after)
    resident.extend([r.h1, r.l1, r.h2, r.l2])
    if ends is not None:
        resident.extend([r.gather, r.scatter])
    return r, dict(w1=[r.h1, r.l1], w2=[r.h2, r.l2])


def side_rows(par, nr):
    return pl.multiple_of((1 - par) * 2 * nr, 16), pl.multiple_of(par * 2 * nr, 16)


def window_parts(k, ref, nr):
    a_at, b_at = side_rows(k.here[1] % 2, nr)
    return [ref.at[:, pl.ds(a_at, nr), :], ref.at[:, nr:2 * nr, :], ref.at[:, pl.ds(b_at, nr), :]]


def sample_weight(k, sample, micro, steps):
    m, t = divmod(sample, steps)
    return jnp.where(t < k.here[3 + m], k.here[3 + micro + sample], 0).astype(f32)


def load_views(k, views, refs, targets, g):
    return [k.load(ref.at[pl.ds(view[1], g)], target) for view, ref, target in zip(views, refs, targets)]


def arrays(views):
    return [v[0] for v in views]


def chunk(g):
    return 2 if g % 2 == 0 else 1


def edge_forward(g, active, here, e, v, n, hot, w, vec, act, box, relay, after, micros):
    rows, F = e[0][0].shape[1:]
    nr = v[0][0].shape[1]
    W = 3 * nr
    cs, part_size = g, chunk(g)

    def body(k):
        load, store = k.load, k.store
        cv = load_views(k, v, k.v, window_parts(k, k.vb, nr), g)
        ce = load_views(k, e, k.e, [k.eb.at[pl.ds(s, part_size)] for s in range(0, g, part_size)], part_size)
        (w1h, w1l), (w2h, w2l), vec = k.w1, k.w2, k.vec
        wait(*cv)
        vw = split(k.vb[...].reshape(g * W, F))
        for i in (0, 1):
            part = pl.ds((i + 1) * F, F)
            h, l = split(dot3(vw, (w1h[part], w1l[part]), NN).reshape(g, W, F))
            k.pp[:, i * W:(i + 1) * W] = h
            k.pp[:, (i + 2) * W:(i + 3) * W] = l
        for s in range(0, g, cs):
            wait(*ce)
            to = pl.ds(s, cs)
            x = k.eb[to].reshape(cs * rows, F)
            a = dot3(split(x), (w1h[0:F], w1l[0:F]), NN) + vec[0:1]
            a = a + jnp.concatenate([dot1(k.gather[...], k.pp[s + t], TN) for t in range(cs)], axis=0)
            k.out_a[to] = a.reshape(cs, rows, F)
            h = a / (1 + jnp.exp(-a))
            n_, r = normalized(dot3(split(h), (w2h[...], w2l[...]), NN) + vec[1:2])
            k.out_n[to] = n_.reshape(cs, rows, F)
            k.out_r[to] = jnp.broadcast_to(r, (cs * rows, 128)).reshape(cs, rows, 128)
            m = n_ * vec[2:3] + vec[3:4]
            k.ob[to] = (x + m).reshape(cs, rows, F)
            done = 0
            for key, size in zip(names, relay):
                store(k.ob.at[pl.ds(done, size)], getattr(k, key))
                done += size
            for t in range(g):
                store(k.ob.at[t], k.act.at[n + t])
            mh, ml = split(m.reshape(cs, rows, F))
            for t in range(cs):
                k.sb[s + t] = dot1(k.scatter[W:], jnp.concatenate([mh[t], ml[t]], axis=0), NN)
        sides = window_parts(k, k.sb, nr)
        store(sides[0], k.box_a.at[pl.ds(box[2], g)])
        store(sides[1], k.own)
        store(sides[2], k.box_b.at[pl.ds(box[2], g)])
        store.wait()

    outs = dict(out_a=near(g, rows, F), out_n=near(g, rows, F), out_r=near(g, rows, 128), own=far(g, nr, F))
    names = "abcd"[:len(relay)]
    outs.update({key: far(size, rows, F) for key, size in zip(names, relay)})
    old = box[0] or (None, None)
    grow = dict(act=(act[0], far(act[1], rows, F)), box_a=(old[0], far(box[1], nr, F)), box_b=(old[1], far(box[1], nr, F)))
    full = pltpu.VMEM((g, rows, F), f32)
    scratch = dict(eb=full, ob=full, vb=pltpu.VMEM((g, W, F), f32), sb=pltpu.VMEM((g, W, F), f32), pp=pltpu.VMEM((g, 4 * W, F), bf16))
    r = call(body, "edge_forward", dict(here=here), active=active, vmem=dict(**w, gather=hot.gather, scatter=hot.scatter, vec=vec), free=dict(e=arrays(e), v=arrays(v)), outs=outs, grow=grow, scratch=scratch, after=after, micros=micros)
    r.relay = [getattr(r, key) for key in names]
    return r


def node_stage(g, forward, backward, active, here, v, n, w, vec, parts, act=None, stash=None, weights=None, cot=None, box=None, after=(), micros=2):
    nr, F = v[0].shape[1:]
    R = g * nr

    def body(k):
        load, store = k.load, k.store
        cx = [load(k.v.at[pl.ds(v[1], g)], k.zb.at[:, :, 0:F])] + load_views(k, parts, k.parts, [k.pb.at[i] for i in range(len(parts))], g)
        if forward and backward:
            cx.append(load(k.cot.at[pl.ds(n, g)], k.gb))
        w1, w2, vec = (k.w1[0][...], k.w1[1][...]), (k.w2[0][...], k.w2[1][...]), k.vec
        wait(*cx)
        given = sum([k.pb[i] for i in range(1, len(parts))], k.pb[0])
        k.zb[:, :, F:] = given if forward else k.gathered[...]
        z = k.zb[...].reshape(R, 2 * F)
        zs = split(z)
        if forward:
            a = dot3_few(zs, w1, NN) + vec[0:1]
            h = a / (1 + jnp.exp(-a))
            n_, r = normalized(dot3_few(split(h), w2, NN) + vec[1:2])
            k.ob[...] = (z[:, :F] + n_ * vec[2:3] + vec[3:4]).reshape(g, nr, F)
            if not backward:
                store(k.ob, k.out_v)
                k.out_a[...] = a.reshape(g, nr, F)
                k.out_n[...] = n_.reshape(g, nr, F)
                k.out_r[...] = jnp.broadcast_to(r, (R, 128)).reshape(g, nr, 128)
                k.out_g[...] = given
            store(k.ob, k.act.at[pl.ds(n, g)])
        else:
            a, n_, r = k.a[...].reshape(R, F), k.n[...].reshape(R, F), k.r[...].reshape(R, 128)[:, 0:1]
        if backward:
            if forward:
                for s in range(g):
                    k.gb[s] = k.gb[s] * sample_weight(k, n + s, *weights)
                gu = k.gb[...].reshape(R, F)
            else:
                gu = given.reshape(R, F)
            gp = norm_back(gu, n_, r, vec[2:3])
            q = 1 / (1 + jnp.exp(-a))
            hs, gps = split(a * q), split(gp)
            ga = dot3_few(gps, w2, NT) * (q * (1 + a * (1 - q)))
            gas = split(ga)
            gz = dot3_few(gas, w1, NT)
            k.ggb[...] = gz[:, F:].reshape(g, nr, F)
            for ref in (k.box_a, k.box_b):
                store(k.ggb, ref.at[pl.ds(box[2], g)])
            k.own[...] = k.ggb[...]
            k.out_gv[...] = (gu + gz[:, :F]).reshape(g, nr, F)
            for i, x in enumerate((zs[0][:, :F], zs[1][:, :F], zs[0][:, F:], zs[1][:, F:], hs[0], hs[1], gas[0], gas[1], gps[0], gps[1])):
                k.ops[i] = x
            k.dv[...] = column_sums(ga, gp, gu * n_, gu)
        store.wait()

    hbm, vmem, free = {}, dict(**w, vec=vec), dict(v=v[0], parts=arrays(parts))
    shape = near(g, nr, F)
    outs, grow = {}, {}
    if not forward:
        vmem.update(a=stash.out_a, n=stash.out_n, r=stash.out_r, gathered=stash.out_g)
    elif backward:
        hbm.update(cot=cot)
    if forward:
        grow.update(act=(act[0], far(act[1], nr, F)))
        if not backward:
            outs.update(out_v=far(g, nr, F), out_a=shape, out_n=shape, out_r=near(g, nr, 128), out_g=shape)
    if backward:
        old = box[0] or (None, None)
        outs.update(own=shape, out_gv=shape, ops=near(10, R, F, dtype=bf16), dv=near(8, F))
        grow.update(box_a=(old[0], far(box[1], nr, F)), box_b=(old[1], far(box[1], nr, F)))
    small = pltpu.VMEM((g, nr, F), f32)
    scratch = dict(zb=pltpu.VMEM((g, nr, 2 * F), f32), pb=pltpu.VMEM((len(parts), g, nr, F), f32), gb=small, ob=small, ggb=small)
    return call(body, "node_stage", dict(here=here), hbm, vmem, free, active=active, outs=outs, grow=grow, scratch=scratch, after=after, micros=micros)


def node_weights(active, here, m, acc, first, after):
    _, R, F = m.ops.shape

    def body(k):
        o = k.ops
        for i, (x, y) in enumerate(((0, 6), (2, 6), (4, 8))):
            part = pl.ds(i * F, F)
            d = dot3((o[x], o[x + 1]), (o[y], o[y + 1]), TN)
            k.total[part] = d if first else k.total[part] + d

    grow = dict(total=(acc and acc.total, near(3 * F, F)))
    return call(body, "node_weights", dict(here=here), active=active, vmem=dict(ops=m.ops), grow=grow, after=after, micros=0.01)


def edge_backward(g, active, here, weights, ge, gg, n, stash, gv, hot, w, vec, box, after, micros):
    rows, F = ge[0].shape[1:]
    nr = gv.shape[1]
    W = 3 * nr
    cs = g

    def body(k):
        load, store = k.load, k.store
        gg_at = window_parts(k, k.ggb, nr)
        cg = load_views(k, (gg[0], gg[2]), k.gg, (gg_at[0], gg_at[2]), g)
        cx = [load(k.ge.at[ge[1] + s], k.gb.at[s]) for s in range(g)]
        k.ggb[:, nr:2 * nr] = k.gg_own[...]
        (w1h, w1l), (w2h, w2l), vec = k.w1, k.w2, k.vec
        wait(*cg)
        h, l = split(k.ggb[...])
        k.gg2[:, 0:W] = h
        k.gg2[:, W:] = l
        flat = lambda x: x.reshape(cs * rows, x.shape[-1])
        sums = []
        for s in range(0, g, cs):
            to = pl.ds(s, cs)
            wait(*cx)
            if weights:
                for t in range(s, s + cs):
                    k.gb[t] = k.gb[t] * sample_weight(k, n + t, *weights)
            hot_r = k.gather[pl.ds(W, W)]
            gu = flat(k.gb[to]) + jnp.concatenate([dot1(hot_r, k.gg2[s + t, 0:W], TN) + dot1(hot_r, k.gg2[s + t, W:], TN) for t in range(cs)], axis=0)
            n_, a = flat(k.n[to]), flat(k.a[to])
            gp = norm_back(gu, n_, flat(k.r[to])[:, 0:1], vec[2:3])
            gps = split(gp)
            q = 1 / (1 + jnp.exp(-a))
            ga = dot3(gps, (w2h[...], w2l[...]), NT) * (q * (1 + a * (1 - q)))
            gas = split(ga)
            for i, x in enumerate((*split(a * q), *gps, *gas)):
                k.ops[i, pl.ds(s * rows, cs * rows)] = x
            for t in range(cs):
                both = jnp.concatenate([x[t * rows:(t + 1) * rows] for x in gas], axis=0)
                k.ssb[s + t] = dot1(k.scatter[...], both, NN)
            sums.append(column_sums(ga, gp, gu * n_, gu))
        ss = split(k.ssb[:, 0:W].reshape(g * W, F))
        sr = split(k.ssb[:, W:].reshape(g * W, F))
        for i, x in enumerate((*ss, *sr)):
            k.sops[i] = x
        wg = dot3(ss, (w1h[F:2 * F], w1l[F:2 * F]), NT) + dot3(sr, (w1h[2 * F:], w1l[2 * F:]), NT)
        k.wgb[...] = wg.reshape(g, W, F)
        k.wgb[:, nr:2 * nr] += k.gv[...]
        sides = window_parts(k, k.wgb, nr)
        store(sides[0], k.box_a.at[pl.ds(box[2], g)])
        store(sides[2], k.box_b.at[pl.ds(box[2], g)])
        k.own[...] = k.wgb[:, nr:2 * nr]
        k.dv[...] = sum(sums[1:], sums[0])
        store.wait()

    free = dict(ge=ge[0], gg=[gg[0][0], gg[2][0]])
    vmem = dict(**w, vec=vec, a=stash.out_a, n=stash.out_n, r=stash.out_r, gv=gv, gg_own=gg[1], gather=hot.gather, scatter=hot.scatter)
    old = box[0] or (None, None)
    outs = dict(own=near(g, nr, F), ops=near(6, g * rows, F, dtype=bf16), sops=near(4, g * W, F, dtype=bf16), dv=near(8, F))
    grow = dict(box_a=(old[0], far(box[1], nr, F)), box_b=(old[1], far(box[1], nr, F)))
    scratch = dict(gb=pltpu.VMEM((g, rows, F), f32), ggb=pltpu.VMEM((g, W, F), f32), gg2=pltpu.VMEM((g, 2 * W, F), bf16), ssb=pltpu.VMEM((g, 2 * W, F), f32), wgb=pltpu.VMEM((g, W, F), f32))
    return call(body, "edge_backward", dict(here=here), active=active, vmem=vmem, free=free, outs=outs, grow=grow, scratch=scratch, after=after, micros=micros)


def add_parts(active, here, views, own, n, grad, relay, after):
    g, (nr, F) = sum(x.shape[0] for x in own), own[0].shape[1:]

    def body(k):
        wait(*load_views(k, views, k.views, [k.pb.at[i] for i in (0, 1)], g))
        done = 0
        for x in k.own:
            to = pl.ds(done, x.shape[0])
            k.pb[0, to] = k.pb[0, to] + k.pb[1, to] + x[...]
            done += x.shape[0]
        if relay:
            k.store(k.pb.at[0], k.out)
        k.store(k.pb.at[0], k.grad.at[pl.ds(n, g)])
        k.store.wait()

    outs = dict(out=far(g, nr, F)) if relay else {}
    grow = dict(grad=(grad[0], far(grad[1], nr, F)))
    return call(body, "add_parts", dict(here=here), active=active, vmem=dict(own=own), free=dict(views=arrays(views)), outs=outs, grow=grow, scratch=dict(pb=pltpu.VMEM((2, g, nr, F), f32)), after=after, micros=0.01)


def edge_out(g, active, here, weights, ge, n, ops, w, grad, relay, after, micros):
    rows, F = ge[0].shape[1:]
    halves = (0, 1) if g % 2 == 0 else (0,)
    m = g // len(halves)

    def body(k):
        cs = [k.load(k.ge.at[pl.ds(ge[1] + i * m, m)], k.gb.at[pl.ds(i * m, m)]) for i in halves]
        w1h, w1l = k.w1
        for i in halves:
            own = dot3([k.ops[x, pl.ds(i * m * rows, m * rows)] for x in (4, 5)], (w1h[0:F], w1l[0:F]), NT)
            cs[i].wait()
            if weights:
                for t in range(i * m, (i + 1) * m):
                    k.gb[t] = k.gb[t] * sample_weight(k, n + t, *weights)
            to = pl.ds(i * m, m)
            k.gb[to] = k.gb[to] + own.reshape(m, rows, F)
            if relay:
                k.store(k.gb.at[to], k.out_ge.at[to])
            k.store(k.gb.at[to], k.grad.at[pl.ds(n + i * m, m)])
        k.store.wait()

    outs = dict(out_ge=far(g, rows, F)) if relay else {}
    grow = dict(grad=(grad[0], far(grad[1], rows, F)))
    return call(body, "edge_out", dict(here=here), active=active, vmem=dict(ops=ops, w1=w["w1"]), free=dict(ge=ge[0]), outs=outs, grow=grow, scratch=dict(gb=pltpu.VMEM((g, rows, F), f32)), after=after, micros=micros)


def edge_weights(g, active, here, b, node_dv, e, v, pad, acc, first, after, micros):
    rows, F = e[0][0].shape[1:]
    nr = v[0][0].shape[1]
    W = 3 * nr

    def body(k):
        cs = chunk(g)
        ce = load_views(k, e, k.e, [k.eb.at[pl.ds(s, cs)] for s in range(0, g, cs)], cs)
        cv = load_views(k, v, k.v, window_parts(k, k.vb, nr), g)
        o = k.ops

        def put(total, i, x, y):
            part = pl.ds(i * F, F)
            d = dot3(x, y, TN)
            total[part] = d if first else total[part] + d

        put(k.total, 3, (o[0], o[1]), (o[2], o[3]))
        if first:
            k.total[4 * F:] = jnp.zeros((pad, F), f32)
        k.total[4 * F:4 * F + 8] += k.dv[...]
        if node_dv:
            k.total[4 * F + 8:4 * F + 16] = sum([x[...] for x in k.node_dv[1:]], k.node_dv[0][...])
        wait(*cv)
        vs = split(k.vb[...].reshape(g * W, F))
        for i in (0, 1):
            put(k.total, i + 1, vs, (k.sops[2 * i], k.sops[2 * i + 1]))
        wait(*ce)
        put(k.total, 0, split(k.eb[...].reshape(g * rows, F)), (o[4], o[5]))

    vmem = dict(ops=b.ops, sops=b.sops, dv=b.dv)
    if node_dv:
        vmem.update(node_dv=node_dv)
    grow = dict(total=(acc and acc.total, near(4 * F + pad, F)))
    scratch = dict(eb=pltpu.VMEM((g, rows, F), f32), vb=pltpu.VMEM((g, W, F), f32))
    return call(body, "edge_weights", dict(here=here), active=active, vmem=vmem, free=dict(e=arrays(e), v=arrays(v)), grow=grow, scratch=scratch, after=after, micros=micros)


def gate(after, *xs, make=far, micros=0.01):
    return call(lambda k: None, "gate", grow={name: (x, make(*x.shape)) for name, x in zip("xyzuvw", xs)}, after=after, micros=micros)


class Total:
    def __init__(self, x, here, orders, cuts, vecs=False):
        self.vecs = vecs
        count = lax.axis_size("node")
        self.here, self.orders = dict(here=here), orders
        self.swaps = [[(i, i ^ (1 << (y if i % 2 else x))) for i in range(count)] for x, y in zip(*orders)]
        self.x, self.cuts = x, cuts
        self.rows, self.F = x.shape
        self.sizes, rows = [], self.rows
        while len(self.sizes) < len(self.swaps) and rows % 16 == 0:
            rows //= 2
            self.sizes.append(rows)
        self.got, self.result, self.token, self.done = [], None, None, False
        self.steps = self.run()

    def flag(self, ref, step):
        x, y = (order[step] for order in self.orders)
        node = ref.here[1]
        return jnp.where(node % 2 == 1, node >> y, node >> x) & 1

    def partial(self, k):
        K, sizes = len(self.sizes), self.sizes
        size = sizes[min(k, K - 1)]

        def body(ref):
            def start(after):
                at = sum(self.flag(ref, m) * sizes[m] for m in range(after + 1, k)) if after + 1 < k else 0
                if k < K:
                    at = at + (1 - self.flag(ref, k)) * size
                return pl.multiple_of(at, 8)

            total = ref.x[pl.ds(start(-1), size)]
            for j, x in enumerate(ref.got):
                total = total + x[pl.ds(start(j), size)]
            ref.out[...] = total

        r = call(body, "partial_sum", self.here, vmem=dict(x=self.x, got=self.got[:k]), outs=dict(out=near(size, self.F)), after=self.after, micros=50)
        self.token = (r.token,)
        return r.out

    def add(self, x, y):
        def body(k):
            k.out[...] = k.x[...] + k.y[...]

        r = call(body, "add", self.here, vmem=dict(x=x, y=y), outs=dict(out=near(*x.shape)), after=self.after, micros=50)
        self.token = (r.token,)
        return r.out

    def join(self, own, got, step):
        R = own.shape[0]

        def body(k):
            bit = self.flag(k, step)
            k.joined[pl.ds(pl.multiple_of(bit * R, 8), R)] = k.own[...]
            k.joined[pl.ds(pl.multiple_of((1 - bit) * R, 8), R)] = k.got[...]

        r = call(body, "join", self.here, vmem=dict(own=own, got=got), outs=dict(joined=near(2 * R, self.F)), after=self.after, micros=50)
        self.token = (r.token,)
        return r.joined

    def finish(self, own, got):
        R = own.shape[0]
        names = "abcdef"[:len(self.cuts)]

        def put(k, low, high):
            done = 0
            for key, rows in zip(names, self.cuts):
                for src, at in ((low, 0), (high, R)):
                    a, b = max(at, done), min(at + R, done + rows)
                    for i in range(a, b, 256):
                        size = min(256, b - i)
                        k.store(src.at[pl.ds(i - at, size)], getattr(k, key).at[pl.ds(i - done, size)])
                done += rows
            if self.vecs:
                assert done >= R
                k.va[...] = high[done - R:done - R + 4]
                k.vb[...] = high[done - R + 8:done - R + 12]
                k.store(k.va, k.first)
                k.store(k.vb, k.second)
            k.store.wait()

        def body(k):
            bit = self.flag(k, 0)
            pl.when(bit == 0)(lambda: put(k, k.own, k.got))
            k.store.all = []
            pl.when(bit == 1)(lambda: put(k, k.got, k.own))

        outs = {key: far(rows, self.F) for key, rows in zip(names, self.cuts)}
        scratch = {}
        if self.vecs:
            outs.update(first=far(4, self.F), second=far(4, self.F))
            scratch.update(va=pltpu.VMEM((4, self.F), f32), vb=pltpu.VMEM((4, self.F), f32))
        r = call(body, "finish", self.here, vmem=dict(own=own, got=got), outs=outs, scratch=scratch, after=self.after, micros=50)
        self.token = (r.token,)
        return [getattr(r, key) for key in outs]

    def run(self):
        K = len(self.sizes)
        for k in range(K):
            send = self.partial(k)
            self.got.append(lax.ppermute(send, "node", self.swaps[k]))
            yield
        own = self.partial(K)
        for pairs in self.swaps[K:]:
            got = lax.ppermute(own, "node", pairs)
            yield
            own = self.add(own, got)
        for k in reversed(range(K)):
            got = lax.ppermute(own, "node", self.swaps[k])
            yield
            if k:
                own = self.join(own, got, k)
            else:
                self.result = self.finish(own, got)
        self.done = True

    def step(self, after):
        if self.done:
            return after
        self.after = after
        next(self.steps, None)
        return self.token


def on_device(in_nodes, in_edges, senders, receivers, edge_w1, edge_w2, edge_vec, node_w1, node_w2, node_vec, cot_nodes, cot_edges, lengths, step_mask):
    samples, nr, F = in_nodes.shape
    count = lax.axis_size("node")
    section, node = lax.axis_index("section"), lax.axis_index("node")
    evec, nvec = edge_vec[0], node_vec[0]
    here = jnp.concatenate([jnp.stack([section, node, count]).astype(jnp.int32), lengths, step_mask.reshape(-1)])
    live = step_mask.shape

    def partner(i, side):
        return i ^ 1 if side == 0 else (i - 1 + 2 * (i % 2)) % count

    def swap(x, side, planes):
        if planes is None:
            return lax.ppermute(x, "node", [(i, partner(i, side)) for i in range(count)])
        return lax.ppermute(x, ("section", "node"), [(s * count + i, s * count + partner(i, side)) for s in planes for i in range(count)])

    def beside(to_a, to_b, planes=None):
        return swap(to_a, 0, planes), swap(to_b, 1, planes)

    def across(x, source, side=None):
        if side is None:
            return lax.ppermute(x, "section", [(source, 1 - source)])
        return lax.ppermute(x, ("section", "node"), [(source * count + i, (1 - source) * count + partner(i, side)) for i in range(count)])

    p, q = [(sum(group_sizes[:i]), n) for i, n in enumerate(group_sizes)]
    both = p[1] + q[1]
    pad = 8 * count
    act_e = act_n = acc_n = acc_e = grad_e = grad_n = None
    after = ()

    def done(r):
        nonlocal after
        after = (r.token,)
        return r

    def stay(r, *names):
        r.kept = [getattr(r, name) for name in names]
        resident.extend(r.kept)
        return r

    def leave(*rs):
        for r in rs:
            resident[:] = [x for x in resident if all(x is not y for y in r.kept)]

    resident.clear()
    from_a, from_b = beside(in_nodes, in_nodes)
    hot, ew = prepare(edge_w1[0], edge_w2[0], (senders.reshape(1, -1), receivers.reshape(1, -1)), here, 3 * nr)

    def forward_0(c, relay):
        nonlocal act_e
        v = [(x, c[0]) for x in (from_a, in_nodes, from_b)]
        e = [(in_edges, c[0] + s) for s in range(0, c[1], chunk(c[1]))]
        f = done(edge_forward(c[1], 0, here, e, v, c[0], hot, ew, evec, (act_e, samples), (None, c[1], 0), relay, after, 0.01))
        act_e, f.v, f.e = f.act, v, e
        return stay(f, "out_a", "out_n", "out_r")

    def nodes_0(c, f, got):
        nonlocal act_n
        m = done(node_stage(c[1], True, False, 0, here, (in_nodes, c[0]), c[0], nw, nvec, [(got[0], 0), (f.own, 0), (got[1], 0)], act=(act_n, samples), after=after, micros=0.01))
        act_n = m.act
        return stay(m, "out_a", "out_n", "out_r", "out_g")

    def forward_1(c, e, nodes, box):
        nonlocal act_e
        v, e = [(x, 0) for x in nodes], [(x, s) for x in e for s in range(0, x.shape[0], chunk(c[1]))]
        f = done(edge_forward(c[1], 1, here, e, v, c[0], hot, ew, evec, (act_e, samples), box, (), after, 0.01))
        act_e, f.v, f.e = f.act, v, e
        return stay(f, "out_a", "out_n", "out_r")

    def middle_1(c, f, got, at, box):
        nonlocal act_n
        m = done(node_stage(c[1], True, True, 1, here, f.v[1], c[0], nw, nvec, [(got[0], at), (f.own, 0), (got[1], at)], act=(act_n, samples), weights=live, cot=cot_nodes, box=box, after=after, micros=0.01))
        act_n = m.act
        return stay(m, "ops", "dv", "own", "out_gv")

    def backward_1(c, f, m, got, at, box):
        b = done(edge_backward(c[1], 1, here, live, (cot_edges, c[0]), ((got[0], at), m.own, (got[1], at)), c[0], f, m.out_gv, hot, ew, evec, box, after, 0.01))
        leave(f)
        return stay(b, "ops", "sops", "dv", "own")

    def add_1(c, b, got, at):
        nonlocal grad_n
        r = done(add_parts(1, here, [(x, at) for x in got], [b.own], c[0], (grad_n, samples), True, after))
        grad_n = r.grad
        return r.out

    def out_1(c, b):
        nonlocal grad_e
        r = done(edge_out(c[1], 1, here, live, (cot_edges, c[0]), c[0], b.ops, ew, (grad_e, samples), True, after, 0.01))
        grad_e = r.grad
        return r.out_ge

    def middle_0(c, gv, stash):
        m = done(node_stage(c[1], False, True, 0, here, (in_nodes, c[0]), c[0], nw, nvec, [(gv, 0)], stash=stash, box=(None, c[1], 0), after=after, micros=50))
        m.got = beside(m.box_a, m.box_b, (0,))
        leave(stash)
        return stay(m, "ops", "dv", "own", "out_gv")

    def backward_0(c, ge, f, m, box):
        b = done(edge_backward(c[1], 0, here, None, (ge, 0), ((m.got[0], 0), m.own, (m.got[1], 0)), c[0], f, m.out_gv, hot, ew, evec, box, after, 50))
        leave(f)
        return stay(b, "ops", "sops", "dv", "own")

    def out_0(c, ge, b):
        nonlocal grad_e
        grad_e = done(edge_out(c[1], 0, here, None, (ge, 0), c[0], b.ops, ew, (grad_e, samples), False, after, 2)).grad

    def node_grads(on, m, first):
        nonlocal acc_n
        acc_n = done(node_weights(on, here, m, acc_n, first, after))
        leave(m)

    def edge_grads(on, c, b, f, first, node_dv=()):
        nonlocal acc_e
        acc_e = done(edge_weights(c[1], on, here, b, list(node_dv), f.e, f.v, pad, acc_e, first, after, 2))
        leave(b)

    f0p = forward_0(p, relay_sizes[0])
    got = beside(f0p.box_a, f0p.box_b)
    e0 = [across(f0p.relay[0], 0)]
    _, nw = prepare(node_w1[0], node_w2[0], after=after)
    n0p = nodes_0(p, f0p, got)
    v0, y = across(n0p.out_v, 0), across(n0p.out_v, 0, 1)
    held = done(gate(after, *f0p.relay[1:]))
    first = (v0, y) + tuple(e0)
    e0 += [across(getattr(held, key), 0) for key, _ in zip("xyz", f0p.relay[1:])]
    f0q = forward_0(q, relay_sizes[1])
    v0 = (swap(v0, 0, (1,)), v0, y)
    held = done(gate(after + first, f0q.box_a, f0q.box_b, *f0q.relay, micros=50))
    e1 = [across(getattr(held, key), 0) for key, _ in zip("zuvw", f0q.relay)]
    got_q = beside(held.x, held.y, (0,))
    f1p = forward_1(p, e0, v0, (None, p[1], 0))
    got = beside(f1p.box_a, f1p.box_b)
    n0q = nodes_0(q, f0q, got_q)
    v1, y = across(n0q.out_v, 0), across(n0q.out_v, 0, 1)
    n1p = middle_1(p, f1p, got, 0, (None, p[1], 0))
    got_p = beside(n1p.box_a, n1p.box_b)
    b1p = backward_1(p, f1p, n1p, got_p, 0, (None, p[1], 0))
    got_p = beside(b1p.box_a, b1p.box_b)
    v1 = done(gate(after, v1, make=loose)).x
    f1q = forward_1(q, e1, (swap(v1, 0, None), v1, y), (None, q[1], 0))
    got_q = beside(f1q.box_a, f1q.box_b)
    ge0 = across(out_1(p, b1p), 1)
    gv0 = across(add_1(p, b1p, got_p, 0), 1)
    n1q = middle_1(q, f1q, got_q, 0, (None, q[1], 0))
    got_q = beside(n1q.box_a, n1q.box_b)
    m0p = middle_0(p, gv0, n0p)
    node_grads(1, n1p, True)
    b1q = backward_1(q, f1q, n1q, got_q, 0, (None, q[1], 0))
    got_q = beside(b1q.box_a, b1q.box_b)
    ge1 = out_1(q, b1q)
    gv1 = across(add_1(q, b1q, got_q, 0), 1)
    ge1 = across(done(gate(after, ge1)).x, 1)
    node_grads(1, n1q, False)
    edge_grads(1, p, b1p, f1p, True)
    edge_grads(1, q, b1q, f1q, False, (n1p.dv, n1q.dv))
    b0p = backward_0(p, ge0, f0p, m0p, (None, both, 0))
    m0q = middle_0(q, gv1, n0q)
    edge_grads(0, p, b0p, f0p, True)
    node_grads(0, m0p, True)
    node_grads(0, m0q, False)
    b0q = backward_0(q, ge1, f0q, m0q, ((b0p.box_a, b0p.box_b), both, p[1]))
    got = beside(b0q.box_a, b0q.box_b)
    edge_grads(0, q, b0q, f0q, False, (m0p.dv, m0q.dv))
    bits = list(range(count.bit_length() - 1))
    yzz, zyz, yzz_turned = [[0] + [bits[i] for i in order] + bits[4:] for order in ((1, 2, 3), (2, 1, 3), (1, 3, 2))]
    total_e = Total(acc_e.total, here, (yzz_turned, zyz), (3 * F, F), True)
    after = total_e.step(after)
    total_n = Total(acc_n.total, here, (yzz, zyz), (2 * F, F))
    totals = [total_e, total_n]
    after = total_n.step(after)
    for turn in range(2 * len(bits)):
        for t in totals:
            after = t.step(after)
        if turn == 0:
            out_0(p, ge0, b0p)
            out_0(q, ge1, b0q)
        if turn == 1:
            grad_n = done(add_parts(0, here, [(x, 0) for x in got], [b0p.own, b0q.own], 0, (grad_n, samples), False, after)).grad
    edge_1, edge_2, edge_v, node_v = total_e.result
    node_1, node_2 = total_n.result
    return (
        act_n[None], act_e[None], grad_n[None], grad_e[None],
        edge_1[None], edge_2[None], edge_v[None], node_1[None], node_2[None], node_v[None],
    )


def solution(mesh):
    nodes, rows, weights = P(None, "node", None), P("node"), P("section", None, None)
    stacked = P("section", None, "node", None)
    in_specs = (nodes, nodes, rows, rows) + (weights,) * 6 + (nodes, nodes, P(), P())
    out_specs = (stacked,) * 4 + (weights,) * 6
    return jax.shard_map(on_device, mesh=mesh, in_specs=in_specs, out_specs=out_specs, check_vma=False)
```

```python
from types import SimpleNamespace

import jax
import jax.numpy as jnp
from jax import lax
from jax.experimental import pallas as pl
from jax.experimental.pallas import tpu as pltpu
from jax.sharding import PartitionSpec as P

f32, bf16 = jnp.float32, jnp.bfloat16
norm_eps = 1e-05
NN = ((1,), (0,))
NT = ((1,), (1,))
TN = ((0,), (0,))
group_sizes = (4, 4)
relay_sizes = ((2, 2), (2, 2))
MIB = 1024 * 1024


def split(x):
    hi = x.astype(bf16)
    return hi, (x - hi.astype(f32)).astype(bf16)


def dot1(a, b, dims):
    return lax.dot_general(a, b, (dims, ((), ())), preferred_element_type=f32)


def dot3(a, b, dims):
    return dot1(a[0], b[0], dims) + (dot1(a[0], b[1], dims) + dot1(a[1], b[0], dims))


def dot3_few(a, b, dims):
    rows = a[0].shape[0]
    both = dot1(jnp.concatenate(a, axis=0), b[0], dims)
    return both[:rows] + (both[rows:] + dot1(a[0], b[1], dims))


def normalized(u):
    c = u - jnp.mean(u, axis=-1, keepdims=True)
    r = lax.rsqrt(jnp.mean(c * c, axis=-1, keepdims=True) + norm_eps)
    return c * r, r


def norm_back(gu, n, r, gain):
    t = gu * gain
    return r * (t - jnp.mean(t, axis=-1, keepdims=True) - n * jnp.mean(t * n, axis=-1, keepdims=True))


def column_sums(*xs):
    F = xs[0].shape[-1]
    return jnp.concatenate([jnp.sum(x, axis=0, keepdims=True) for x in xs] + [jnp.zeros((8 - len(xs), F), f32)], axis=0)


class Copies:
    def __init__(self, sems):
        self.sems, self.all = sems, []

    def __call__(self, src, dst):
        c = pltpu.make_async_copy(src, dst, self.sems.at[len(self.all)])
        self.all.append(c)
        c.start()
        return c

    def wait(self):
        wait(*self.all)


def wait(*copies):
    for c in copies:
        c.wait()


def far(*shape, dtype=f32):
    return pltpu.HBM(shape, dtype)


def near(*shape, dtype=f32):
    return pltpu.VMEM(shape, dtype)


resident = []


def loose(*shape):
    return jax.ShapeDtypeStruct(shape, f32)


def call(body, name, scalars={}, hbm={}, vmem={}, free={}, outs={}, grow={}, scratch={}, after=(), micros=2, copies=24, active=None):
    args, specs, where = [], [], {}

    def add(values, space, pinned):
        for key, value in values.items():
            at = []
            for x in value if isinstance(value, (list, tuple)) else [value]:
                at.append(len(args))
                args.append(pltpu.with_memory_space_constraint(x, space) if pinned else x)
                specs.append(pl.BlockSpec(memory_space=space))
            where[key] = at if isinstance(value, (list, tuple)) else at[0]

    add(scalars, pltpu.SMEM, False)
    add(hbm, pltpu.HBM, True)
    add(vmem, pltpu.VMEM, True)
    add(free, pl.ANY, False)
    add(dict(after=[x for x in after if x.shape == (8, 128)]), pltpu.HBM, True)
    add(dict(arrived=[x for x in after if x.shape != (8, 128)]), pl.ANY, False)
    used = {id(x) for value in vmem.values() for x in (value if isinstance(value, (list, tuple)) else [value])}
    add(dict(kept=[x for x in resident if id(x) not in used]), pltpu.VMEM, True)
    shapes, out_specs, aliases = [], [], {}
    for key, value in list(outs.items()) + list(grow.items()) + [("token", far(8, 128))]:
        old, shape = value if key in grow else (None, value)
        space = pl.ANY if isinstance(shape, jax.ShapeDtypeStruct) else shape.memory_space
        where[key] = -1 - len(shapes)
        if old is not None:
            aliases[len(args)] = len(shapes)
            args.append(old if space is pl.ANY else pltpu.with_memory_space_constraint(old, space))
            specs.append(pl.BlockSpec(memory_space=space))
        shapes.append(shape)
        out_specs.append(pl.BlockSpec(memory_space=space))
    first_out, first_scratch = len(args), len(args) + len(shapes)
    kept = dict(scratch)

    def kernel(*refs):
        k = SimpleNamespace()
        pick = lambda i: refs[i] if i >= 0 else refs[first_out - 1 - i]
        for key, at in where.items():
            setattr(k, key, [pick(i) for i in at] if isinstance(at, list) else pick(at))
        for i, key in enumerate(kept):
            setattr(k, key, refs[first_scratch + i])
        k.load, k.store = Copies(refs[-2]), Copies(refs[-1])
        if active is None:
            body(k)
        else:
            pl.when(k.section[0] == active)(lambda: body(k))

    res = pl.pallas_call(
        kernel,
        out_shape=shapes,
        in_specs=specs,
        out_specs=out_specs,
        scratch_shapes=list(kept.values()) + [pltpu.SemaphoreType.DMA((copies,))] * 2,
        input_output_aliases=aliases,
        compiler_params=pltpu.CompilerParams(vmem_limit_bytes=16 * MIB),
        cost_estimate=pl.CostEstimate(flops=int(micros * 1.15e9), bytes_accessed=0, transcendentals=0),
        name=name,
    )(*args)
    return SimpleNamespace(**{key: res[-1 - at] for key, at in where.items() if not isinstance(at, list) and at < 0})


def prepare(w1, w2, ends=None, here=None, count=0, W=0, after=()):
    F = w1.shape[1]

    def body(k):
        c2 = k.load(k.w2, k.b2)
        parts = [pl.ds(i, F) for i in range(0, w1.shape[0], F)]
        c1 = [k.load(k.w1.at[part], k.b1.at[part]) for part in parts]
        ce = [k.load(src, ref) for src, ref in zip(k.ends, (k.e0, k.e1))] if ends is not None else []
        c2.wait()
        k.h2[...], k.l2[...] = split(k.b2[...])
        for part, c in zip(parts, c1):
            c.wait()
            k.h1[part], k.l1[part] = split(k.b1[part])
        if ends is not None:
            wait(*ce)
            hots = []
            for ref in (k.e0, k.e1):
                total = count * (W // 3)
                at = ref[...] - (k.node[0] - 1) * (W // 3)
                at = jnp.where(at < 0, at + total, at)
                at = jnp.where(at >= total, at - total, at)
                hots.append((lax.broadcasted_iota(jnp.int32, (W, at.shape[1]), 0) == at).astype(f32).astype(bf16))
            both = jnp.concatenate(hots, axis=0)
            k.gather[...] = jnp.concatenate([both, both], axis=0)
            k.scatter[...] = jnp.concatenate([both, both], axis=1)

    half = lambda *s: near(*s, dtype=bf16)
    outs = dict(h1=half(*w1.shape), l1=half(*w1.shape), h2=half(*w2.shape), l2=half(*w2.shape))
    scalars, hbm = {}, dict(w1=w1, w2=w2)
    scratch = dict(b1=pltpu.VMEM(w1.shape, f32), b2=pltpu.VMEM(w2.shape, f32))
    if ends is not None:
        rows = ends[0].shape[1]
        outs.update(gather=half(4 * W, rows), scatter=half(2 * W, 2 * rows))
        scalars = here
        hbm.update(ends=list(ends))
        scratch.update(e0=pltpu.VMEM((1, rows), jnp.int32), e1=pltpu.VMEM((1, rows), jnp.int32))
    r = call(body, "prepare", scalars, hbm, outs=outs, scratch=scratch, after=after)
    resident.extend([r.h1, r.l1, r.h2, r.l2])
    if ends is not None:
        resident.extend([r.gather, r.scatter])
    return r, dict(w1=[r.h1, r.l1], w2=[r.h2, r.l2])


def side_rows(par, nr):
    return pl.multiple_of((1 - par) * 2 * nr, 16), pl.multiple_of(par * 2 * nr, 16)


def window_parts(k, ref, nr):
    a_at, b_at = side_rows(k.node[0] % 2, nr)
    return [ref.at[:, pl.ds(a_at, nr), :], ref.at[:, nr:2 * nr, :], ref.at[:, pl.ds(b_at, nr), :]]


def load_weights(k, weights):
    return [k.load(k.weights[0], k.lengths), k.load(k.weights[1], k.mask)] if weights else []


def weight_scratch(weights):
    return dict(lengths=pltpu.SMEM(weights[0].shape, jnp.int32), mask=pltpu.SMEM(weights[1].shape, jnp.int32)) if weights else {}


def sample_weight(k, sample):
    m, t = divmod(sample, k.mask.shape[0])
    return jnp.where(t < k.lengths[m], k.mask[t, m], 0).astype(f32)


def load_views(k, views, refs, targets, g):
    return [k.load(ref.at[pl.ds(view[1], g)], target) for view, ref, target in zip(views, refs, targets)]


def arrays(views):
    return [v[0] for v in views]


def chunk(g):
    return 2 if g % 2 == 0 else 1


def edge_forward(g, active, here, e, v, n, hot, w, vec, act, box, relay, after, micros):
    rows, F = e[0][0].shape[1:]
    nr = v[0][0].shape[1]
    W = 3 * nr
    cs, part_size = g, chunk(g)

    def body(k):
        load, store = k.load, k.store
        cv = load_views(k, v, k.v, window_parts(k, k.vb, nr), g)
        ce = load_views(k, e, k.e, [k.eb.at[pl.ds(s, part_size)] for s in range(0, g, part_size)], part_size)
        (w1h, w1l), (w2h, w2l), vec = k.w1, k.w2, k.vec
        wait(*cv)
        vw = split(k.vb[...].reshape(g * W, F))
        for i in (0, 1):
            part = pl.ds((i + 1) * F, F)
            h, l = split(dot3(vw, (w1h[part], w1l[part]), NN).reshape(g, W, F))
            k.pp[:, i * W:(i + 1) * W] = h
            k.pp[:, (i + 2) * W:(i + 3) * W] = l
        for s in range(0, g, cs):
            wait(*ce)
            to = pl.ds(s, cs)
            x = k.eb[to].reshape(cs * rows, F)
            a = dot3(split(x), (w1h[0:F], w1l[0:F]), NN) + vec[0:1]
            a = a + jnp.concatenate([dot1(k.gather[...], k.pp[s + t], TN) for t in range(cs)], axis=0)
            k.out_a[to] = a.reshape(cs, rows, F)
            h = a / (1 + jnp.exp(-a))
            n_, r = normalized(dot3(split(h), (w2h[...], w2l[...]), NN) + vec[1:2])
            k.out_n[to] = n_.reshape(cs, rows, F)
            k.out_r[to] = jnp.broadcast_to(r, (cs * rows, 128)).reshape(cs, rows, 128)
            m = n_ * vec[2:3] + vec[3:4]
            k.ob[to] = (x + m).reshape(cs, rows, F)
            done = 0
            for key, size in zip(names, relay):
                store(k.ob.at[pl.ds(done, size)], getattr(k, key))
                done += size
            for t in range(g):
                store(k.ob.at[t], k.act.at[n + t])
            mh, ml = split(m.reshape(cs, rows, F))
            for t in range(cs):
                k.sb[s + t] = dot1(k.scatter[W:], jnp.concatenate([mh[t], ml[t]], axis=0), NN)
        sides = window_parts(k, k.sb, nr)
        store(sides[0], k.box_a.at[pl.ds(box[2], g)])
        store(sides[1], k.own)
        store(sides[2], k.box_b.at[pl.ds(box[2], g)])
        store.wait()

    outs = dict(out_a=near(g, rows, F), out_n=near(g, rows, F), out_r=near(g, rows, 128), own=far(g, nr, F))
    names = "abcd"[:len(relay)]
    outs.update({key: far(size, rows, F) for key, size in zip(names, relay)})
    old = box[0] or (None, None)
    grow = dict(act=(act[0], far(act[1], rows, F)), box_a=(old[0], far(box[1], nr, F)), box_b=(old[1], far(box[1], nr, F)))
    full = pltpu.VMEM((g, rows, F), f32)
    scratch = dict(eb=full, ob=full, vb=pltpu.VMEM((g, W, F), f32), sb=pltpu.VMEM((g, W, F), f32), pp=pltpu.VMEM((g, 4 * W, F), bf16))
    r = call(body, "edge_forward", here, active=active, vmem=dict(**w, gather=hot.gather, scatter=hot.scatter, vec=vec), free=dict(e=arrays(e), v=arrays(v)), outs=outs, grow=grow, scratch=scratch, after=after, micros=micros)
    r.relay = [getattr(r, key) for key in names]
    return r


def node_stage(g, forward, backward, active, here, v, n, w, vec, parts, act=None, stash=None, weights=None, cot=None, box=None, after=(), micros=2):
    nr, F = v[0].shape[1:]
    R = g * nr

    def body(k):
        load, store = k.load, k.store
        cx = [load(k.v.at[pl.ds(v[1], g)], k.zb.at[:, :, 0:F])] + load_views(k, parts, k.parts, [k.pb.at[i] for i in range(len(parts))], g)
        if forward and backward:
            cx.append(load(k.cot.at[pl.ds(n, g)], k.gb))
            cx += load_weights(k, weights)
        w1, w2, vec = (k.w1[0][...], k.w1[1][...]), (k.w2[0][...], k.w2[1][...]), k.vec
        wait(*cx)
        given = sum([k.pb[i] for i in range(1, len(parts))], k.pb[0])
        k.zb[:, :, F:] = given if forward else k.gathered[...]
        z = k.zb[...].reshape(R, 2 * F)
        zs = split(z)
        if forward:
            a = dot3_few(zs, w1, NN) + vec[0:1]
            h = a / (1 + jnp.exp(-a))
            n_, r = normalized(dot3_few(split(h), w2, NN) + vec[1:2])
            k.ob[...] = (z[:, :F] + n_ * vec[2:3] + vec[3:4]).reshape(g, nr, F)
            if not backward:
                store(k.ob, k.out_v)
                k.out_a[...] = a.reshape(g, nr, F)
                k.out_n[...] = n_.reshape(g, nr, F)
                k.out_r[...] = jnp.broadcast_to(r, (R, 128)).reshape(g, nr, 128)
                k.out_g[...] = given
            store(k.ob, k.act.at[pl.ds(n, g)])
        else:
            a, n_, r = k.a[...].reshape(R, F), k.n[...].reshape(R, F), k.r[...].reshape(R, 128)[:, 0:1]
        if backward:
            if forward:
                for s in range(g):
                    k.gb[s] = k.gb[s] * sample_weight(k, n + s)
                gu = k.gb[...].reshape(R, F)
            else:
                gu = given.reshape(R, F)
            gp = norm_back(gu, n_, r, vec[2:3])
            q = 1 / (1 + jnp.exp(-a))
            hs, gps = split(a * q), split(gp)
            ga = dot3_few(gps, w2, NT) * (q * (1 + a * (1 - q)))
            gas = split(ga)
            gz = dot3_few(gas, w1, NT)
            k.ggb[...] = gz[:, F:].reshape(g, nr, F)
            for ref in (k.box_a, k.box_b):
                store(k.ggb, ref.at[pl.ds(box[2], g)])
            k.own[...] = k.ggb[...]
            k.out_gv[...] = (gu + gz[:, :F]).reshape(g, nr, F)
            for i, x in enumerate((zs[0][:, :F], zs[1][:, :F], zs[0][:, F:], zs[1][:, F:], hs[0], hs[1], gas[0], gas[1], gps[0], gps[1])):
                k.ops[i] = x
            k.dv[...] = column_sums(ga, gp, gu * n_, gu)
        store.wait()

    hbm, vmem, free = {}, dict(**w, vec=vec), dict(v=v[0], parts=arrays(parts))
    shape = near(g, nr, F)
    outs, grow = {}, {}
    if not forward:
        vmem.update(a=stash.out_a, n=stash.out_n, r=stash.out_r, gathered=stash.out_g)
    elif backward:
        hbm.update(cot=cot, weights=weights)
    if forward:
        grow.update(act=(act[0], far(act[1], nr, F)))
        if not backward:
            outs.update(out_v=far(g, nr, F), out_a=shape, out_n=shape, out_r=near(g, nr, 128), out_g=shape)
    if backward:
        old = box[0] or (None, None)
        outs.update(own=shape, out_gv=shape, ops=near(10, R, F, dtype=bf16), dv=near(8, F))
        grow.update(box_a=(old[0], far(box[1], nr, F)), box_b=(old[1], far(box[1], nr, F)))
    small = pltpu.VMEM((g, nr, F), f32)
    scratch = dict(zb=pltpu.VMEM((g, nr, 2 * F), f32), pb=pltpu.VMEM((len(parts), g, nr, F), f32), gb=small, ob=small, ggb=small, **weight_scratch(weights))
    return call(body, "node_stage", here, hbm, vmem, free, active=active, outs=outs, grow=grow, scratch=scratch, after=after, micros=micros)


def node_weights(active, here, m, acc, first, after):
    _, R, F = m.ops.shape

    def body(k):
        o = k.ops
        for i, (x, y) in enumerate(((0, 6), (2, 6), (4, 8))):
            part = pl.ds(i * F, F)
            d = dot3((o[x], o[x + 1]), (o[y], o[y + 1]), TN)
            k.total[part] = d if first else k.total[part] + d

    grow = dict(total=(acc and acc.total, near(3 * F, F)))
    return call(body, "node_weights", here, active=active, vmem=dict(ops=m.ops), grow=grow, after=after, micros=0.01)


def edge_backward(g, active, here, weights, ge, gg, n, stash, gv, hot, w, vec, box, after, micros):
    rows, F = ge[0].shape[1:]
    nr = gv.shape[1]
    W = 3 * nr
    cs = g

    def body(k):
        load, store = k.load, k.store
        gg_at = window_parts(k, k.ggb, nr)
        cg = load_views(k, (gg[0], gg[2]), k.gg, (gg_at[0], gg_at[2]), g)
        cx = [load(k.ge.at[ge[1] + s], k.gb.at[s]) for s in range(g)]
        cx += load_weights(k, weights)
        k.ggb[:, nr:2 * nr] = k.gg_own[...]
        (w1h, w1l), (w2h, w2l), vec = k.w1, k.w2, k.vec
        wait(*cg)
        h, l = split(k.ggb[...])
        k.gg2[:, 0:W] = h
        k.gg2[:, W:] = l
        flat = lambda x: x.reshape(cs * rows, x.shape[-1])
        sums = []
        for s in range(0, g, cs):
            to = pl.ds(s, cs)
            wait(*cx)
            if weights:
                for t in range(s, s + cs):
                    k.gb[t] = k.gb[t] * sample_weight(k, n + t)
            hot_r = k.gather[pl.ds(W, W)]
            gu = flat(k.gb[to]) + jnp.concatenate([dot1(hot_r, k.gg2[s + t, 0:W], TN) + dot1(hot_r, k.gg2[s + t, W:], TN) for t in range(cs)], axis=0)
            n_, a = flat(k.n[to]), flat(k.a[to])
            gp = norm_back(gu, n_, flat(k.r[to])[:, 0:1], vec[2:3])
            gps = split(gp)
            q = 1 / (1 + jnp.exp(-a))
            ga = dot3(gps, (w2h[...], w2l[...]), NT) * (q * (1 + a * (1 - q)))
            gas = split(ga)
            for i, x in enumerate((*split(a * q), *gps, *gas)):
                k.ops[i, pl.ds(s * rows, cs * rows)] = x
            for t in range(cs):
                both = jnp.concatenate([x[t * rows:(t + 1) * rows] for x in gas], axis=0)
                k.ssb[s + t] = dot1(k.scatter[...], both, NN)
            sums.append(column_sums(ga, gp, gu * n_, gu))
        ss = split(k.ssb[:, 0:W].reshape(g * W, F))
        sr = split(k.ssb[:, W:].reshape(g * W, F))
        for i, x in enumerate((*ss, *sr)):
            k.sops[i] = x
        wg = dot3(ss, (w1h[F:2 * F], w1l[F:2 * F]), NT) + dot3(sr, (w1h[2 * F:], w1l[2 * F:]), NT)
        k.wgb[...] = wg.reshape(g, W, F)
        k.wgb[:, nr:2 * nr] += k.gv[...]
        sides = window_parts(k, k.wgb, nr)
        store(sides[0], k.box_a.at[pl.ds(box[2], g)])
        store(sides[2], k.box_b.at[pl.ds(box[2], g)])
        k.own[...] = k.wgb[:, nr:2 * nr]
        k.dv[...] = sum(sums[1:], sums[0])
        store.wait()

    free = dict(ge=ge[0], gg=[gg[0][0], gg[2][0]])
    vmem = dict(**w, vec=vec, a=stash.out_a, n=stash.out_n, r=stash.out_r, gv=gv, gg_own=gg[1], gather=hot.gather, scatter=hot.scatter)
    old = box[0] or (None, None)
    outs = dict(own=near(g, nr, F), ops=near(6, g * rows, F, dtype=bf16), sops=near(4, g * W, F, dtype=bf16), dv=near(8, F))
    grow = dict(box_a=(old[0], far(box[1], nr, F)), box_b=(old[1], far(box[1], nr, F)))
    scratch = dict(gb=pltpu.VMEM((g, rows, F), f32), ggb=pltpu.VMEM((g, W, F), f32), gg2=pltpu.VMEM((g, 2 * W, F), bf16), ssb=pltpu.VMEM((g, 2 * W, F), f32), wgb=pltpu.VMEM((g, W, F), f32), **weight_scratch(weights))
    return call(body, "edge_backward", here, dict(weights=weights) if weights else {}, active=active, vmem=vmem, free=free, outs=outs, grow=grow, scratch=scratch, after=after, micros=micros)


def add_parts(active, here, views, own, n, grad, relay, after):
    g, (nr, F) = sum(x.shape[0] for x in own), own[0].shape[1:]

    def body(k):
        wait(*load_views(k, views, k.views, [k.pb.at[i] for i in (0, 1)], g))
        done = 0
        for x in k.own:
            to = pl.ds(done, x.shape[0])
            k.pb[0, to] = k.pb[0, to] + k.pb[1, to] + x[...]
            done += x.shape[0]
        if relay:
            k.store(k.pb.at[0], k.out)
        k.store(k.pb.at[0], k.grad.at[pl.ds(n, g)])
        k.store.wait()

    outs = dict(out=far(g, nr, F)) if relay else {}
    grow = dict(grad=(grad[0], far(grad[1], nr, F)))
    return call(body, "add_parts", here, active=active, vmem=dict(own=own), free=dict(views=arrays(views)), outs=outs, grow=grow, scratch=dict(pb=pltpu.VMEM((2, g, nr, F), f32)), after=after, micros=0.01)


def edge_out(g, active, here, weights, ge, n, ops, w, grad, relay, after, micros):
    rows, F = ge[0].shape[1:]
    halves = (0, 1) if g % 2 == 0 else (0,)
    m = g // len(halves)

    def body(k):
        cs = [k.load(k.ge.at[pl.ds(ge[1] + i * m, m)], k.gb.at[pl.ds(i * m, m)]) for i in halves]
        cw = load_weights(k, weights)
        w1h, w1l = k.w1
        for i in halves:
            own = dot3([k.ops[x, pl.ds(i * m * rows, m * rows)] for x in (4, 5)], (w1h[0:F], w1l[0:F]), NT)
            cs[i].wait()
            if i == 0:
                wait(*cw)
            if weights:
                for t in range(i * m, (i + 1) * m):
                    k.gb[t] = k.gb[t] * sample_weight(k, n + t)
            to = pl.ds(i * m, m)
            k.gb[to] = k.gb[to] + own.reshape(m, rows, F)
            if relay:
                k.store(k.gb.at[to], k.out_ge.at[to])
            k.store(k.gb.at[to], k.grad.at[pl.ds(n + i * m, m)])
        k.store.wait()

    outs = dict(out_ge=far(g, rows, F)) if relay else {}
    grow = dict(grad=(grad[0], far(grad[1], rows, F)))
    return call(body, "edge_out", here, dict(weights=weights) if weights else {}, active=active, vmem=dict(ops=ops, w1=w["w1"]), free=dict(ge=ge[0]), outs=outs, grow=grow, scratch=dict(gb=pltpu.VMEM((g, rows, F), f32), **weight_scratch(weights)), after=after, micros=micros)


def edge_weights(g, active, here, b, node_dv, e, v, pad, acc, first, after, micros):
    rows, F = e[0][0].shape[1:]
    nr = v[0][0].shape[1]
    W = 3 * nr

    def body(k):
        cs = chunk(g)
        ce = load_views(k, e, k.e, [k.eb.at[pl.ds(s, cs)] for s in range(0, g, cs)], cs)
        cv = load_views(k, v, k.v, window_parts(k, k.vb, nr), g)
        o = k.ops

        def put(total, i, x, y):
            part = pl.ds(i * F, F)
            d = dot3(x, y, TN)
            total[part] = d if first else total[part] + d

        put(k.total, 3, (o[0], o[1]), (o[2], o[3]))
        if first:
            k.total[4 * F:] = jnp.zeros((pad, F), f32)
        k.total[4 * F:4 * F + 8] += k.dv[...]
        if node_dv:
            k.total[4 * F + 8:4 * F + 16] = sum([x[...] for x in k.node_dv[1:]], k.node_dv[0][...])
        wait(*cv)
        vs = split(k.vb[...].reshape(g * W, F))
        for i in (0, 1):
            put(k.total, i + 1, vs, (k.sops[2 * i], k.sops[2 * i + 1]))
        wait(*ce)
        put(k.total, 0, split(k.eb[...].reshape(g * rows, F)), (o[4], o[5]))

    vmem = dict(ops=b.ops, sops=b.sops, dv=b.dv)
    if node_dv:
        vmem.update(node_dv=node_dv)
    grow = dict(total=(acc and acc.total, near(4 * F + pad, F)))
    scratch = dict(eb=pltpu.VMEM((g, rows, F), f32), vb=pltpu.VMEM((g, W, F), f32))
    return call(body, "edge_weights", here, active=active, vmem=vmem, free=dict(e=arrays(e), v=arrays(v)), grow=grow, scratch=scratch, after=after, micros=micros)


def gate(after, *xs, make=far, micros=0.01):
    return call(lambda k: None, "gate", grow={name: (x, make(*x.shape)) for name, x in zip("xyzuvw", xs)}, after=after, micros=micros)


class Total:
    def __init__(self, x, here, orders, cuts, vecs=False):
        self.vecs = vecs
        count = lax.axis_size("node")
        self.here, self.orders = here, orders
        self.swaps = [[(i, i ^ (1 << (y if i % 2 else x))) for i in range(count)] for x, y in zip(*orders)]
        self.x, self.cuts = x, cuts
        self.rows, self.F = x.shape
        self.sizes, rows = [], self.rows
        while len(self.sizes) < len(self.swaps) and rows % 16 == 0:
            rows //= 2
            self.sizes.append(rows)
        self.got, self.result, self.token, self.done = [], None, None, False
        self.steps = self.run()

    def flag(self, ref, step):
        x, y = (order[step] for order in self.orders)
        node = ref.node[0]
        return jnp.where(node % 2 == 1, node >> y, node >> x) & 1

    def partial(self, k):
        K, sizes = len(self.sizes), self.sizes
        size = sizes[min(k, K - 1)]

        def body(ref):
            def start(after):
                at = sum(self.flag(ref, m) * sizes[m] for m in range(after + 1, k)) if after + 1 < k else 0
                if k < K:
                    at = at + (1 - self.flag(ref, k)) * size
                return pl.multiple_of(at, 8)

            total = ref.x[pl.ds(start(-1), size)]
            for j, x in enumerate(ref.got):
                total = total + x[pl.ds(start(j), size)]
            ref.out[...] = total

        r = call(body, "partial_sum", self.here, vmem=dict(x=self.x, got=self.got[:k]), outs=dict(out=near(size, self.F)), after=self.after, micros=50)
        self.token = (r.token,)
        return r.out

    def add(self, x, y):
        def body(k):
            k.out[...] = k.x[...] + k.y[...]

        r = call(body, "add", self.here, vmem=dict(x=x, y=y), outs=dict(out=near(*x.shape)), after=self.after, micros=50)
        self.token = (r.token,)
        return r.out

    def join(self, own, got, step):
        R = own.shape[0]

        def body(k):
            bit = self.flag(k, step)
            k.joined[pl.ds(pl.multiple_of(bit * R, 8), R)] = k.own[...]
            k.joined[pl.ds(pl.multiple_of((1 - bit) * R, 8), R)] = k.got[...]

        r = call(body, "join", self.here, vmem=dict(own=own, got=got), outs=dict(joined=near(2 * R, self.F)), after=self.after, micros=50)
        self.token = (r.token,)
        return r.joined

    def finish(self, own, got):
        R = own.shape[0]
        names = "abcdef"[:len(self.cuts)]

        def put(k, low, high):
            done = 0
            for key, rows in zip(names, self.cuts):
                for src, at in ((low, 0), (high, R)):
                    a, b = max(at, done), min(at + R, done + rows)
                    for i in range(a, b, 256):
                        size = min(256, b - i)
                        k.store(src.at[pl.ds(i - at, size)], getattr(k, key).at[pl.ds(i - done, size)])
                done += rows
            if self.vecs:
                assert done >= R
                k.va[...] = high[done - R:done - R + 4]
                k.vb[...] = high[done - R + 8:done - R + 12]
                k.store(k.va, k.first)
                k.store(k.vb, k.second)
            k.store.wait()

        def body(k):
            bit = self.flag(k, 0)
            pl.when(bit == 0)(lambda: put(k, k.own, k.got))
            k.store.all = []
            pl.when(bit == 1)(lambda: put(k, k.got, k.own))

        outs = {key: far(rows, self.F) for key, rows in zip(names, self.cuts)}
        scratch = {}
        if self.vecs:
            outs.update(first=far(4, self.F), second=far(4, self.F))
            scratch.update(va=pltpu.VMEM((4, self.F), f32), vb=pltpu.VMEM((4, self.F), f32))
        r = call(body, "finish", self.here, vmem=dict(own=own, got=got), outs=outs, scratch=scratch, after=self.after, micros=50)
        self.token = (r.token,)
        return [getattr(r, key) for key in outs]

    def run(self):
        K = len(self.sizes)
        for k in range(K):
            send = self.partial(k)
            self.got.append(lax.ppermute(send, "node", self.swaps[k]))
            yield
        own = self.partial(K)
        for pairs in self.swaps[K:]:
            got = lax.ppermute(own, "node", pairs)
            yield
            own = self.add(own, got)
        for k in reversed(range(K)):
            got = lax.ppermute(own, "node", self.swaps[k])
            yield
            if k:
                own = self.join(own, got, k)
            else:
                self.result = self.finish(own, got)
        self.done = True

    def step(self, after):
        if self.done:
            return after
        self.after = after
        next(self.steps, None)
        return self.token


def on_device(in_nodes, in_edges, senders, receivers, edge_w1, edge_w2, edge_vec, node_w1, node_w2, node_vec, cot_nodes, cot_edges, lengths, step_mask):
    samples, nr, F = in_nodes.shape
    count = lax.axis_size("node")
    section, node = lax.axis_index("section"), lax.axis_index("node")
    evec, nvec = edge_vec[0], node_vec[0]
    here = dict(section=section.astype(jnp.int32).reshape(1), node=node.astype(jnp.int32).reshape(1))
    live = [lengths, step_mask.T]

    def partner(i, side):
        return i ^ 1 if side == 0 else (i - 1 + 2 * (i % 2)) % count

    def swap(x, side, planes):
        if planes is None:
            return lax.ppermute(x, "node", [(i, partner(i, side)) for i in range(count)])
        return lax.ppermute(x, ("section", "node"), [(s * count + i, s * count + partner(i, side)) for s in planes for i in range(count)])

    def beside(to_a, to_b, planes=None):
        return swap(to_a, 0, planes), swap(to_b, 1, planes)

    def across(x, source, side=None):
        if side is None:
            return lax.ppermute(x, "section", [(source, 1 - source)])
        return lax.ppermute(x, ("section", "node"), [(source * count + i, (1 - source) * count + partner(i, side)) for i in range(count)])

    p, q = [(sum(group_sizes[:i]), n) for i, n in enumerate(group_sizes)]
    both = p[1] + q[1]
    pad = 8 * count
    act_e = act_n = acc_n = acc_e = grad_e = grad_n = None
    after = ()

    def done(r):
        nonlocal after
        after = (r.token,)
        return r

    def stay(r, *names):
        r.kept = [getattr(r, name) for name in names]
        resident.extend(r.kept)
        return r

    def leave(*rs):
        for r in rs:
            resident[:] = [x for x in resident if all(x is not y for y in r.kept)]

    resident.clear()
    from_a, from_b = beside(in_nodes, in_nodes)
    hot, ew = prepare(edge_w1[0], edge_w2[0], (senders.reshape(1, -1), receivers.reshape(1, -1)), here, count, 3 * nr)

    def forward_0(c, relay):
        nonlocal act_e
        v = [(x, c[0]) for x in (from_a, in_nodes, from_b)]
        e = [(in_edges, c[0] + s) for s in range(0, c[1], chunk(c[1]))]
        f = done(edge_forward(c[1], 0, here, e, v, c[0], hot, ew, evec, (act_e, samples), (None, c[1], 0), relay, after, 0.01))
        act_e, f.v, f.e = f.act, v, e
        return stay(f, "out_a", "out_n", "out_r")

    def nodes_0(c, f, got):
        nonlocal act_n
        m = done(node_stage(c[1], True, False, 0, here, (in_nodes, c[0]), c[0], nw, nvec, [(got[0], 0), (f.own, 0), (got[1], 0)], act=(act_n, samples), after=after, micros=0.01))
        act_n = m.act
        return stay(m, "out_a", "out_n", "out_r", "out_g")

    def forward_1(c, e, nodes, box):
        nonlocal act_e
        v, e = [(x, 0) for x in nodes], [(x, s) for x in e for s in range(0, x.shape[0], chunk(c[1]))]
        f = done(edge_forward(c[1], 1, here, e, v, c[0], hot, ew, evec, (act_e, samples), box, (), after, 0.01))
        act_e, f.v, f.e = f.act, v, e
        return stay(f, "out_a", "out_n", "out_r")

    def middle_1(c, f, got, at, box):
        nonlocal act_n
        m = done(node_stage(c[1], True, True, 1, here, f.v[1], c[0], nw, nvec, [(got[0], at), (f.own, 0), (got[1], at)], act=(act_n, samples), weights=live, cot=cot_nodes, box=box, after=after, micros=0.01))
        act_n = m.act
        return stay(m, "ops", "dv", "own", "out_gv")

    def backward_1(c, f, m, got, at, box):
        b = done(edge_backward(c[1], 1, here, live, (cot_edges, c[0]), ((got[0], at), m.own, (got[1], at)), c[0], f, m.out_gv, hot, ew, evec, box, after, 0.01))
        leave(f)
        return stay(b, "ops", "sops", "dv", "own")

    def add_1(c, b, got, at):
        nonlocal grad_n
        r = done(add_parts(1, here, [(x, at) for x in got], [b.own], c[0], (grad_n, samples), True, after))
        grad_n = r.grad
        return r.out

    def out_1(c, b):
        nonlocal grad_e
        r = done(edge_out(c[1], 1, here, live, (cot_edges, c[0]), c[0], b.ops, ew, (grad_e, samples), True, after, 0.01))
        grad_e = r.grad
        return r.out_ge

    def middle_0(c, gv, stash):
        m = done(node_stage(c[1], False, True, 0, here, (in_nodes, c[0]), c[0], nw, nvec, [(gv, 0)], stash=stash, box=(None, c[1], 0), after=after, micros=50))
        m.got = beside(m.box_a, m.box_b, (0,))
        leave(stash)
        return stay(m, "ops", "dv", "own", "out_gv")

    def backward_0(c, ge, f, m, box):
        b = done(edge_backward(c[1], 0, here, None, (ge, 0), ((m.got[0], 0), m.own, (m.got[1], 0)), c[0], f, m.out_gv, hot, ew, evec, box, after, 50))
        leave(f)
        return stay(b, "ops", "sops", "dv", "own")

    def out_0(c, ge, b):
        nonlocal grad_e
        grad_e = done(edge_out(c[1], 0, here, None, (ge, 0), c[0], b.ops, ew, (grad_e, samples), False, after, 2)).grad

    def node_grads(on, m, first):
        nonlocal acc_n
        acc_n = done(node_weights(on, here, m, acc_n, first, after))
        leave(m)

    def edge_grads(on, c, b, f, first, node_dv=()):
        nonlocal acc_e
        acc_e = done(edge_weights(c[1], on, here, b, list(node_dv), f.e, f.v, pad, acc_e, first, after, 2))
        leave(b)

    f0p = forward_0(p, relay_sizes[0])
    got = beside(f0p.box_a, f0p.box_b)
    e0 = [across(f0p.relay[0], 0)]
    _, nw = prepare(node_w1[0], node_w2[0], after=after)
    n0p = nodes_0(p, f0p, got)
    v0, y = across(n0p.out_v, 0), across(n0p.out_v, 0, 1)
    held = done(gate(after, *f0p.relay[1:]))
    first = (v0, y) + tuple(e0)
    e0 += [across(getattr(held, key), 0) for key, _ in zip("xyz", f0p.relay[1:])]
    f0q = forward_0(q, relay_sizes[1])
    v0 = (swap(v0, 0, (1,)), v0, y)
    held = done(gate(after + first, f0q.box_a, f0q.box_b, *f0q.relay, micros=50))
    e1 = [across(getattr(held, key), 0) for key, _ in zip("zuvw", f0q.relay)]
    got_q = beside(held.x, held.y, (0,))
    f1p = forward_1(p, e0, v0, (None, p[1], 0))
    got = beside(f1p.box_a, f1p.box_b)
    n0q = nodes_0(q, f0q, got_q)
    v1, y = across(n0q.out_v, 0), across(n0q.out_v, 0, 1)
    n1p = middle_1(p, f1p, got, 0, (None, p[1], 0))
    got_p = beside(n1p.box_a, n1p.box_b)
    b1p = backward_1(p, f1p, n1p, got_p, 0, (None, p[1], 0))
    got_p = beside(b1p.box_a, b1p.box_b)
    v1 = done(gate(after, v1, make=loose)).x
    f1q = forward_1(q, e1, (swap(v1, 0, None), v1, y), (None, q[1], 0))
    got_q = beside(f1q.box_a, f1q.box_b)
    ge0 = across(out_1(p, b1p), 1)
    gv0 = across(add_1(p, b1p, got_p, 0), 1)
    n1q = middle_1(q, f1q, got_q, 0, (None, q[1], 0))
    got_q = beside(n1q.box_a, n1q.box_b)
    m0p = middle_0(p, gv0, n0p)
    node_grads(1, n1p, True)
    b1q = backward_1(q, f1q, n1q, got_q, 0, (None, q[1], 0))
    got_q = beside(b1q.box_a, b1q.box_b)
    ge1 = out_1(q, b1q)
    gv1 = across(add_1(q, b1q, got_q, 0), 1)
    ge1 = across(done(gate(after, ge1)).x, 1)
    node_grads(1, n1q, False)
    edge_grads(1, p, b1p, f1p, True)
    edge_grads(1, q, b1q, f1q, False, (n1p.dv, n1q.dv))
    b0p = backward_0(p, ge0, f0p, m0p, (None, both, 0))
    m0q = middle_0(q, gv1, n0q)
    edge_grads(0, p, b0p, f0p, True)
    node_grads(0, m0p, True)
    node_grads(0, m0q, False)
    b0q = backward_0(q, ge1, f0q, m0q, ((b0p.box_a, b0p.box_b), both, p[1]))
    got = beside(b0q.box_a, b0q.box_b)
    edge_grads(0, q, b0q, f0q, False, (m0p.dv, m0q.dv))
    bits = list(range(count.bit_length() - 1))
    yzz, zyz, yzz_turned = [[0] + [bits[i] for i in order] + bits[4:] for order in ((1, 2, 3), (2, 1, 3), (1, 3, 2))]
    total_e = Total(acc_e.total, here, (yzz_turned, zyz), (3 * F, F), True)
    after = total_e.step(after)
    total_n = Total(acc_n.total, here, (yzz, zyz), (2 * F, F))
    totals = [total_e, total_n]
    after = total_n.step(after)
    for turn in range(2 * len(bits)):
        for t in totals:
            after = t.step(after)
        if turn == 0:
            out_0(p, ge0, b0p)
            out_0(q, ge1, b0q)
        if turn == 4:
            grad_n = done(add_parts(0, here, [(x, 0) for x in got], [b0p.own, b0q.own], 0, (grad_n, samples), False, after)).grad
    edge_1, edge_2, edge_v, node_v = total_e.result
    node_1, node_2 = total_n.result
    return (
        act_n[None], act_e[None], grad_n[None], grad_e[None],
        edge_1[None], edge_2[None], edge_v[None], node_1[None], node_2[None], node_v[None],
    )


def solution(mesh):
    nodes, rows, weights = P(None, "node", None), P("node"), P("section", None, None)
    stacked = P("section", None, "node", None)
    in_specs = (nodes, nodes, rows, rows) + (weights,) * 6 + (nodes, nodes, P(), P())
    out_specs = (stacked,) * 4 + (weights,) * 6
    return jax.shard_map(on_device, mesh=mesh, in_specs=in_specs, out_specs=out_specs, check_vma=False)
```

```python
from types import SimpleNamespace

import jax
import jax.numpy as jnp
from jax import lax
from jax.experimental import pallas as pl
from jax.experimental.pallas import tpu as pltpu
from jax.sharding import PartitionSpec as P

f32, bf16 = jnp.float32, jnp.bfloat16
norm_eps = 1e-05
NN = ((1,), (0,))
NT = ((1,), (1,))
TN = ((0,), (0,))
group_sizes = (4, 4)
relay_sizes = ((2, 2), (2, 2))
MIB = 1024 * 1024


def split(x):
    hi = x.astype(bf16)
    return hi, (x - hi.astype(f32)).astype(bf16)


def dot1(a, b, dims):
    return lax.dot_general(a, b, (dims, ((), ())), preferred_element_type=f32)


def dot3(a, b, dims):
    return dot1(a[0], b[0], dims) + (dot1(a[0], b[1], dims) + dot1(a[1], b[0], dims))


def dot3_few(a, b, dims):
    rows = a[0].shape[0]
    both = dot1(jnp.concatenate(a, axis=0), b[0], dims)
    return both[:rows] + (both[rows:] + dot1(a[0], b[1], dims))


def normalized(u):
    c = u - jnp.mean(u, axis=-1, keepdims=True)
    r = lax.rsqrt(jnp.mean(c * c, axis=-1, keepdims=True) + norm_eps)
    return c * r, r


def norm_back(gu, n, r, gain):
    t = gu * gain
    return r * (t - jnp.mean(t, axis=-1, keepdims=True) - n * jnp.mean(t * n, axis=-1, keepdims=True))


def column_sums(*xs):
    F = xs[0].shape[-1]
    return jnp.concatenate([jnp.sum(x, axis=0, keepdims=True) for x in xs] + [jnp.zeros((8 - len(xs), F), f32)], axis=0)


class Copies:
    def __init__(self, sems):
        self.sems, self.all = sems, []

    def __call__(self, src, dst):
        c = pltpu.make_async_copy(src, dst, self.sems.at[len(self.all)])
        self.all.append(c)
        c.start()
        return c

    def wait(self):
        wait(*self.all)


def wait(*copies):
    for c in copies:
        c.wait()


def far(*shape, dtype=f32):
    return pltpu.HBM(shape, dtype)


def near(*shape, dtype=f32):
    return pltpu.VMEM(shape, dtype)


def only(here, *names):
    return {name: here[name] for name in names}


resident = []


def loose(*shape):
    return jax.ShapeDtypeStruct(shape, f32)


def call(body, name, scalars={}, hbm={}, vmem={}, free={}, outs={}, grow={}, scratch={}, after=(), micros=2, copies=24, active=None):
    args, specs, where = [], [], {}

    def add(values, space, pinned):
        for key, value in values.items():
            at = []
            for x in value if isinstance(value, (list, tuple)) else [value]:
                at.append(len(args))
                args.append(pltpu.with_memory_space_constraint(x, space) if pinned else x)
                specs.append(pl.BlockSpec(memory_space=space))
            where[key] = at if isinstance(value, (list, tuple)) else at[0]

    add(scalars, pltpu.SMEM, False)
    add(hbm, pltpu.HBM, True)
    add(vmem, pltpu.VMEM, True)
    add(free, pl.ANY, False)
    add(dict(after=[x for x in after if x.shape == (8, 128)]), pltpu.HBM, True)
    add(dict(arrived=[x for x in after if x.shape != (8, 128)]), pl.ANY, False)
    used = {id(x) for value in vmem.values() for x in (value if isinstance(value, (list, tuple)) else [value])}
    add(dict(kept=[x for x in resident if id(x) not in used]), pltpu.VMEM, True)
    shapes, out_specs, aliases = [], [], {}
    for key, value in list(outs.items()) + list(grow.items()) + [("token", far(8, 128))]:
        old, shape = value if key in grow else (None, value)
        space = pl.ANY if isinstance(shape, jax.ShapeDtypeStruct) else shape.memory_space
        where[key] = -1 - len(shapes)
        if old is not None:
            aliases[len(args)] = len(shapes)
            args.append(old if space is pl.ANY else pltpu.with_memory_space_constraint(old, space))
            specs.append(pl.BlockSpec(memory_space=space))
        shapes.append(shape)
        out_specs.append(pl.BlockSpec(memory_space=space))
    first_out, first_scratch = len(args), len(args) + len(shapes)
    kept = dict(scratch)

    def kernel(*refs):
        k = SimpleNamespace()
        pick = lambda i: refs[i] if i >= 0 else refs[first_out - 1 - i]
        for key, at in where.items():
            setattr(k, key, [pick(i) for i in at] if isinstance(at, list) else pick(at))
        for i, key in enumerate(kept):
            setattr(k, key, refs[first_scratch + i])
        k.load, k.store = Copies(refs[-2]), Copies(refs[-1])
        if active is None:
            body(k)
        else:
            pl.when(k.section[0] == active)(lambda: body(k))

    res = pl.pallas_call(
        kernel,
        out_shape=shapes,
        in_specs=specs,
        out_specs=out_specs,
        scratch_shapes=list(kept.values()) + [pltpu.SemaphoreType.DMA((copies,))] * 2,
        input_output_aliases=aliases,
        compiler_params=pltpu.CompilerParams(vmem_limit_bytes=16 * MIB),
        cost_estimate=pl.CostEstimate(flops=int(micros * 1.15e9), bytes_accessed=0, transcendentals=0),
        name=name,
    )(*args)
    return SimpleNamespace(**{key: res[-1 - at] for key, at in where.items() if not isinstance(at, list) and at < 0})


def prepare(w1, w2, ends=None, here=None, count=0, W=0, after=()):
    F = w1.shape[1]

    def body(k):
        c2 = k.load(k.w2, k.b2)
        parts = [pl.ds(i, F) for i in range(0, w1.shape[0], F)]
        c1 = [k.load(k.w1.at[part], k.b1.at[part]) for part in parts]
        ce = [k.load(src, ref) for src, ref in zip(k.ends, (k.e0, k.e1))] if ends is not None else []
        c2.wait()
        k.h2[...], k.l2[...] = split(k.b2[...])
        for part, c in zip(parts, c1):
            c.wait()
            k.h1[part], k.l1[part] = split(k.b1[part])
        if ends is not None:
            wait(*ce)
            hots = []
            for ref in (k.e0, k.e1):
                total = count * (W // 3)
                at = ref[...] - (k.node[0] - 1) * (W // 3)
                at = jnp.where(at < 0, at + total, at)
                at = jnp.where(at >= total, at - total, at)
                hots.append((lax.broadcasted_iota(jnp.int32, (W, at.shape[1]), 0) == at).astype(f32).astype(bf16))
            both = jnp.concatenate(hots, axis=0)
            k.gather[...] = jnp.concatenate([both, both], axis=0)
            k.scatter[...] = jnp.concatenate([both, both], axis=1)

    half = lambda *s: near(*s, dtype=bf16)
    outs = dict(h1=half(*w1.shape), l1=half(*w1.shape), h2=half(*w2.shape), l2=half(*w2.shape))
    scalars, hbm = {}, dict(w1=w1, w2=w2)
    scratch = dict(b1=pltpu.VMEM(w1.shape, f32), b2=pltpu.VMEM(w2.shape, f32))
    if ends is not None:
        rows = ends[0].shape[1]
        outs.update(gather=half(4 * W, rows), scatter=half(2 * W, 2 * rows))
        scalars = only(here, "node")
        hbm.update(ends=list(ends))
        scratch.update(e0=pltpu.VMEM((1, rows), jnp.int32), e1=pltpu.VMEM((1, rows), jnp.int32))
    r = call(body, "prepare", scalars, hbm, outs=outs, scratch=scratch, after=after)
    resident.extend([r.h1, r.l1, r.h2, r.l2])
    if ends is not None:
        resident.extend([r.gather, r.scatter])
    return r, dict(w1=[r.h1, r.l1], w2=[r.h2, r.l2])


def side_rows(par, nr):
    return pl.multiple_of((1 - par) * 2 * nr, 16), pl.multiple_of(par * 2 * nr, 16)


def window_parts(k, ref, nr):
    a_at, b_at = side_rows(k.node[0] % 2, nr)
    return [ref.at[:, pl.ds(a_at, nr), :], ref.at[:, nr:2 * nr, :], ref.at[:, pl.ds(b_at, nr), :]]


def load_weights(k, weights):
    return [k.load(k.weights[0], k.lengths), k.load(k.weights[1], k.mask)] if weights else []


def weight_scratch(weights):
    return dict(lengths=pltpu.SMEM(weights[0].shape, jnp.int32), mask=pltpu.SMEM(weights[1].shape, jnp.int32)) if weights else {}


def sample_weight(k, sample):
    m, t = divmod(sample, k.mask.shape[0])
    return jnp.where(t < k.lengths[m], k.mask[t, m], 0).astype(f32)


def load_views(k, views, refs, targets, g):
    return [k.load(ref.at[pl.ds(view[1], g)], target) for view, ref, target in zip(views, refs, targets)]


def arrays(views):
    return [v[0] for v in views]


def chunk(g):
    return 2 if g % 2 == 0 else 1


def edge_forward(g, active, here, e, v, n, hot, w, vec, act, box, relay, after, micros):
    rows, F = e[0][0].shape[1:]
    nr = v[0][0].shape[1]
    W = 3 * nr
    cs, part_size = g, chunk(g)

    def body(k):
        load, store = k.load, k.store
        cv = load_views(k, v, k.v, window_parts(k, k.vb, nr), g)
        ce = load_views(k, e, k.e, [k.eb.at[pl.ds(s, part_size)] for s in range(0, g, part_size)], part_size)
        (w1h, w1l), (w2h, w2l), vec = k.w1, k.w2, k.vec
        wait(*cv)
        vw = split(k.vb[...].reshape(g * W, F))
        for i in (0, 1):
            part = pl.ds((i + 1) * F, F)
            h, l = split(dot3(vw, (w1h[part], w1l[part]), NN).reshape(g, W, F))
            k.pp[:, i * W:(i + 1) * W] = h
            k.pp[:, (i + 2) * W:(i + 3) * W] = l
        for s in range(0, g, cs):
            wait(*ce)
            to = pl.ds(s, cs)
            x = k.eb[to].reshape(cs * rows, F)
            a = dot3(split(x), (w1h[0:F], w1l[0:F]), NN) + vec[0:1]
            a = a + jnp.concatenate([dot1(k.gather[...], k.pp[s + t], TN) for t in range(cs)], axis=0)
            k.out_a[to] = a.reshape(cs, rows, F)
            h = a / (1 + jnp.exp(-a))
            n_, r = normalized(dot3(split(h), (w2h[...], w2l[...]), NN) + vec[1:2])
            k.out_n[to] = n_.reshape(cs, rows, F)
            k.out_r[to] = jnp.broadcast_to(r, (cs * rows, 128)).reshape(cs, rows, 128)
            m = n_ * vec[2:3] + vec[3:4]
            k.ob[to] = (x + m).reshape(cs, rows, F)
            done = 0
            for key, size in zip(names, relay):
                store(k.ob.at[pl.ds(done, size)], getattr(k, key))
                done += size
            for t in range(g):
                store(k.ob.at[t], k.act.at[n + t])
            mh, ml = split(m.reshape(cs, rows, F))
            for t in range(cs):
                k.sb[s + t] = dot1(k.scatter[W:], jnp.concatenate([mh[t], ml[t]], axis=0), NN)
        sides = window_parts(k, k.sb, nr)
        store(sides[0], k.box_a.at[pl.ds(box[2], g)])
        store(sides[1], k.own)
        store(sides[2], k.box_b.at[pl.ds(box[2], g)])
        store.wait()

    outs = dict(out_a=near(g, rows, F), out_n=near(g, rows, F), out_r=near(g, rows, 128), own=far(g, nr, F))
    names = "abcd"[:len(relay)]
    outs.update({key: far(size, rows, F) for key, size in zip(names, relay)})
    old = box[0] or (None, None)
    grow = dict(act=(act[0], far(act[1], rows, F)), box_a=(old[0], far(box[1], nr, F)), box_b=(old[1], far(box[1], nr, F)))
    full = pltpu.VMEM((g, rows, F), f32)
    scratch = dict(eb=full, ob=full, vb=pltpu.VMEM((g, W, F), f32), sb=pltpu.VMEM((g, W, F), f32), pp=pltpu.VMEM((g, 4 * W, F), bf16))
    r = call(body, "edge_forward", here, active=active, vmem=dict(**w, gather=hot.gather, scatter=hot.scatter, vec=vec), free=dict(e=arrays(e), v=arrays(v)), outs=outs, grow=grow, scratch=scratch, after=after, micros=micros)
    r.relay = [getattr(r, key) for key in names]
    return r


def node_stage(g, forward, backward, active, here, v, n, w, vec, parts, act=None, stash=None, weights=None, cot=None, box=None, after=(), micros=2):
    nr, F = v[0].shape[1:]
    R = g * nr

    def body(k):
        load, store = k.load, k.store
        cx = [load(k.v.at[pl.ds(v[1], g)], k.zb.at[:, :, 0:F])] + load_views(k, parts, k.parts, [k.pb.at[i] for i in range(len(parts))], g)
        if forward and backward:
            cx.append(load(k.cot.at[pl.ds(n, g)], k.gb))
            cx += load_weights(k, weights)
        w1, w2, vec = (k.w1[0][...], k.w1[1][...]), (k.w2[0][...], k.w2[1][...]), k.vec
        wait(*cx)
        given = sum([k.pb[i] for i in range(1, len(parts))], k.pb[0])
        k.zb[:, :, F:] = given if forward else k.gathered[...]
        z = k.zb[...].reshape(R, 2 * F)
        zs = split(z)
        if forward:
            a = dot3_few(zs, w1, NN) + vec[0:1]
            h = a / (1 + jnp.exp(-a))
            n_, r = normalized(dot3_few(split(h), w2, NN) + vec[1:2])
            k.ob[...] = (z[:, :F] + n_ * vec[2:3] + vec[3:4]).reshape(g, nr, F)
            if not backward:
                store(k.ob, k.out_v)
                k.out_a[...] = a.reshape(g, nr, F)
                k.out_n[...] = n_.reshape(g, nr, F)
                k.out_r[...] = jnp.broadcast_to(r, (R, 128)).reshape(g, nr, 128)
                k.out_g[...] = given
            store(k.ob, k.act.at[pl.ds(n, g)])
        else:
            a, n_, r = k.a[...].reshape(R, F), k.n[...].reshape(R, F), k.r[...].reshape(R, 128)[:, 0:1]
        if backward:
            if forward:
                for s in range(g):
                    k.gb[s] = k.gb[s] * sample_weight(k, n + s)
                gu = k.gb[...].reshape(R, F)
            else:
                gu = given.reshape(R, F)
            gp = norm_back(gu, n_, r, vec[2:3])
            q = 1 / (1 + jnp.exp(-a))
            hs, gps = split(a * q), split(gp)
            ga = dot3_few(gps, w2, NT) * (q * (1 + a * (1 - q)))
            gas = split(ga)
            gz = dot3_few(gas, w1, NT)
            k.ggb[...] = gz[:, F:].reshape(g, nr, F)
            for ref in (k.box_a, k.box_b):
                store(k.ggb, ref.at[pl.ds(box[2], g)])
            k.own[...] = k.ggb[...]
            k.out_gv[...] = (gu + gz[:, :F]).reshape(g, nr, F)
            for i, x in enumerate((zs[0][:, :F], zs[1][:, :F], zs[0][:, F:], zs[1][:, F:], hs[0], hs[1], gas[0], gas[1], gps[0], gps[1])):
                k.ops[i] = x
            k.dv[...] = column_sums(ga, gp, gu * n_, gu)
        store.wait()

    hbm, vmem, free = {}, dict(**w, vec=vec), dict(v=v[0], parts=arrays(parts))
    shape = near(g, nr, F)
    outs, grow = {}, {}
    if not forward:
        vmem.update(a=stash.out_a, n=stash.out_n, r=stash.out_r, gathered=stash.out_g)
    elif backward:
        hbm.update(cot=cot, weights=weights)
    if forward:
        grow.update(act=(act[0], far(act[1], nr, F)))
        if not backward:
            outs.update(out_v=far(g, nr, F), out_a=shape, out_n=shape, out_r=near(g, nr, 128), out_g=shape)
    if backward:
        old = box[0] or (None, None)
        outs.update(own=shape, out_gv=shape, ops=near(10, R, F, dtype=bf16), dv=near(8, F))
        grow.update(box_a=(old[0], far(box[1], nr, F)), box_b=(old[1], far(box[1], nr, F)))
    small = pltpu.VMEM((g, nr, F), f32)
    scratch = dict(zb=pltpu.VMEM((g, nr, 2 * F), f32), pb=pltpu.VMEM((len(parts), g, nr, F), f32), gb=small, ob=small, ggb=small, **weight_scratch(weights))
    return call(body, "node_stage", only(here, "section"), hbm, vmem, free, active=active, outs=outs, grow=grow, scratch=scratch, after=after, micros=micros)


def node_weights(active, here, m, acc, first, after):
    _, R, F = m.ops.shape

    def body(k):
        o = k.ops
        for i, (x, y) in enumerate(((0, 6), (2, 6), (4, 8))):
            part = pl.ds(i * F, F)
            d = dot3((o[x], o[x + 1]), (o[y], o[y + 1]), TN)
            k.total[part] = d if first else k.total[part] + d

    grow = dict(total=(acc and acc.total, near(3 * F, F)))
    return call(body, "node_weights", only(here, "section"), active=active, vmem=dict(ops=m.ops), grow=grow, after=after, micros=0.01)


def edge_backward(g, active, here, weights, ge, gg, n, stash, gv, hot, w, vec, box, after, micros):
    rows, F = ge[0].shape[1:]
    nr = gv.shape[1]
    W = 3 * nr
    cs = g

    def body(k):
        load, store = k.load, k.store
        gg_at = window_parts(k, k.ggb, nr)
        cg = load_views(k, (gg[0], gg[2]), k.gg, (gg_at[0], gg_at[2]), g)
        cx = [load(k.ge.at[ge[1] + s], k.gb.at[s]) for s in range(g)]
        cx += load_weights(k, weights)
        k.ggb[:, nr:2 * nr] = k.gg_own[...]
        (w1h, w1l), (w2h, w2l), vec = k.w1, k.w2, k.vec
        wait(*cg)
        h, l = split(k.ggb[...])
        k.gg2[:, 0:W] = h
        k.gg2[:, W:] = l
        flat = lambda x: x.reshape(cs * rows, x.shape[-1])
        sums = []
        for s in range(0, g, cs):
            to = pl.ds(s, cs)
            wait(*cx)
            if weights:
                for t in range(s, s + cs):
                    k.gb[t] = k.gb[t] * sample_weight(k, n + t)
            hot_r = k.gather[pl.ds(W, W)]
            gu = flat(k.gb[to]) + jnp.concatenate([dot1(hot_r, k.gg2[s + t, 0:W], TN) + dot1(hot_r, k.gg2[s + t, W:], TN) for t in range(cs)], axis=0)
            n_, a = flat(k.n[to]), flat(k.a[to])
            gp = norm_back(gu, n_, flat(k.r[to])[:, 0:1], vec[2:3])
            gps = split(gp)
            q = 1 / (1 + jnp.exp(-a))
            ga = dot3(gps, (w2h[...], w2l[...]), NT) * (q * (1 + a * (1 - q)))
            gas = split(ga)
            for i, x in enumerate((*split(a * q), *gps, *gas)):
                k.ops[i, pl.ds(s * rows, cs * rows)] = x
            for t in range(cs):
                both = jnp.concatenate([x[t * rows:(t + 1) * rows] for x in gas], axis=0)
                k.ssb[s + t] = dot1(k.scatter[...], both, NN)
            sums.append(column_sums(ga, gp, gu * n_, gu))
        ss = split(k.ssb[:, 0:W].reshape(g * W, F))
        sr = split(k.ssb[:, W:].reshape(g * W, F))
        for i, x in enumerate((*ss, *sr)):
            k.sops[i] = x
        wg = dot3(ss, (w1h[F:2 * F], w1l[F:2 * F]), NT) + dot3(sr, (w1h[2 * F:], w1l[2 * F:]), NT)
        k.wgb[...] = wg.reshape(g, W, F)
        k.wgb[:, nr:2 * nr] += k.gv[...]
        sides = window_parts(k, k.wgb, nr)
        store(sides[0], k.box_a.at[pl.ds(box[2], g)])
        store(sides[2], k.box_b.at[pl.ds(box[2], g)])
        k.own[...] = k.wgb[:, nr:2 * nr]
        k.dv[...] = sum(sums[1:], sums[0])
        store.wait()

    free = dict(ge=ge[0], gg=[gg[0][0], gg[2][0]])
    vmem = dict(**w, vec=vec, a=stash.out_a, n=stash.out_n, r=stash.out_r, gv=gv, gg_own=gg[1], gather=hot.gather, scatter=hot.scatter)
    old = box[0] or (None, None)
    outs = dict(own=near(g, nr, F), ops=near(6, g * rows, F, dtype=bf16), sops=near(4, g * W, F, dtype=bf16), dv=near(8, F))
    grow = dict(box_a=(old[0], far(box[1], nr, F)), box_b=(old[1], far(box[1], nr, F)))
    scratch = dict(gb=pltpu.VMEM((g, rows, F), f32), ggb=pltpu.VMEM((g, W, F), f32), gg2=pltpu.VMEM((g, 2 * W, F), bf16), ssb=pltpu.VMEM((g, 2 * W, F), f32), wgb=pltpu.VMEM((g, W, F), f32), **weight_scratch(weights))
    return call(body, "edge_backward", here, dict(weights=weights) if weights else {}, active=active, vmem=vmem, free=free, outs=outs, grow=grow, scratch=scratch, after=after, micros=micros)


def add_parts(active, here, views, own, n, grad, relay, after):
    g, (nr, F) = sum(x.shape[0] for x in own), own[0].shape[1:]

    def body(k):
        wait(*load_views(k, views, k.views, [k.pb.at[i] for i in (0, 1)], g))
        done = 0
        for x in k.own:
            to = pl.ds(done, x.shape[0])
            k.pb[0, to] = k.pb[0, to] + k.pb[1, to] + x[...]
            done += x.shape[0]
        if relay:
            k.store(k.pb.at[0], k.out)
        k.store(k.pb.at[0], k.grad.at[pl.ds(n, g)])
        k.store.wait()

    outs = dict(out=far(g, nr, F)) if relay else {}
    grow = dict(grad=(grad[0], far(grad[1], nr, F)))
    return call(body, "add_parts", only(here, "section"), active=active, vmem=dict(own=own), free=dict(views=arrays(views)), outs=outs, grow=grow, scratch=dict(pb=pltpu.VMEM((2, g, nr, F), f32)), after=after, micros=0.01)


def edge_out(g, active, here, weights, ge, n, ops, w, grad, relay, after, micros):
    rows, F = ge[0].shape[1:]
    halves = (0, 1) if g % 2 == 0 else (0,)
    m = g // len(halves)

    def body(k):
        cs = [k.load(k.ge.at[pl.ds(ge[1] + i * m, m)], k.gb.at[pl.ds(i * m, m)]) for i in halves]
        cw = load_weights(k, weights)
        w1h, w1l = k.w1
        for i in halves:
            own = dot3([k.ops[x, pl.ds(i * m * rows, m * rows)] for x in (4, 5)], (w1h[0:F], w1l[0:F]), NT)
            cs[i].wait()
            if i == 0:
                wait(*cw)
            if weights:
                for t in range(i * m, (i + 1) * m):
                    k.gb[t] = k.gb[t] * sample_weight(k, n + t)
            to = pl.ds(i * m, m)
            k.gb[to] = k.gb[to] + own.reshape(m, rows, F)
            if relay:
                k.store(k.gb.at[to], k.out_ge.at[to])
            k.store(k.gb.at[to], k.grad.at[pl.ds(n + i * m, m)])
        k.store.wait()

    outs = dict(out_ge=far(g, rows, F)) if relay else {}
    grow = dict(grad=(grad[0], far(grad[1], rows, F)))
    return call(body, "edge_out", only(here, "section"), dict(weights=weights) if weights else {}, active=active, vmem=dict(ops=ops, w1=w["w1"]), free=dict(ge=ge[0]), outs=outs, grow=grow, scratch=dict(gb=pltpu.VMEM((g, rows, F), f32), **weight_scratch(weights)), after=after, micros=micros)


def edge_weights(g, active, here, b, node_dv, e, v, pad, acc, first, after, micros):
    rows, F = e[0][0].shape[1:]
    nr = v[0][0].shape[1]
    W = 3 * nr

    def body(k):
        cs = chunk(g)
        ce = load_views(k, e, k.e, [k.eb.at[pl.ds(s, cs)] for s in range(0, g, cs)], cs)
        cv = load_views(k, v, k.v, window_parts(k, k.vb, nr), g)
        o = k.ops

        def put(total, i, x, y):
            part = pl.ds(i * F, F)
            d = dot3(x, y, TN)
            total[part] = d if first else total[part] + d

        put(k.total, 3, (o[0], o[1]), (o[2], o[3]))
        if first:
            k.total[4 * F:] = jnp.zeros((pad, F), f32)
        k.total[4 * F:4 * F + 8] += k.dv[...]
        if node_dv:
            k.total[4 * F + 8:4 * F + 16] = sum([x[...] for x in k.node_dv[1:]], k.node_dv[0][...])
        wait(*cv)
        vs = split(k.vb[...].reshape(g * W, F))
        for i in (0, 1):
            put(k.total, i + 1, vs, (k.sops[2 * i], k.sops[2 * i + 1]))
        wait(*ce)
        put(k.total, 0, split(k.eb[...].reshape(g * rows, F)), (o[4], o[5]))

    vmem = dict(ops=b.ops, sops=b.sops, dv=b.dv)
    if node_dv:
        vmem.update(node_dv=node_dv)
    grow = dict(total=(acc and acc.total, near(4 * F + pad, F)))
    scratch = dict(eb=pltpu.VMEM((g, rows, F), f32), vb=pltpu.VMEM((g, W, F), f32))
    return call(body, "edge_weights", here, active=active, vmem=vmem, free=dict(e=arrays(e), v=arrays(v)), grow=grow, scratch=scratch, after=after, micros=micros)


def gate(after, *xs, make=far, micros=0.01):
    return call(lambda k: None, "gate", grow={name: (x, make(*x.shape)) for name, x in zip("xyzuvw", xs)}, after=after, micros=micros)


class Total:
    def __init__(self, x, here, orders, cuts, vecs=False):
        self.vecs = vecs
        count = lax.axis_size("node")
        self.here, self.orders = only(here, "node"), orders
        self.swaps = [[(i, i ^ (1 << (y if i % 2 else x))) for i in range(count)] for x, y in zip(*orders)]
        self.x, self.cuts = x, cuts
        self.rows, self.F = x.shape
        self.sizes, rows = [], self.rows
        while len(self.sizes) < len(self.swaps) and rows % 16 == 0:
            rows //= 2
            self.sizes.append(rows)
        self.got, self.result, self.token, self.done = [], None, None, False
        self.steps = self.run()

    def flag(self, ref, step):
        x, y = (order[step] for order in self.orders)
        node = ref.node[0]
        return jnp.where(node % 2 == 1, node >> y, node >> x) & 1

    def partial(self, k):
        K, sizes = len(self.sizes), self.sizes
        size = sizes[min(k, K - 1)]

        def body(ref):
            def start(after):
                at = sum(self.flag(ref, m) * sizes[m] for m in range(after + 1, k)) if after + 1 < k else 0
                if k < K:
                    at = at + (1 - self.flag(ref, k)) * size
                return pl.multiple_of(at, 8)

            total = ref.x[pl.ds(start(-1), size)]
            for j, x in enumerate(ref.got):
                total = total + x[pl.ds(start(j), size)]
            ref.out[...] = total

        r = call(body, "partial_sum", self.here, vmem=dict(x=self.x, got=self.got[:k]), outs=dict(out=near(size, self.F)), after=self.after, micros=50)
        self.token = (r.token,)
        return r.out

    def add(self, x, y):
        def body(k):
            k.out[...] = k.x[...] + k.y[...]

        r = call(body, "add", self.here, vmem=dict(x=x, y=y), outs=dict(out=near(*x.shape)), after=self.after, micros=50)
        self.token = (r.token,)
        return r.out

    def join(self, own, got, step):
        R = own.shape[0]

        def body(k):
            bit = self.flag(k, step)
            k.joined[pl.ds(pl.multiple_of(bit * R, 8), R)] = k.own[...]
            k.joined[pl.ds(pl.multiple_of((1 - bit) * R, 8), R)] = k.got[...]

        r = call(body, "join", self.here, vmem=dict(own=own, got=got), outs=dict(joined=near(2 * R, self.F)), after=self.after, micros=50)
        self.token = (r.token,)
        return r.joined

    def finish(self, own, got):
        R = own.shape[0]
        names = "abcdef"[:len(self.cuts)]

        def put(k, low, high):
            done = 0
            for key, rows in zip(names, self.cuts):
                for src, at in ((low, 0), (high, R)):
                    a, b = max(at, done), min(at + R, done + rows)
                    for i in range(a, b, 256):
                        size = min(256, b - i)
                        k.store(src.at[pl.ds(i - at, size)], getattr(k, key).at[pl.ds(i - done, size)])
                done += rows
            if self.vecs:
                assert done >= R
                k.va[...] = high[done - R:done - R + 4]
                k.vb[...] = high[done - R + 8:done - R + 12]
                k.store(k.va, k.first)
                k.store(k.vb, k.second)
            k.store.wait()

        def body(k):
            bit = self.flag(k, 0)
            pl.when(bit == 0)(lambda: put(k, k.own, k.got))
            k.store.all = []
            pl.when(bit == 1)(lambda: put(k, k.got, k.own))

        outs = {key: far(rows, self.F) for key, rows in zip(names, self.cuts)}
        scratch = {}
        if self.vecs:
            outs.update(first=far(4, self.F), second=far(4, self.F))
            scratch.update(va=pltpu.VMEM((4, self.F), f32), vb=pltpu.VMEM((4, self.F), f32))
        r = call(body, "finish", self.here, vmem=dict(own=own, got=got), outs=outs, scratch=scratch, after=self.after, micros=50)
        self.token = (r.token,)
        return [getattr(r, key) for key in outs]

    def run(self):
        K = len(self.sizes)
        for k in range(K):
            send = self.partial(k)
            self.got.append(lax.ppermute(send, "node", self.swaps[k]))
            yield
        own = self.partial(K)
        for pairs in self.swaps[K:]:
            got = lax.ppermute(own, "node", pairs)
            yield
            own = self.add(own, got)
        for k in reversed(range(K)):
            got = lax.ppermute(own, "node", self.swaps[k])
            yield
            if k:
                own = self.join(own, got, k)
            else:
                self.result = self.finish(own, got)
        self.done = True

    def step(self, after):
        if self.done:
            return after
        self.after = after
        next(self.steps, None)
        return self.token


def on_device(in_nodes, in_edges, senders, receivers, edge_w1, edge_w2, edge_vec, node_w1, node_w2, node_vec, cot_nodes, cot_edges, lengths, step_mask):
    samples, nr, F = in_nodes.shape
    count = lax.axis_size("node")
    section, node = lax.axis_index("section"), lax.axis_index("node")
    evec, nvec = edge_vec[0], node_vec[0]
    here = dict(section=section.astype(jnp.int32).reshape(1), node=node.astype(jnp.int32).reshape(1))
    live = [lengths, step_mask.T]

    def partner(i, side):
        return i ^ 1 if side == 0 else (i - 1 + 2 * (i % 2)) % count

    def swap(x, side, planes):
        if planes is None:
            return lax.ppermute(x, "node", [(i, partner(i, side)) for i in range(count)])
        return lax.ppermute(x, ("section", "node"), [(s * count + i, s * count + partner(i, side)) for s in planes for i in range(count)])

    def beside(to_a, to_b, planes=None):
        return swap(to_a, 0, planes), swap(to_b, 1, planes)

    def across(x, source, side=None):
        if side is None:
            return lax.ppermute(x, "section", [(source, 1 - source)])
        return lax.ppermute(x, ("section", "node"), [(source * count + i, (1 - source) * count + partner(i, side)) for i in range(count)])

    p, q = [(sum(group_sizes[:i]), n) for i, n in enumerate(group_sizes)]
    both = p[1] + q[1]
    pad = 8 * count
    act_e = act_n = acc_n = acc_e = grad_e = grad_n = None
    after = ()

    def done(r):
        nonlocal after
        after = (r.token,)
        return r

    def stay(r, *names):
        r.kept = [getattr(r, name) for name in names]
        resident.extend(r.kept)
        return r

    def leave(*rs):
        for r in rs:
            resident[:] = [x for x in resident if all(x is not y for y in r.kept)]

    resident.clear()
    from_a, from_b = beside(in_nodes, in_nodes)
    hot, ew = prepare(edge_w1[0], edge_w2[0], (senders.reshape(1, -1), receivers.reshape(1, -1)), here, count, 3 * nr)

    def forward_0(c, relay):
        nonlocal act_e
        v = [(x, c[0]) for x in (from_a, in_nodes, from_b)]
        e = [(in_edges, c[0] + s) for s in range(0, c[1], chunk(c[1]))]
        f = done(edge_forward(c[1], 0, here, e, v, c[0], hot, ew, evec, (act_e, samples), (None, c[1], 0), relay, after, 0.01))
        act_e, f.v, f.e = f.act, v, e
        return stay(f, "out_a", "out_n", "out_r")

    def nodes_0(c, f, got):
        nonlocal act_n
        m = done(node_stage(c[1], True, False, 0, here, (in_nodes, c[0]), c[0], nw, nvec, [(got[0], 0), (f.own, 0), (got[1], 0)], act=(act_n, samples), after=after, micros=0.01))
        act_n = m.act
        return stay(m, "out_a", "out_n", "out_r", "out_g")

    def forward_1(c, e, nodes, box):
        nonlocal act_e
        v, e = [(x, 0) for x in nodes], [(x, s) for x in e for s in range(0, x.shape[0], chunk(c[1]))]
        f = done(edge_forward(c[1], 1, here, e, v, c[0], hot, ew, evec, (act_e, samples), box, (), after, 0.01))
        act_e, f.v, f.e = f.act, v, e
        return stay(f, "out_a", "out_n", "out_r")

    def middle_1(c, f, got, at, box):
        nonlocal act_n
        m = done(node_stage(c[1], True, True, 1, here, f.v[1], c[0], nw, nvec, [(got[0], at), (f.own, 0), (got[1], at)], act=(act_n, samples), weights=live, cot=cot_nodes, box=box, after=after, micros=0.01))
        act_n = m.act
        return stay(m, "ops", "dv", "own", "out_gv")

    def backward_1(c, f, m, got, at, box):
        b = done(edge_backward(c[1], 1, here, live, (cot_edges, c[0]), ((got[0], at), m.own, (got[1], at)), c[0], f, m.out_gv, hot, ew, evec, box, after, 0.01))
        leave(f)
        return stay(b, "ops", "sops", "dv", "own")

    def add_1(c, b, got, at):
        nonlocal grad_n
        r = done(add_parts(1, here, [(x, at) for x in got], [b.own], c[0], (grad_n, samples), True, after))
        grad_n = r.grad
        return r.out

    def out_1(c, b):
        nonlocal grad_e
        r = done(edge_out(c[1], 1, here, live, (cot_edges, c[0]), c[0], b.ops, ew, (grad_e, samples), True, after, 0.01))
        grad_e = r.grad
        return r.out_ge

    def middle_0(c, gv, stash):
        m = done(node_stage(c[1], False, True, 0, here, (in_nodes, c[0]), c[0], nw, nvec, [(gv, 0)], stash=stash, box=(None, c[1], 0), after=after, micros=50))
        m.got = beside(m.box_a, m.box_b, (0,))
        leave(stash)
        return stay(m, "ops", "dv", "own", "out_gv")

    def backward_0(c, ge, f, m, box):
        b = done(edge_backward(c[1], 0, here, None, (ge, 0), ((m.got[0], 0), m.own, (m.got[1], 0)), c[0], f, m.out_gv, hot, ew, evec, box, after, 50))
        leave(f)
        return stay(b, "ops", "sops", "dv", "own")

    def out_0(c, ge, b):
        nonlocal grad_e
        grad_e = done(edge_out(c[1], 0, here, None, (ge, 0), c[0], b.ops, ew, (grad_e, samples), False, after, 2)).grad

    def node_grads(on, m, first):
        nonlocal acc_n
        acc_n = done(node_weights(on, here, m, acc_n, first, after))
        leave(m)

    def edge_grads(on, c, b, f, first, node_dv=()):
        nonlocal acc_e
        acc_e = done(edge_weights(c[1], on, here, b, list(node_dv), f.e, f.v, pad, acc_e, first, after, 2))
        leave(b)

    f0p = forward_0(p, relay_sizes[0])
    got = beside(f0p.box_a, f0p.box_b)
    e0 = [across(f0p.relay[0], 0)]
    _, nw = prepare(node_w1[0], node_w2[0], after=after)
    n0p = nodes_0(p, f0p, got)
    v0, y = across(n0p.out_v, 0), across(n0p.out_v, 0, 1)
    held = done(gate(after, *f0p.relay[1:]))
    first = (v0, y) + tuple(e0)
    e0 += [across(getattr(held, key), 0) for key, _ in zip("xyz", f0p.relay[1:])]
    f0q = forward_0(q, relay_sizes[1])
    v0 = (swap(v0, 0, (1,)), v0, y)
    held = done(gate(after + first, f0q.box_a, f0q.box_b, *f0q.relay, micros=50))
    e1 = [across(getattr(held, key), 0) for key, _ in zip("zuvw", f0q.relay)]
    got_q = beside(held.x, held.y, (0,))
    f1p = forward_1(p, e0, v0, (None, p[1], 0))
    got = beside(f1p.box_a, f1p.box_b)
    n0q = nodes_0(q, f0q, got_q)
    v1, y = across(n0q.out_v, 0), across(n0q.out_v, 0, 1)
    n1p = middle_1(p, f1p, got, 0, (None, p[1], 0))
    got_p = beside(n1p.box_a, n1p.box_b)
    b1p = backward_1(p, f1p, n1p, got_p, 0, (None, p[1], 0))
    got_p = beside(b1p.box_a, b1p.box_b)
    v1 = done(gate(after, v1, make=loose)).x
    f1q = forward_1(q, e1, (swap(v1, 0, None), v1, y), (None, q[1], 0))
    got_q = beside(f1q.box_a, f1q.box_b)
    ge0 = across(out_1(p, b1p), 1)
    gv0 = across(add_1(p, b1p, got_p, 0), 1)
    n1q = middle_1(q, f1q, got_q, 0, (None, q[1], 0))
    got_q = beside(n1q.box_a, n1q.box_b)
    m0p = middle_0(p, gv0, n0p)
    node_grads(1, n1p, True)
    b1q = backward_1(q, f1q, n1q, got_q, 0, (None, q[1], 0))
    got_q = beside(b1q.box_a, b1q.box_b)
    ge1 = out_1(q, b1q)
    gv1 = across(add_1(q, b1q, got_q, 0), 1)
    ge1 = across(done(gate(after, ge1)).x, 1)
    node_grads(1, n1q, False)
    edge_grads(1, p, b1p, f1p, True)
    edge_grads(1, q, b1q, f1q, False, (n1p.dv, n1q.dv))
    b0p = backward_0(p, ge0, f0p, m0p, (None, both, 0))
    m0q = middle_0(q, gv1, n0q)
    edge_grads(0, p, b0p, f0p, True)
    node_grads(0, m0p, True)
    node_grads(0, m0q, False)
    b0q = backward_0(q, ge1, f0q, m0q, ((b0p.box_a, b0p.box_b), both, p[1]))
    got = beside(b0q.box_a, b0q.box_b)
    edge_grads(0, q, b0q, f0q, False, (m0p.dv, m0q.dv))
    bits = list(range(count.bit_length() - 1))
    yzz, zyz, yzz_turned = [[0] + [bits[i] for i in order] + bits[4:] for order in ((1, 2, 3), (2, 1, 3), (1, 3, 2))]
    total_e = Total(acc_e.total, here, (yzz_turned, zyz), (3 * F, F), True)
    after = total_e.step(after)
    total_n = Total(acc_n.total, here, (yzz, zyz), (2 * F, F))
    totals = [total_e, total_n]
    after = total_n.step(after)
    for turn in range(2 * len(bits)):
        for t in totals:
            after = t.step(after)
        if turn == 0:
            out_0(p, ge0, b0p)
            out_0(q, ge1, b0q)
        if turn == 4:
            grad_n = done(add_parts(0, here, [(x, 0) for x in got], [b0p.own, b0q.own], 0, (grad_n, samples), False, after)).grad
    edge_1, edge_2, edge_v, node_v = total_e.result
    node_1, node_2 = total_n.result
    return (
        act_n[None], act_e[None], grad_n[None], grad_e[None],
        edge_1[None], edge_2[None], edge_v[None], node_1[None], node_2[None], node_v[None],
    )


def solution(mesh):
    nodes, rows, weights = P(None, "node", None), P("node"), P("section", None, None)
    stacked = P("section", None, "node", None)
    in_specs = (nodes, nodes, rows, rows) + (weights,) * 6 + (nodes, nodes, P(), P())
    out_specs = (stacked,) * 4 + (weights,) * 6
    return jax.shard_map(on_device, mesh=mesh, in_specs=in_specs, out_specs=out_specs, check_vma=False)
```
